32 devices in a mesh: replica: 8 (over y, x, core), fsdp: 4 (over z).
Axes of the slice: x: 2, y: 2, z: 4, core: 2. Of those that a mesh axis runs over, the one named last changes fastest.
Arguments:
- activations: bfloat16 [8, 1792, 4096], P('replica', 'fsdp'), may hold values from -84 to 84
- targets: bfloat16 [8, 1792, 512], P('replica', 'fsdp'), may hold values from -8 to 8
- weights: float32 [8, 4096, 512], P('replica', 'fsdp'), may hold values from -19 to 19
- lengths: int32 [8, 28], P('replica'), may hold values from 1 to 64, 896 in all within a row
Outputs:
- averaged: float32 [8, 4096, 512], P('replica', 'fsdp')
The draws below stay inside these ranges and needn't reach their ends.
Inputs may be any that keep to these rules, and one draw needn't show every extreme that they name: `lengths`: each row sums to 896; sequence s of a replica fills slot s from its first position.
All inputs are finite; a program needn't handle non-finite values.
Results may differ from the reference program's by a relative error of at most 0.0014.
Values may be sent and summed in bfloat16 or wider, within the bound.
No kernel may reach another device: no remote copies, remote signals or barrier semaphores. Data moves between devices by JAX's collectives and lax.ppermute only.
A program may use at most 64 MiB of HBM per device.

```python
import math
import jax
import jax.numpy as jnp
import numpy as np
from jax import lax

D = 4096
KV = 512
SLOT = 64
STEP = 3
TOK_DEV = 448
TOKENS = 1792
NSEQ = 28
LIVE = 896
N_REPLICA = 8
N_FSDP = 4


def draw_activations(key, part):
    base_key, rough_key = jax.random.split(jax.random.fold_in(key, 7), 2)
    ramp = 10.0 ** (jnp.arange(D, dtype=jnp.float32) / D)
    rough = jax.random.uniform(rough_key, (D,), jnp.float32, 0.7, 1.4)
    base = jax.random.normal(base_key, (N_REPLICA, TOKENS, D), jnp.float32)
    base = jnp.clip(base, -6.0, 6.0)
    return (base * (ramp * rough)).astype(jnp.bfloat16)


def draw_weights(key, part):
    base_key, column_key = jax.random.split(jax.random.fold_in(key, 13), 2)
    column_scale = 10.0 ** jax.random.uniform(column_key, (N_REPLICA, 1, KV), jnp.float32, -0.5, 0.5)
    base = jnp.clip(jax.random.normal(base_key, (N_REPLICA, D, KV), jnp.float32), -6.0, 6.0)
    return base * column_scale


def levels(stream_key, extent, shards, low, largest):
    def one(dim, blocks):
        draws = jax.random.uniform(jax.random.fold_in(jax.random.fold_in(stream_key, 6), dim), (blocks,), jnp.float32, low / len(shards), largest / len(shards))
        return jnp.repeat(jnp.exp(draws), extent[dim] // blocks).reshape((-1,) + (1,) * (len(extent) - dim - 1))

    gain = one(*shards[0])
    for cut in shards[1:]:
        gain = gain * one(*cut)
    return gain


def length_profile(count, total, limit, lean):
    loads = [(1 << 20) // math.isqrt(rank ** lean) + 1 for rank in range(2, count + 1)]
    rest, given = total - limit - (count - 1), [1] * (count - 1)
    while rest > 0:
        movable = [i for i in range(count - 1) if given[i] < limit]
        whole, remaining = sum([loads[i] for i in movable]), rest
        for i in movable:
            addition = min(limit - given[i], max(1, remaining * loads[i] // whole), rest)
            given[i] = given[i] + addition
            rest = rest - addition
    return np.array([limit] + given)


def uneven_parts(own_key, amount, total, most, lean):
    if amount == 2:
        one = jax.random.randint(own_key, (), max(1, total - most), min(most, total - 1) + 1)
        return jnp.stack([one, total - one])
    tallies = jnp.asarray(length_profile(amount, total, most, lean), jnp.int32)
    pairs = (amount - 1) // 2
    source_of, taker = tallies[1:1 + 2 * pairs:2], tallies[2:2 + 2 * pairs:2]
    margin = jnp.minimum(source_of - 1, most - taker)
    shifted = jax.random.randint(jax.random.fold_in(own_key, 1), (pairs,), 0, 1 << 20) % (margin + 1)
    tallies = tallies.at[1:1 + 2 * pairs:2].set(source_of - shifted).at[2:2 + 2 * pairs:2].set(taker + shifted)
    return tallies[jax.random.permutation(jax.random.fold_in(own_key, 2), amount)]


def gaussian(own_key, extent, spread, bound, shards=(), kind=jnp.bfloat16):
    loudness = levels(own_key, extent, shards, -0.22, 0.18) if shards else 1.0
    array = jax.random.normal(own_key, extent, jnp.float32) * spread * loudness
    return jnp.minimum(jnp.maximum(array, -bound), bound).astype(kind)


def setup_inputs(seed: int = 0) -> dict:
    streams_of = jax.random.split(jax.random.key(seed), 5)
    return {
        "activations": draw_activations(jax.random.fold_in(streams_of[4], 71), 0),
        "targets": gaussian(streams_of[1], (N_REPLICA, TOKENS, KV), 2.0, 8.0, ((0, 8), (1, 4))),
        "weights": draw_weights(jax.random.fold_in(streams_of[4], 71), 0),
        "lengths": jax.vmap(lambda own: uneven_parts(own, NSEQ, LIVE, SLOT, 2))(jax.random.split(streams_of[3], N_REPLICA)).reshape((N_REPLICA, NSEQ)).astype(jnp.int32),
    }


learning_rate = 0.1
epsilon = 1e-06

def replica_update(features, wanted, master, lengths_row):
    keys_out = jnp.dot(features, master.astype(jnp.bfloat16), preferred_element_type=jnp.float32) * D ** (-0.5)
    positions = jnp.arange(TOKENS, dtype=jnp.int32)
    sequence_ids = (positions // SLOT).astype(jnp.int32)
    own_lengths = jnp.take(lengths_row, sequence_ids)
    live_mask = positions % SLOT < own_lengths
    residual = jnp.where(live_mask[:, None], keys_out - wanted.astype(jnp.float32), 0.0).astype(jnp.bfloat16)
    grouped_features = features.reshape(N_FSDP, TOK_DEV, D).astype(jnp.float32)
    grouped_residual = residual.reshape(N_FSDP, TOK_DEV, KV).astype(jnp.float32)
    partials = jnp.einsum('ftd,ftk->fdk', grouped_features, grouped_residual)
    rounded = lax.optimization_barrier(partials.astype(jnp.bfloat16))
    gradient = lax.optimization_barrier(jnp.sum(rounded.astype(jnp.float32), axis=0))
    square_sum = jnp.sum(gradient * gradient)
    direction = gradient * lax.rsqrt(square_sum / (D * KV) + epsilon)
    return master - learning_rate * direction

def reference(activations, targets, weights, lengths):
    updated = lax.map(lambda items: replica_update(items[0], items[1], items[2], items[3]), (activations, targets, weights, lengths))
    distance_bit = STEP % (N_REPLICA.bit_length() - 1)
    partner_ids = jnp.bitwise_xor(jnp.arange(N_REPLICA, dtype=jnp.int32), 1 << distance_bit).astype(jnp.int32)
    return 0.5 * (updated + updated[partner_ids])
```

```python
import jax
import jax.numpy as jnp
from jax import lax
from jax.sharding import PartitionSpec as P

SLOT = 64
STEP = 3
PARTS = 4

learning_rate = 0.1
epsilon = 1e-06


def swapped(value, axis, bit):
    mask = 2**bit
    pairs = [(source, source ^ mask) for source in range(lax.axis_size(axis))]
    return lax.ppermute(value, axis, pairs)


def moved(value, senders, distance):
    return lax.ppermute(value, "fsdp", [(source, source + distance) for source in senders])


def gathered(own, members, index):
    rights, lefts = [own], [own]
    for i in range(1, members):
        rights.append(moved(rights[-1], range(i - 1, members - 1), 1))
        lefts.append(moved(lefts[-1], range(1, members - i + 1), -1))
    return [own] + [
        jnp.where(index >= i, rights[i], lefts[members - i]) for i in range(1, members)
    ]


def reduced(terms, members):
    def added(received, term):
        return (received.astype(jnp.float32) + term.astype(jnp.float32)).astype(term.dtype)

    right, left = terms[members - 1], terms[1]
    for i in range(1, members):
        right = moved(right, range(0, i), 1)
        left = moved(left, range(members - i, members), -1)
        if i < members - 1:
            right = added(right, terms[members - i - 1])
            left = added(left, terms[i + 1])
    return terms[0].astype(jnp.float32) + right.astype(jnp.float32) + left.astype(jnp.float32)


def local(activations, targets, weights, lengths):
    features = activations[0]
    wanted = targets[0]
    master = weights[0]
    lengths_row = lengths[0]
    tokens_here = features.shape[0]
    local_rows, columns = master.shape
    members = lax.axis_size("fsdp")
    index = lax.axis_index("fsdp")
    distance_bit = STEP % (lax.axis_size("replica").bit_length() - 1)
    width = columns // PARTS

    sequences_here = tokens_here // SLOT
    local_lengths = lax.dynamic_slice_in_dim(lengths_row, index * sequences_here, sequences_here)
    slot_positions = jnp.arange(SLOT, dtype=jnp.int32)
    live = (slot_positions[None, :] < local_lengths[:, None]).reshape(tokens_here)[:, None]

    blocks = [
        lax.dynamic_slice_in_dim(features, ((index + i) % members) * local_rows, local_rows, axis=1)
        for i in range(members)
    ]
    low = master.astype(jnp.bfloat16)
    halves = 0.5 * (master + swapped(master, "replica", distance_bit))

    gradients, partners = [], []
    for part in range(PARTS):
        cut = slice(part * width, (part + 1) * width)
        weight_blocks = gathered(low[:, cut], members, index)
        projected = sum(
            jnp.dot(
                blocks[(members - i) % members],
                weight_blocks[i],
                preferred_element_type=jnp.float32,
            )
            for i in range(members)
        )
        keys_out = projected * features.shape[1] ** (-0.5)
        residual = jnp.where(live, keys_out - wanted[:, cut].astype(jnp.float32), 0.0).astype(
            jnp.bfloat16
        )
        terms = [
            lax.dot_general(
                block, residual, (((0,), (0,)), ((), ())), preferred_element_type=jnp.float32
            ).astype(jnp.bfloat16)
            for block in blocks
        ]
        gradient = reduced(terms, members)
        gradients.append(gradient)
        partners.append(swapped(gradient, "replica", distance_bit))

    squares = jnp.stack(
        [sum(jnp.sum(g * g) for g in gradients), sum(jnp.sum(g * g) for g in partners)]
    )
    total = squares
    for i in range(1, members):
        ring = [(source, (source + i) % members) for source in range(members)]
        total = total + lax.ppermute(squares, "fsdp", ring)
    scales = lax.rsqrt(total / (members * local_rows * columns) + epsilon)
    step = 0.5 * learning_rate
    averaged = [
        halves[:, part * width : (part + 1) * width]
        - step * (gradients[part] * scales[0] + partners[part] * scales[1])
        for part in range(PARTS)
    ]
    return jnp.concatenate(averaged, axis=1)[None]


def solution(mesh):
    return jax.shard_map(
        local,
        mesh=mesh,
        in_specs=(
            P("replica", "fsdp", None),
            P("replica", "fsdp", None),
            P("replica", "fsdp", None),
            P("replica", None),
        ),
        out_specs=P("replica", "fsdp", None),
        check_vma=False,
    )
```

```python
import functools

import jax
import jax.numpy as jnp
from jax import lax
from jax.sharding import PartitionSpec as P

SLOT = 64
STEP = 3

learning_rate = 0.1
epsilon = 1e-06


def swapped(value, axis, bit):
    mask = 2**bit
    pairs = [(source, source ^ mask) for source in range(lax.axis_size(axis))]
    return lax.ppermute(value, axis, pairs)


def turned(value, distance):
    members = lax.axis_size("fsdp")
    ring = [(source, (source + distance) % members) for source in range(members)]
    return lax.ppermute(value, "fsdp", ring)


def capacities(tokens_here):
    first = -(-(tokens_here // 2 + 32) // 16) * 16
    return [c for c in range(first, first + 80, 16) if c < tokens_here] + [
        c for c in range(first + 96, tokens_here, 32)
    ] + [tokens_here]


def own_gradient(capacity, features, wanted, low, place, live):
    members = lax.axis_size("fsdp")
    index = lax.axis_index("fsdp")
    local_rows = low.shape[0]
    slots = jnp.arange(capacity, dtype=jnp.int32)
    pick = ((slots[:, None] == place[None, :]) & live[None, :]).astype(jnp.bfloat16)

    def picked(array):
        return jnp.dot(pick, array, preferred_element_type=jnp.float32).astype(jnp.bfloat16)

    def block(i):
        start = ((index + i) % members) * local_rows
        return lax.dynamic_slice_in_dim(features, start, local_rows, axis=1)

    held = [picked(block(i)) for i in range(members)]
    held = [held[0]] + [turned(held[i], i) for i in range(1, members)]
    parts = [jnp.dot(h, low, preferred_element_type=jnp.float32) for h in held]
    keys_out = parts[0]
    for i in range(1, members):
        keys_out = keys_out + turned(parts[i].astype(jnp.bfloat16), -i).astype(jnp.float32)
    keys_out = keys_out * features.shape[1] ** (-0.5)
    residual = (keys_out - picked(wanted).astype(jnp.float32)).astype(jnp.bfloat16)
    gradient = 0.0
    for i in range(members):
        gradient = gradient + lax.dot_general(
            held[i],
            turned(residual, i) if i else residual,
            (((0,), (0,)), ((), ())),
            preferred_element_type=jnp.float32,
        )
    return gradient


def local(activations, targets, weights, lengths):
    features = activations[0]
    wanted = targets[0]
    master = weights[0]
    lengths_row = lengths[0]
    tokens_here = features.shape[0]
    local_rows, columns = master.shape
    members = lax.axis_size("fsdp")
    index = lax.axis_index("fsdp")
    distance_bit = STEP % (lax.axis_size("replica").bit_length() - 1)

    sequences_here = tokens_here // SLOT
    per_member = lengths_row.reshape(members, sequences_here)
    own_lengths = lax.dynamic_index_in_dim(per_member, index, 0, keepdims=False)
    starts = jnp.cumsum(own_lengths) - own_lengths
    slot_positions = jnp.arange(SLOT, dtype=jnp.int32)
    live = (slot_positions[None, :] < own_lengths[:, None]).reshape(tokens_here)
    place = (slot_positions[None, :] + starts[:, None]).reshape(tokens_here)

    sizes = capacities(tokens_here)
    most = jnp.max(jnp.sum(per_member, axis=1))
    choice = sum((most > size).astype(jnp.int32) for size in sizes[:-1])
    gradient = lax.switch(
        choice,
        [functools.partial(own_gradient, size) for size in sizes],
        features,
        wanted,
        master.astype(jnp.bfloat16),
        place,
        live,
    )

    square = jnp.sum(gradient * gradient)
    total = square
    for i in range(1, members):
        total = total + turned(square, i)
    scale = lax.rsqrt(total / (members * local_rows * columns) + epsilon)
    updated = master - learning_rate * (gradient * scale)
    averaged = 0.5 * (updated + swapped(updated, "replica", distance_bit))
    return averaged[None]


def solution(mesh):
    return jax.shard_map(
        local,
        mesh=mesh,
        in_specs=(
            P("replica", "fsdp", None),
            P("replica", "fsdp", None),
            P("replica", "fsdp", None),
            P("replica", None),
        ),
        out_specs=P("replica", "fsdp", None),
        check_vma=False,
    )
```

```python
import functools

import jax
import jax.numpy as jnp
from jax import lax
from jax.experimental import pallas as pl
from jax.experimental.pallas import tpu as pltpu
from jax.sharding import PartitionSpec as P

SLOT = 64
STEP = 3
ALIGN = 16
MORE = 32

learning_rate = 0.1
epsilon = 1e-06


def swapped(value, axis, bit):
    mask = 2**bit
    pairs = [(source, source ^ mask) for source in range(lax.axis_size(axis))]
    return lax.ppermute(value, axis, pairs)


def turned(value, distance):
    members = lax.axis_size("fsdp")
    ring = [(source, (source + distance) % members) for source in range(members)]
    return lax.ppermute(value, "fsdp", ring)


def live_before(lengths_ref, sequence):
    total = jnp.int32(0)
    for q in range(lengths_ref.shape[1]):
        total = total + jnp.where(q < sequence, lengths_ref[0, q], 0)
    return total


def aligned(place):
    return pl.multiple_of(place // ALIGN * ALIGN, ALIGN)


def picking(lengths_ref, member, rows, tokens):
    sequences = tokens // SLOT
    place = live_before(lengths_ref, member * sequences) % ALIGN
    slot = lax.broadcasted_iota(jnp.int32, (1, tokens), 1)
    places = jnp.full((1, tokens), -1, jnp.int32)
    for s in range(sequences):
        length = lengths_ref[0, member * sequences + s]
        position = slot - s * SLOT
        places = jnp.where((position >= 0) & (position < length), position + place, places)
        place = place + length
    row = lax.broadcasted_iota(jnp.int32, (rows, tokens), 0)
    return jnp.where(row == places, 1.0, 0.0).astype(jnp.bfloat16)


def compact_kernel(index_ref, lengths_ref, features_ref, first_ref, more_ref):
    first, more = first_ref.shape[0], more_ref.shape[0]
    pick = picking(lengths_ref, index_ref[0], first + more, features_ref.shape[0])
    rows = jnp.dot(pick, features_ref[...], preferred_element_type=jnp.float32)
    rows = rows.astype(jnp.bfloat16)
    first_ref[...] = rows[:first]
    more_ref[...] = rows[first:]


def compacted(features, lengths, index, offset, local_rows, first, more):
    members = lax.axis_size("fsdp")
    tokens = features.shape[0]
    width = min(512, local_rows)
    steps = local_rows // width
    scalars = jnp.stack([index, (index + offset) % members * steps])
    return pl.pallas_call(
        compact_kernel,
        grid_spec=pltpu.PrefetchScalarGridSpec(
            num_scalar_prefetch=2,
            grid=(steps,),
            in_specs=[pl.BlockSpec((tokens, width), lambda j, scalars, lengths: (0, scalars[1] + j))],
            out_specs=[
                pl.BlockSpec((first, width), lambda j, scalars, lengths: (0, j)),
                pl.BlockSpec((more, width), lambda j, scalars, lengths: (0, j)),
            ],
        ),
        out_shape=[
            jax.ShapeDtypeStruct((first, local_rows), jnp.bfloat16),
            jax.ShapeDtypeStruct((more, local_rows), jnp.bfloat16),
        ],
        compiler_params=pltpu.CompilerParams(vmem_limit_bytes=32 * 2**20),
        cost_estimate=pl.CostEstimate(
            flops=2 * (first + more) * tokens * local_rows,
            bytes_accessed=2 * (first + more + tokens) * local_rows,
            transcendentals=0,
        ),
    )(scalars, lengths, features)


def load_rows(held, rows_ref, sems, first, more):
    copies = []
    for i in range(len(held) // 2):
        start = i * (first + more)
        for part, (offset, size) in enumerate(((0, first), (first, more))):
            copy = pltpu.make_async_copy(
                held[2 * i + part], rows_ref.at[pl.ds(start + offset, size)], sems.at[2 * i + part]
            )
            copy.start()
            copies.append(copy)
    return copies


def keys_kernel(members, first, more, scale, index_ref, lengths_ref, targets_ref, master_ref, *refs):
    held, sums = refs[: 2 * members], refs[2 * members : 3 * members]
    rows_ref, low_ref, total_ref, sems = refs[3 * members :]
    index = index_ref[0]
    tokens = targets_ref.shape[0]
    sequences = tokens // SLOT
    share = sums[0].shape[0]
    copies = load_rows(held, rows_ref, sems, first, more)
    low_ref[...] = master_ref[...].astype(jnp.bfloat16)
    total_ref[...] = jnp.zeros_like(total_ref)
    pick = picking(lengths_ref, index, first + more, tokens)
    own_start = aligned(live_before(lengths_ref, index * sequences))
    total_ref[pl.ds(own_start, first + more)] = -jnp.dot(
        pick, targets_ref[...], preferred_element_type=jnp.float32
    )
    for i in range(members):
        member = lax.rem(index + members - i, members)
        begin = live_before(lengths_ref, member * sequences)
        end = live_before(lengths_ref, (member + 1) * sequences)
        start = aligned(begin)

        def add(offset, size, i=i, start=start):
            block = rows_ref[pl.ds(i * (first + more) + offset, size)]
            total_ref[pl.ds(start + offset, size)] += (
                jnp.dot(block, low_ref[...], preferred_element_type=jnp.float32) * scale
            )

        copies[2 * i].wait()
        add(0, first)
        copies[2 * i + 1].wait()
        pl.when(end - start > first)(functools.partial(add, first, more))
    for i in range(members):
        owner = lax.rem(index + i, members)
        block = total_ref[pl.ds(pl.multiple_of(owner * share, ALIGN), share)]
        sums[i][...] = block.astype(sums[i].dtype)


def gradient_kernel(members, first, more, index_ref, lengths_ref, *refs):
    residuals, held = refs[:members], refs[members : 3 * members]
    gradient_ref, squares_ref, rows_ref, all_ref, sems = refs[3 * members :]
    index = index_ref[0]
    share = residuals[0].shape[0]
    sequences = lengths_ref.shape[1] // members
    copies = load_rows(held, rows_ref, sems, first, more)
    rest = first + more
    all_ref[pl.ds(members * share, rest)] = jnp.zeros((rest, all_ref.shape[1]), all_ref.dtype)
    for i in range(members):
        owner = lax.rem(index + members - i, members)
        all_ref[pl.ds(pl.multiple_of(owner * share, ALIGN), share)] = residuals[i][...]
    for i in range(members):
        member = lax.rem(index + members - i, members)
        begin = live_before(lengths_ref, member * sequences)
        end = live_before(lengths_ref, (member + 1) * sequences)
        start = aligned(begin)

        def product(offset, size, i=i, start=start):
            return lax.dot_general(
                rows_ref[pl.ds(i * (first + more) + offset, size)],
                all_ref[pl.ds(start + offset, size)],
                (((0,), (0,)), ((), ())),
                preferred_element_type=jnp.float32,
            )

        def add_more(product=product):
            gradient_ref[...] += product(first, more)

        copies[2 * i].wait()
        if i:
            gradient_ref[...] += product(0, first)
        else:
            gradient_ref[...] = product(0, first)
        copies[2 * i + 1].wait()
        pl.when(end - start > first)(add_more)
    gradient = gradient_ref[...]
    squares = jnp.sum((gradient * gradient).reshape(-1, 8, gradient.shape[1]), axis=0)
    lanes = squares.shape[1] // 128
    squares_ref[...] = sum(squares[:, 128 * j : 128 * (j + 1)] for j in range(lanes))


def local(activations, targets, weights, lengths):
    features = activations[0]
    wanted = targets[0]
    master = weights[0]
    tokens_here = features.shape[0]
    local_rows, columns = master.shape
    members = lax.axis_size("fsdp")
    index = lax.axis_index("fsdp")
    distance_bit = STEP % (lax.axis_size("replica").bit_length() - 1)
    share = tokens_here // 2
    first = -(-(share + 32) // MORE) * MORE
    more = -(-(tokens_here + ALIGN - first) // MORE) * MORE

    partner_master = swapped(master, "replica", distance_bit)

    sent = [
        compacted(features, lengths, index, i, local_rows, first, more) for i in range(members)
    ]
    held_first = [sent[0][0]] + [turned(sent[i][0], i) for i in range(1, members)]

    per_member = jnp.sum(lengths.reshape(members, -1), axis=1)
    begins = jnp.cumsum(per_member) - per_member
    longest = jnp.max(per_member + begins % ALIGN)
    steps = (jnp.maximum(longest - first, 0) + MORE - 1) // MORE

    def more_step(carry):
        step, arrays = carry
        start = step * MORE
        moved = [
            turned(lax.dynamic_slice_in_dim(sent[i][1], start, MORE), i) for i in range(1, members)
        ]
        arrays = [
            lax.dynamic_update_slice_in_dim(array, block, start, 0)
            for array, block in zip(arrays, moved)
        ]
        return step + 1, arrays

    _, held_more = lax.while_loop(
        lambda carry: carry[0] < steps,
        more_step,
        (jnp.int32(0), [jnp.zeros((more, local_rows), jnp.bfloat16) for _ in range(1, members)]),
    )
    held_more = [sent[0][1]] + list(held_more)
    held = [array for pair in zip(held_first, held_more) for array in pair]

    vmem = pl.BlockSpec(memory_space=pltpu.VMEM)
    anywhere = pl.BlockSpec(memory_space=pl.ANY)
    smem = pl.BlockSpec(memory_space=pltpu.SMEM)
    scalars = jnp.stack([index, index])
    params = pltpu.CompilerParams(vmem_limit_bytes=48 * 2**20)
    sums = pl.pallas_call(
        functools.partial(keys_kernel, members, first, more, features.shape[1] ** (-0.5)),
        in_specs=[smem, smem, vmem, vmem] + [anywhere] * (2 * members),
        out_specs=[vmem] * members,
        out_shape=[
            jax.ShapeDtypeStruct((share, columns), jnp.bfloat16 if i else jnp.float32)
            for i in range(members)
        ],
        scratch_shapes=[
            pltpu.VMEM((members * (first + more), local_rows), jnp.bfloat16),
            pltpu.VMEM((local_rows, columns), jnp.bfloat16),
            pltpu.VMEM((members * share + first + more, columns), jnp.float32),
            pltpu.SemaphoreType.DMA((2 * members,)),
        ],
        compiler_params=params,
    )(scalars, lengths, wanted, master, *held)

    residual = sums[0]
    for i in range(1, members):
        residual = residual + turned(sums[i], i).astype(jnp.float32)
    residual = residual.astype(jnp.bfloat16)
    residuals = [residual] + [turned(residual, i) for i in range(1, members)]

    gradient, squares = pl.pallas_call(
        functools.partial(gradient_kernel, members, first, more),
        in_specs=[smem, smem] + [vmem] * members + [anywhere] * (2 * members),
        out_specs=[vmem, vmem],
        out_shape=[
            jax.ShapeDtypeStruct((local_rows, columns), jnp.float32),
            jax.ShapeDtypeStruct((8, 128), jnp.float32),
        ],
        scratch_shapes=[
            pltpu.VMEM((members * (first + more), local_rows), jnp.bfloat16),
            pltpu.VMEM((members * share + first + more, columns), jnp.bfloat16),
            pltpu.SemaphoreType.DMA((2 * members,)),
        ],
        compiler_params=params,
    )(scalars, lengths, *residuals, *held)

    partner_gradient = swapped(gradient, "replica", distance_bit)
    total = squares
    for i in range(1, members):
        total = total + turned(squares, i)
    both = jnp.stack([jnp.sum(total), jnp.sum(swapped(total, "replica", distance_bit))])
    scales = lax.rsqrt(both / (members * local_rows * columns) + epsilon)
    averaged = 0.5 * (master + partner_master) - (0.5 * learning_rate) * (
        gradient * scales[0] + partner_gradient * scales[1]
    )
    return averaged[None]


def solution(mesh):
    return jax.shard_map(
        local,
        mesh=mesh,
        in_specs=(
            P("replica", "fsdp", None),
            P("replica", "fsdp", None),
            P("replica", "fsdp", None),
            P("replica", None),
        ),
        out_specs=P("replica", "fsdp", None),
        check_vma=False,
    )
```

```python
import functools

import jax
import jax.numpy as jnp
from jax import lax
from jax.experimental import pallas as pl
from jax.experimental.pallas import tpu as pltpu
from jax.sharding import PartitionSpec as P

SLOT = 64
STEP = 3
ALIGN = 16
MORE = 32

learning_rate = 0.1
epsilon = 1e-06


def swapped(value, axis, bit):
    mask = 2**bit
    pairs = [(source, source ^ mask) for source in range(lax.axis_size(axis))]
    return lax.ppermute(value, axis, pairs)


def turned(value, distance):
    members = lax.axis_size("fsdp")
    ring = [(source, (source + distance) % members) for source in range(members)]
    return lax.ppermute(value, "fsdp", ring)


def live_before(lengths_ref, sequence):
    total = jnp.int32(0)
    for q in range(lengths_ref.shape[1]):
        total = total + jnp.where(q < sequence, lengths_ref[0, q], 0)
    return total


def aligned(place):
    return pl.multiple_of(place // ALIGN * ALIGN, ALIGN)


def picking(lengths_ref, member, rows, tokens):
    sequences = tokens // SLOT
    place = live_before(lengths_ref, member * sequences) % ALIGN
    slot = lax.broadcasted_iota(jnp.int32, (1, tokens), 1)
    places = jnp.full((1, tokens), -1, jnp.int32)
    for s in range(sequences):
        length = lengths_ref[0, member * sequences + s]
        position = slot - s * SLOT
        places = jnp.where((position >= 0) & (position < length), position + place, places)
        place = place + length
    row = lax.broadcasted_iota(jnp.int32, (rows, tokens), 0)
    return jnp.where(row == places, 1.0, 0.0).astype(jnp.bfloat16)


def compact_kernel(first, index_ref, lengths_ref, features_ref, *refs):
    others = (len(refs) - 3) // 2
    outs, (choice_ref, blocks_ref, sems) = refs[: 2 * others], refs[2 * others :]
    index = index_ref[0]
    members = others + 1
    tokens, local_rows = blocks_ref.shape[1:]
    copies = []
    for i in range(others):
        owner = lax.rem(index + i + 1, members)
        columns = pl.ds(pl.multiple_of(owner * local_rows, 128), local_rows)
        copies.append(
            pltpu.make_async_copy(features_ref.at[:, columns], blocks_ref.at[i], sems.at[i])
        )
        copies[-1].start()
    more = outs[1].shape[0]
    longest = jnp.int32(0)
    before = jnp.int32(0)
    sequences = tokens // SLOT
    for member in range(members):
        after = before
        for q in range(sequences):
            after = after + lengths_ref[0, member * sequences + q]
        longest = jnp.maximum(longest, after - aligned(before))
        before = after
    choice = jnp.int32(0)
    for size in more_sizes(more)[:-1]:
        choice = choice + jnp.where(longest > first + size, 1, 0)
    choice_ref[0] = choice
    pick = picking(lengths_ref, index, first + more, tokens)
    width = min(256, local_rows)
    for i in range(others):
        copies[i].wait()

        @pl.loop(0, local_rows // width)
        def _(j, i=i):
            columns = pl.ds(pl.multiple_of(j * width, width), width)
            rows = jnp.dot(pick, blocks_ref[i, :, columns], preferred_element_type=jnp.float32)
            rows = rows.astype(jnp.bfloat16)
            outs[2 * i][:, columns] = rows[:first]
            outs[2 * i + 1][:, columns] = rows[first:]


def own_kernel(
    scale,
    index_ref,
    lengths_ref,
    features_ref,
    targets_ref,
    master_ref,
    partner_ref,
    first_ref,
    more_ref,
    keys_ref,
    low_ref,
    halves_ref,
    block_ref,
    sem,
):
    index = index_ref[0]
    tokens, local_rows = block_ref.shape
    columns = pl.ds(pl.multiple_of(index * local_rows, 128), local_rows)
    copy = pltpu.make_async_copy(features_ref.at[:, columns], block_ref, sem)
    copy.start()
    first, more = first_ref.shape[0], more_ref.shape[0]
    low_ref[...] = master_ref[...].astype(jnp.bfloat16)
    halves_ref[...] = 0.5 * (master_ref[...] + partner_ref[...])
    pick = picking(lengths_ref, index, first + more, tokens)
    copy.wait()
    rows = jnp.dot(pick, block_ref[...], preferred_element_type=jnp.float32).astype(jnp.bfloat16)
    first_ref[...] = rows[:first]
    more_ref[...] = rows[first:]
    keys_ref[...] = jnp.dot(
        rows, low_ref[...], preferred_element_type=jnp.float32
    ) * scale - jnp.dot(pick, targets_ref[...], preferred_element_type=jnp.float32)


def keys_kernel(members, scale, index_ref, lengths_ref, keys_ref, low_ref, *refs):
    held, sums, total_ref = refs[: 2 * members - 2], refs[2 * members - 2 : -1], refs[-1]
    index = index_ref[0]
    sequences = lengths_ref.shape[1] // members
    share = sums[0].shape[0]
    total_ref[...] = jnp.zeros_like(total_ref)
    own_start = aligned(live_before(lengths_ref, index * sequences))
    total_ref[pl.ds(own_start, keys_ref.shape[0])] = keys_ref[...]
    for i in range(1, members):
        member = lax.rem(index + members - i, members)
        end = live_before(lengths_ref, (member + 1) * sequences)
        start = aligned(live_before(lengths_ref, member * sequences))
        first_ref, more_ref = held[2 * i - 2 : 2 * i]
        first = first_ref.shape[0]

        def add(ref, offset, start=start):
            total_ref[pl.ds(start + offset, ref.shape[0])] += (
                jnp.dot(ref[...], low_ref[...], preferred_element_type=jnp.float32) * scale
            )

        add(first_ref, 0)
        pl.when(end - start > first)(functools.partial(add, more_ref, first))
    for i in range(members):
        owner = lax.rem(index + i, members)
        block = total_ref[pl.ds(pl.multiple_of(owner * share, ALIGN), share)]
        sums[i][...] = block.astype(sums[i].dtype)


def gradient_kernel(members, index_ref, lengths_ref, *refs):
    residuals, held = refs[:members], refs[members : 3 * members]
    gradient_ref, low_ref, squares_ref, all_ref = refs[3 * members :]
    index = index_ref[0]
    share = residuals[0].shape[0]
    first, more = held[0].shape[0], held[1].shape[0]
    sequences = lengths_ref.shape[1] // members
    rest = first + more
    all_ref[pl.ds(members * share, rest)] = jnp.zeros((rest, all_ref.shape[1]), all_ref.dtype)
    for i in range(members):
        owner = lax.rem(index + members - i, members)
        all_ref[pl.ds(pl.multiple_of(owner * share, ALIGN), share)] = residuals[i][...]
    for i in range(members):
        member = lax.rem(index + members - i, members)
        end = live_before(lengths_ref, (member + 1) * sequences)
        start = aligned(live_before(lengths_ref, member * sequences))

        def product(ref, offset, start=start):
            return lax.dot_general(
                ref[...],
                all_ref[pl.ds(start + offset, ref.shape[0])],
                (((0,), (0,)), ((), ())),
                preferred_element_type=jnp.float32,
            )

        def add_more(product=product, ref=held[2 * i + 1]):
            gradient_ref[...] += product(ref, first)

        if i:
            gradient_ref[...] += product(held[2 * i], 0)
        else:
            gradient_ref[...] = product(held[2 * i], 0)
        pl.when(end - start > first)(add_more)
    gradient = gradient_ref[...]
    low_ref[...] = gradient.astype(low_ref.dtype)
    squares = jnp.sum((gradient * gradient).reshape(-1, 8, gradient.shape[1]), axis=0)
    lanes = squares.shape[1] // 128
    squares_ref[...] = sum(squares[:, 128 * j : 128 * (j + 1)] for j in range(lanes))


def average_kernel(entries, own_ref, other_ref, halves_ref, gradient_ref, partner_ref, out_ref):
    half = 0.5 * learning_rate
    own = half * lax.rsqrt(jnp.sum(own_ref[...], keepdims=True) / entries + epsilon)
    other = half * lax.rsqrt(jnp.sum(other_ref[...], keepdims=True) / entries + epsilon)
    out_ref[...] = (
        halves_ref[...]
        - gradient_ref[...] * own
        - partner_ref[...].astype(jnp.float32) * other
    )


def more_sizes(more):
    return [0] + [size for size in (32, 64, 96) if size < more] + [more]


def more_rows(size, blocks):
    members = lax.axis_size("fsdp")
    if size == 0:
        return [jnp.zeros_like(block) for block in blocks]
    moved = [turned(blocks[i - 1][:size], i) for i in range(1, members)]
    return [jnp.pad(m, ((0, b.shape[0] - size), (0, 0))) for m, b in zip(moved, blocks)]


def local(activations, targets, weights, lengths):
    features = activations[0]
    wanted = targets[0]
    master = weights[0]
    tokens_here = features.shape[0]
    local_rows, columns = master.shape
    members = lax.axis_size("fsdp")
    index = lax.axis_index("fsdp")
    distance_bit = STEP % (lax.axis_size("replica").bit_length() - 1)
    share = tokens_here // 2
    first = -(-(share + 64) // MORE) * MORE
    more = -(-(tokens_here + ALIGN - first) // MORE) * MORE
    scale = features.shape[1] ** (-0.5)

    vmem = pl.BlockSpec(memory_space=pltpu.VMEM)
    anywhere = pl.BlockSpec(memory_space=pl.ANY)
    smem = pl.BlockSpec(memory_space=pltpu.SMEM)
    params = pltpu.CompilerParams(vmem_limit_bytes=40 * 2**20)
    scalars = jnp.stack([index, index])
    first_shape = jax.ShapeDtypeStruct((first, local_rows), jnp.bfloat16)
    more_shape = jax.ShapeDtypeStruct((more, local_rows), jnp.bfloat16)

    partner_master = swapped(master, "replica", distance_bit)

    *sent, choice = pl.pallas_call(
        functools.partial(compact_kernel, first),
        in_specs=[smem, smem, anywhere],
        out_specs=[vmem] * (2 * members - 2) + [smem],
        out_shape=[first_shape, more_shape] * (members - 1) + [jax.ShapeDtypeStruct((1,), jnp.int32)],
        scratch_shapes=[
            pltpu.VMEM((members - 1, tokens_here, local_rows), jnp.bfloat16),
            pltpu.SemaphoreType.DMA((members - 1,)),
        ],
        compiler_params=pltpu.CompilerParams(vmem_limit_bytes=56 * 2**20),
    )(scalars, lengths, features)

    held_first = [turned(sent[2 * i - 2], i) for i in range(1, members)]
    held_more = lax.switch(
        choice[0], [functools.partial(more_rows, size) for size in more_sizes(more)], sent[1::2]
    )
    held = [array for pair in zip(held_first, held_more) for array in pair]

    own_first, own_more, own_keys, low, halves = pl.pallas_call(
        functools.partial(own_kernel, scale),
        in_specs=[smem, smem, anywhere, vmem, vmem, vmem],
        out_specs=[vmem] * 5,
        out_shape=[
            first_shape,
            more_shape,
            jax.ShapeDtypeStruct((first + more, columns), jnp.float32),
            jax.ShapeDtypeStruct((local_rows, columns), jnp.bfloat16),
            jax.ShapeDtypeStruct((local_rows, columns), jnp.float32),
        ],
        scratch_shapes=[
            pltpu.VMEM((tokens_here, local_rows), jnp.bfloat16),
            pltpu.SemaphoreType.DMA,
        ],
        compiler_params=params,
        cost_estimate=pl.CostEstimate(
            flops=2 * (first + more) * local_rows * (tokens_here + columns),
            bytes_accessed=20 * local_rows * columns,
            transcendentals=0,
        ),
    )(scalars, lengths, features, wanted, master, partner_master)

    sums = pl.pallas_call(
        functools.partial(keys_kernel, members, scale),
        in_specs=[smem, smem, vmem, vmem] + [vmem] * (2 * members - 2),
        out_specs=[vmem] * members,
        out_shape=[
            jax.ShapeDtypeStruct((share, columns), jnp.bfloat16 if i else jnp.float32)
            for i in range(members)
        ],
        scratch_shapes=[pltpu.VMEM((members * share + first + more, columns), jnp.float32)],
        compiler_params=params,
    )(scalars, lengths, own_keys, low, *held)

    residual = sums[0]
    for i in range(1, members):
        residual = residual + turned(sums[i], i).astype(jnp.float32)
    residual = residual.astype(jnp.bfloat16)
    residuals = [residual] + [turned(residual, i) for i in range(1, members)]

    gradient, low_gradient, squares = pl.pallas_call(
        functools.partial(gradient_kernel, members),
        in_specs=[smem, smem] + [vmem] * (3 * members),
        out_specs=[vmem] * 3,
        out_shape=[
            jax.ShapeDtypeStruct((local_rows, columns), jnp.float32),
            jax.ShapeDtypeStruct((local_rows, columns), jnp.bfloat16),
            jax.ShapeDtypeStruct((8, 128), jnp.float32),
        ],
        scratch_shapes=[pltpu.VMEM((members * share + first + more, columns), jnp.bfloat16)],
        compiler_params=params,
    )(scalars, lengths, *residuals, own_first, own_more, *held)

    partner_gradient = swapped(low_gradient, "replica", distance_bit)
    total = squares
    for i in range(1, members):
        total = total + turned(squares, i)
    partner_total = swapped(total, "replica", distance_bit)

    rows = min(256, local_rows)
    whole = pl.BlockSpec((8, 128), lambda j: (0, 0))
    tile = pl.BlockSpec((rows, columns), lambda j: (j, 0))
    averaged = pl.pallas_call(
        functools.partial(average_kernel, members * local_rows * columns),
        grid=(local_rows // rows,),
        in_specs=[whole, whole, tile, tile, tile],
        out_specs=tile,
        out_shape=jax.ShapeDtypeStruct((local_rows, columns), jnp.float32),
    )(total, partner_total, halves, gradient, partner_gradient)
    return averaged[None]


def solution(mesh):
    return jax.shard_map(
        local,
        mesh=mesh,
        in_specs=(
            P("replica", "fsdp", None),
            P("replica", "fsdp", None),
            P("replica", "fsdp", None),
            P("replica", None),
        ),
        out_specs=P("replica", "fsdp", None),
        check_vma=False,
    )
```

```python
import functools

import jax
import jax.numpy as jnp
from jax import lax
from jax.experimental import pallas as pl
from jax.experimental.pallas import tpu as pltpu
from jax.sharding import PartitionSpec as P

SLOT = 64
STEP = 3
ALIGN = 16
MORE = 32

learning_rate = 0.1
epsilon = 1e-06


def swapped(value, axis, bit):
    mask = 2**bit
    pairs = [(source, source ^ mask) for source in range(lax.axis_size(axis))]
    return lax.ppermute(value, axis, pairs)


def turned(value, distance):
    members = lax.axis_size("fsdp")
    ring = [(source, (source + distance) % members) for source in range(members)]
    return lax.ppermute(value, "fsdp", ring)


def live_before(lengths_ref, sequence):
    total = jnp.int32(0)
    for q in range(lengths_ref.shape[1]):
        total = total + jnp.where(q < sequence, lengths_ref[0, q], 0)
    return total


def aligned(place):
    return pl.multiple_of(place // ALIGN * ALIGN, ALIGN)


def picking(lengths_ref, member, rows, tokens):
    sequences = tokens // SLOT
    place = live_before(lengths_ref, member * sequences) % ALIGN
    slot = lax.broadcasted_iota(jnp.int32, (1, tokens), 1)
    places = jnp.full((1, tokens), -1, jnp.int32)
    for s in range(sequences):
        length = lengths_ref[0, member * sequences + s]
        position = slot - s * SLOT
        places = jnp.where((position >= 0) & (position < length), position + place, places)
        place = place + length
    row = lax.broadcasted_iota(jnp.int32, (rows, tokens), 0)
    return jnp.where(row == places, 1.0, 0.0).astype(jnp.bfloat16)


def compact(lengths_ref, member, block, first_ref, more_ref):
    tokens, local_rows = block.shape
    first, more = first_ref.shape[0], more_ref.shape[0]
    sequences = tokens // SLOT
    pick = picking(lengths_ref, member, first + more, tokens)
    end = live_before(lengths_ref, (member + 1) * sequences)
    start = aligned(live_before(lengths_ref, member * sequences))
    width = min(256, local_rows)

    def rows(part, ref):
        @pl.loop(0, local_rows // width)
        def _(j):
            columns = pl.ds(pl.multiple_of(j * width, width), width)
            ref[:, columns] = jnp.dot(
                part, block[:, columns], preferred_element_type=jnp.float32
            ).astype(ref.dtype)

    rows(pick[:first], first_ref)
    needed = end - start > first

    @pl.when(needed)
    def _():
        rows(pick[first:], more_ref)

    @pl.when(jnp.logical_not(needed))
    def _():
        more_ref[...] = jnp.zeros_like(more_ref)

    return pick


def feature_copy(features_ref, member, block_ref, sem):
    local_rows = block_ref.shape[1]
    columns = pl.ds(pl.multiple_of(member * local_rows, 128), local_rows)
    return pltpu.make_async_copy(features_ref.at[:, columns], block_ref, sem)


def sent_kernel(members, offset, index_ref, lengths_ref, features_ref, first_ref, more_ref, block_ref, sem):
    index = index_ref[0]
    copy = feature_copy(features_ref, lax.rem(index + offset, members), block_ref, sem)
    copy.start()
    copy.wait()
    compact(lengths_ref, index, block_ref, first_ref, more_ref)


def own_kernel(
    members,
    index_ref,
    lengths_ref,
    features_ref,
    targets_ref,
    master_ref,
    partner_ref,
    first_ref,
    more_ref,
    wanted_ref,
    low_ref,
    halves_ref,
    choice_ref,
    block_ref,
    sem,
):
    index = index_ref[0]
    copy = feature_copy(features_ref, index, block_ref, sem)
    copy.start()
    low_ref[...] = master_ref[...].astype(jnp.bfloat16)
    halves_ref[...] = 0.5 * (master_ref[...] + partner_ref[...])
    first, more = first_ref.shape[0], more_ref.shape[0]
    sequences = block_ref.shape[0] // SLOT
    longest = jnp.int32(0)
    before = jnp.int32(0)
    for member in range(members):
        after = before
        for q in range(sequences):
            after = after + lengths_ref[0, member * sequences + q]
        longest = jnp.maximum(longest, after - aligned(before))
        before = after
    choice = jnp.int32(0)
    for size in more_sizes(more)[:-1]:
        choice = choice + jnp.where(longest > first + size, 1, 0)
    choice_ref[0] = choice
    copy.wait()
    pick = compact(lengths_ref, index, block_ref, first_ref, more_ref)
    wanted_ref[...] = jnp.dot(pick, targets_ref[...], preferred_element_type=jnp.float32)


def keys_kernel(members, scale, index_ref, lengths_ref, wanted_ref, low_ref, *refs):
    held, sums = refs[: 2 * members], refs[2 * members : 3 * members]
    all_ref, total_ref = refs[3 * members :]
    index = index_ref[0]
    sequences = lengths_ref.shape[1] // members
    share = sums[0].shape[0]
    all_ref[...] = jnp.zeros_like(all_ref)
    for i in range(members):
        member = lax.rem(index + members - i, members)
        end = live_before(lengths_ref, (member + 1) * sequences)
        start = aligned(live_before(lengths_ref, member * sequences))
        first_ref, more_ref = held[2 * i : 2 * i + 2]
        first = first_ref.shape[0]

        def add(ref, offset, start=start):
            all_ref[pl.ds(start + offset, ref.shape[0])] += ref[...]

        add(first_ref, 0)
        pl.when(end - start > first)(functools.partial(add, more_ref, first))

    @pl.loop(0, members)
    def _(j):
        rows = pl.ds(pl.multiple_of(j * share, ALIGN), share)
        total_ref[rows] = (
            jnp.dot(all_ref[rows], low_ref[...], preferred_element_type=jnp.float32) * scale
        )

    own_start = aligned(live_before(lengths_ref, index * sequences))
    total_ref[pl.ds(own_start, wanted_ref.shape[0])] -= wanted_ref[...]
    for i in range(members):
        owner = lax.rem(index + i, members)
        block = total_ref[pl.ds(pl.multiple_of(owner * share, ALIGN), share)]
        sums[i][...] = block.astype(sums[i].dtype)


def turn_kernel(all_ref, turned_ref):
    for start in range(0, turned_ref.shape[1], 128):
        turned_ref[:, start : start + 128] = all_ref[start : start + 128, :].T


def gradient_kernel(members, index_ref, turned_ref, *refs):
    residuals, (gradient_ref, low_ref, squares_ref, all_ref) = refs[:members], refs[members:]
    index = index_ref[0]
    share = residuals[0].shape[0]
    for i in range(members):
        owner = lax.rem(index + members - i, members)
        all_ref[pl.ds(pl.multiple_of(owner * share, ALIGN), share)] = residuals[i][...]
    squares_ref[...] = jnp.zeros_like(squares_ref)
    height = min(256, turned_ref.shape[0])

    @pl.loop(0, turned_ref.shape[0] // height)
    def _(j):
        rows = pl.ds(pl.multiple_of(j * height, height), height)
        gradient = jnp.dot(turned_ref[rows], all_ref[...], preferred_element_type=jnp.float32)
        gradient_ref[rows] = gradient
        low_ref[rows] = gradient.astype(low_ref.dtype)
        squares = jnp.sum((gradient * gradient).reshape(-1, 8, gradient.shape[1]), axis=0)
        lanes = squares.shape[1] // 128
        squares_ref[...] += sum(squares[:, 128 * k : 128 * (k + 1)] for k in range(lanes))


def average_kernel(entries, own_ref, other_ref, halves_ref, gradient_ref, partner_ref, out_ref, done_ref, sems):
    half = 0.5 * learning_rate
    own = half * lax.rsqrt(jnp.sum(own_ref[...], keepdims=True) / entries + epsilon)
    other = half * lax.rsqrt(jnp.sum(other_ref[...], keepdims=True) / entries + epsilon)
    pieces = sems.shape[0]
    height = done_ref.shape[0] // pieces
    copies = []
    for j in range(pieces):
        rows = pl.ds(j * height, height)
        done_ref[rows] = (
            halves_ref[rows]
            - gradient_ref[rows] * own
            - partner_ref[rows].astype(jnp.float32) * other
        )
        copies.append(pltpu.make_async_copy(done_ref.at[rows], out_ref.at[rows], sems.at[j]))
        copies[-1].start()
    for copy in copies:
        copy.wait()


def more_sizes(more):
    return [0] + [size for size in (16, 32, 48, 64, 80, 96, 128, 160) if size < more] + [more]


def more_rows(size, blocks):
    members = lax.axis_size("fsdp")
    if size == 0:
        return [jnp.zeros_like(block) for block in blocks]
    moved = [turned(blocks[i - 1][:size], i) for i in range(1, members)]
    return [jnp.pad(m, ((0, b.shape[0] - size), (0, 0))) for m, b in zip(moved, blocks)]


def local(activations, targets, weights, lengths):
    features = activations[0]
    wanted = targets[0]
    master = weights[0]
    tokens_here = features.shape[0]
    local_rows, columns = master.shape
    members = lax.axis_size("fsdp")
    index = lax.axis_index("fsdp")
    distance_bit = STEP % (lax.axis_size("replica").bit_length() - 1)
    share = tokens_here // 2
    first = -(-(share + 32) // MORE) * MORE
    more = -(-(tokens_here + ALIGN - first) // MORE) * MORE
    scale = features.shape[1] ** (-0.5)
    places = members * share + first + more

    vmem = pl.BlockSpec(memory_space=pltpu.VMEM)
    anywhere = pl.BlockSpec(memory_space=pl.ANY)
    smem = pl.BlockSpec(memory_space=pltpu.SMEM)
    params = pltpu.CompilerParams(vmem_limit_bytes=40 * 2**20)
    scalars = jnp.stack([index, index])

    def array(rows, width, dtype):
        return jax.ShapeDtypeStruct((rows, width), dtype)

    def cost(flops, moved):
        return pl.CostEstimate(flops=flops, bytes_accessed=moved, transcendentals=0)

    first_shape = array(first, local_rows, jnp.bfloat16)
    more_shape = array(more, local_rows, jnp.bfloat16)
    block_scratch = [pltpu.VMEM((tokens_here, local_rows), jnp.bfloat16), pltpu.SemaphoreType.DMA]

    sent_more, held_first = [], []
    for i in range(1, members):
        sent, rest = pl.pallas_call(
            functools.partial(sent_kernel, members, i),
            in_specs=[smem, smem, anywhere],
            out_specs=[vmem] * 2,
            out_shape=[first_shape, more_shape],
            scratch_shapes=block_scratch,
            compiler_params=pltpu.CompilerParams(vmem_limit_bytes=56 * 2**20),
            cost_estimate=cost(
                2 * first * tokens_here * local_rows, 2 * (tokens_here + first) * local_rows
            ),
        )(scalars, lengths, features)
        held_first.append(turned(sent, i))
        sent_more.append(rest)

    partner_master = swapped(master, "replica", distance_bit)
    own_first, own_more, own_wanted, low, halves, choice = pl.pallas_call(
        functools.partial(own_kernel, members),
        in_specs=[smem, smem, anywhere, vmem, vmem, vmem],
        out_specs=[vmem] * 5 + [smem],
        out_shape=[
            first_shape,
            more_shape,
            array(first + more, columns, jnp.float32),
            array(local_rows, columns, jnp.bfloat16),
            array(local_rows, columns, jnp.float32),
            jax.ShapeDtypeStruct((1,), jnp.int32),
        ],
        scratch_shapes=block_scratch,
        compiler_params=params,
        cost_estimate=cost(
            2 * (first + more) * tokens_here * (local_rows + columns), 20 * local_rows * columns
        ),
    )(scalars, lengths, features, wanted, master, partner_master)

    held_more = lax.switch(
        choice[0], [functools.partial(more_rows, size) for size in more_sizes(more)], sent_more
    )
    held = [own_first, own_more]
    for pair in zip(held_first, held_more):
        held.extend(pair)

    *sums, rows = pl.pallas_call(
        functools.partial(keys_kernel, members, scale),
        in_specs=[smem, smem, vmem, vmem] + [vmem] * (2 * members),
        out_specs=[vmem] * (members + 1),
        out_shape=[
            array(share, columns, jnp.bfloat16 if i else jnp.float32) for i in range(members)
        ]
        + [array(places, local_rows, jnp.bfloat16)],
        scratch_shapes=[pltpu.VMEM((places, columns), jnp.float32)],
        compiler_params=params,
        cost_estimate=cost(
            2 * members * share * local_rows * columns, 4 * places * (local_rows + columns)
        ),
    )(scalars, lengths, own_wanted, low, *held)

    turned_rows = pl.pallas_call(
        turn_kernel,
        in_specs=[vmem],
        out_specs=vmem,
        out_shape=array(local_rows, members * share, jnp.bfloat16),
        compiler_params=params,
        cost_estimate=cost(0, 4 * members * share * local_rows),
    )(rows)

    residual = sums[0]
    for i in range(1, members):
        residual = residual + turned(sums[i], i).astype(jnp.float32)
    residual = residual.astype(jnp.bfloat16)
    residuals = [residual] + [turned(residual, i) for i in range(1, members)]

    gradient, low_gradient, squares = pl.pallas_call(
        functools.partial(gradient_kernel, members),
        in_specs=[smem, vmem] + [vmem] * members,
        out_specs=[vmem] * 3,
        out_shape=[
            array(local_rows, columns, jnp.float32),
            array(local_rows, columns, jnp.bfloat16),
            array(8, 128, jnp.float32),
        ],
        scratch_shapes=[pltpu.VMEM((members * share, columns), jnp.bfloat16)],
        compiler_params=params,
        cost_estimate=cost(
            2 * members * share * local_rows * columns, 8 * local_rows * columns
        ),
    )(scalars, turned_rows, *residuals)

    partner_gradient = swapped(low_gradient, "replica", distance_bit)
    total = squares
    for i in range(1, members):
        total = total + turned(squares, i)
    partner_total = swapped(total, "replica", distance_bit)

    averaged = pl.pallas_call(
        functools.partial(average_kernel, members * local_rows * columns),
        in_specs=[vmem] * 5,
        out_specs=anywhere,
        out_shape=array(local_rows, columns, jnp.float32),
        scratch_shapes=[
            pltpu.VMEM((local_rows, columns), jnp.float32),
            pltpu.SemaphoreType.DMA((4,)),
        ],
        compiler_params=params,
    )(total, partner_total, halves, gradient, partner_gradient)
    return averaged[None]


def solution(mesh):
    return jax.shard_map(
        local,
        mesh=mesh,
        in_specs=(
            P("replica", "fsdp", None),
            P("replica", "fsdp", None),
            P("replica", "fsdp", None),
            P("replica", None),
        ),
        out_specs=P("replica", "fsdp", None),
        check_vma=False,
    )
```

```python
import functools

import jax
import jax.numpy as jnp
from jax import lax
from jax.experimental import pallas as pl
from jax.experimental.pallas import tpu as pltpu
from jax.sharding import PartitionSpec as P

SLOT = 64
STEP = 3
ALIGN = 16
MORE = 32

learning_rate = 0.1
epsilon = 1e-06


def swapped(value, axis, bit):
    mask = 2**bit
    pairs = [(source, source ^ mask) for source in range(lax.axis_size(axis))]
    return lax.ppermute(value, axis, pairs)


def turned(value, distance):
    members = lax.axis_size("fsdp")
    ring = [(source, (source + distance) % members) for source in range(members)]
    return lax.ppermute(value, "fsdp", ring)


def live_before(lengths_ref, members):
    sequences = lengths_ref.shape[1] // members
    totals = [jnp.int32(0)]
    for member in range(members):
        total = totals[-1]
        for q in range(sequences):
            total = total + lengths_ref[0, member * sequences + q]
        totals.append(total)
    return totals


def chosen(values, index):
    value = values[0]
    for i in range(1, len(values)):
        value = jnp.where(index == i, values[i], value)
    return value


def aligned(place):
    return pl.multiple_of(place // ALIGN * ALIGN, ALIGN)


def token_places(lengths_ref, member, before, tokens):
    sequences = tokens // SLOT
    place = before % ALIGN
    slot = lax.broadcasted_iota(jnp.int32, (1, tokens), 1)
    places = jnp.full((1, tokens), -1, jnp.int32)
    for s in range(sequences):
        length = lengths_ref[0, member * sequences + s]
        position = slot - s * SLOT
        places = jnp.where((position >= 0) & (position < length), position + place, places)
        place = place + length
    return places


def picking(places, start, rows):
    row = lax.broadcasted_iota(jnp.int32, (rows, places.shape[1]), 0) + start
    return jnp.where(row == places, 1.0, 0.0).astype(jnp.bfloat16)


class Block:
    def __init__(self, features_ref, member, block_ref, sems):
        self.block_ref, self.width = block_ref, block_ref.shape[1] // sems.shape[0]
        start = member * block_ref.shape[1]
        self.copies = []
        for j in range(sems.shape[0]):
            there = pl.ds(pl.multiple_of(start + j * self.width, 128), self.width)
            here = pl.ds(j * self.width, self.width)
            copy = pltpu.make_async_copy(
                features_ref.at[:, there], block_ref.at[:, here], sems.at[j]
            )
            copy.start()
            self.copies.append(copy)

    def picked(self, pick, store, wait):
        for j, copy in enumerate(self.copies):
            if wait:
                copy.wait()
            here = slice(j * self.width, (j + 1) * self.width)
            rows = jnp.dot(pick, self.block_ref[:, here], preferred_element_type=jnp.float32)
            store(here, rows.astype(jnp.bfloat16))


def sent_kernel(members, offset, lengths_ref, features_ref, first_ref, more_ref, block_ref, sems):
    index = lax.axis_index("fsdp")
    block = Block(features_ref, lax.rem(index + offset, members), block_ref, sems)
    first, more = first_ref.shape[0], more_ref.shape[0]
    totals = live_before(lengths_ref, members)
    before, end = chosen(totals[:-1], index), chosen(totals[1:], index)
    places = token_places(lengths_ref, index, before, block_ref.shape[0])

    def store_first(here, rows):
        first_ref[:, here] = rows

    def store_more(here, rows):
        more_ref[:, here] = rows

    block.picked(picking(places, 0, first), store_first, True)
    needed = end - aligned(before) > first

    @pl.when(needed)
    def _():
        block.picked(picking(places, first, more), store_more, False)

    @pl.when(jnp.logical_not(needed))
    def _():
        more_ref[...] = jnp.zeros_like(more_ref)


def own_kernel(
    members,
    first,
    more,
    lengths_ref,
    features_ref,
    targets_ref,
    master_ref,
    partner_ref,
    rows_ref,
    wanted_ref,
    low_ref,
    halves_ref,
    choice_ref,
    block_ref,
    sems,
):
    index = lax.axis_index("fsdp")
    block = Block(features_ref, index, block_ref, sems)
    rows_ref[...] = jnp.zeros_like(rows_ref)
    low_ref[...] = master_ref[...].astype(jnp.bfloat16)
    halves_ref[...] = 0.5 * (master_ref[...] + partner_ref[...])
    totals = live_before(lengths_ref, members)
    longest = jnp.int32(0)
    for member in range(members):
        longest = jnp.maximum(longest, totals[member + 1] - aligned(totals[member]))
    choice = jnp.int32(0)
    for size in more_sizes(more)[:-1]:
        choice = choice + jnp.where(longest > first + size, 1, 0)
    choice_ref[0] = choice
    before = chosen(totals[:-1], index)
    places = token_places(lengths_ref, index, before, block_ref.shape[0])
    pick = picking(places, 0, first + more)
    wanted_ref[...] = jnp.dot(pick, targets_ref[...], preferred_element_type=jnp.float32)

    def store(here, rows):
        rows_ref[pl.ds(aligned(before), first + more), here] = rows

    block.picked(pick, store, True)


def keys_kernel(members, scale, lengths_ref, wanted_ref, low_ref, rows_ref, *refs):
    held, sums = refs[: 2 * members - 2], refs[2 * members - 2 : 3 * members - 2]
    all_ref, total_ref, more_ref, sems = refs[3 * members - 2 :]
    del rows_ref
    index = lax.axis_index("fsdp")
    share = sums[0].shape[0]
    totals = live_before(lengths_ref, members)
    for i in range(1, members):
        member = lax.rem(index + members - i, members)
        start = aligned(chosen(totals[:-1], member))
        used = chosen(totals[1:], member) - start
        first_ref, further_ref = held[2 * i - 2 : 2 * i]
        first = first_ref.shape[0]
        all_ref[pl.ds(start, first)] += first_ref[...]

        @pl.when(used > first)
        def _(i=i, start=start, used=used, further_ref=further_ref, first=first):
            copy = pltpu.make_async_copy(further_ref, more_ref, sems.at[i - 1])
            copy.start()
            copy.wait()
            for k in range(0, more_ref.shape[0], ALIGN):

                @pl.when(used > first + k)
                def _(k=k):
                    all_ref[pl.ds(start + first + k, ALIGN)] += more_ref[k : k + ALIGN]

    @pl.loop(0, members)
    def _(j):
        rows = pl.ds(pl.multiple_of(j * share, ALIGN), share)
        total_ref[rows] = (
            jnp.dot(all_ref[rows], low_ref[...], preferred_element_type=jnp.float32) * scale
        )

    own_start = aligned(chosen(totals[:-1], index))
    total_ref[pl.ds(own_start, wanted_ref.shape[0])] -= wanted_ref[...]
    for i in range(members):
        owner = lax.rem(index + i, members)
        block = total_ref[pl.ds(pl.multiple_of(owner * share, ALIGN), share)]
        sums[i][...] = block.astype(sums[i].dtype)


def turn_kernel(all_ref, turned_ref):
    for start in range(0, turned_ref.shape[1], 128):
        turned_ref[:, start : start + 128] = all_ref[start : start + 128, :].T


def gradient_kernel(members, turned_ref, *refs):
    residuals, (gradient_ref, low_ref, squares_ref, all_ref) = refs[:members], refs[members:]
    index = lax.axis_index("fsdp")
    share = residuals[0].shape[0]
    for i in range(members):
        owner = lax.rem(index + members - i, members)
        all_ref[pl.ds(pl.multiple_of(owner * share, ALIGN), share)] = residuals[i][...]
    squares_ref[...] = jnp.zeros_like(squares_ref)
    height = min(256, turned_ref.shape[0])

    @pl.loop(0, turned_ref.shape[0] // height)
    def _(j):
        rows = pl.ds(pl.multiple_of(j * height, height), height)
        gradient = jnp.dot(turned_ref[rows], all_ref[...], preferred_element_type=jnp.float32)
        gradient_ref[rows] = gradient
        low_ref[rows] = gradient.astype(low_ref.dtype)
        squares = jnp.sum((gradient * gradient).reshape(-1, 8, gradient.shape[1]), axis=0)
        lanes = squares.shape[1] // 128
        squares_ref[...] += sum(squares[:, 128 * k : 128 * (k + 1)] for k in range(lanes))


def average_kernel(entries, own_ref, other_ref, halves_ref, gradient_ref, partner_ref, out_ref, done_ref, sems):
    half = 0.5 * learning_rate
    own = half * lax.rsqrt(jnp.sum(own_ref[...], keepdims=True) / entries + epsilon)
    other = half * lax.rsqrt(jnp.sum(other_ref[...], keepdims=True) / entries + epsilon)
    pieces = sems.shape[0]
    height = done_ref.shape[0] // pieces
    copies = []
    for j in range(pieces):
        rows = pl.ds(j * height, height)
        done_ref[rows] = (
            halves_ref[rows]
            - gradient_ref[rows] * own
            - partner_ref[rows].astype(jnp.float32) * other
        )
        copies.append(pltpu.make_async_copy(done_ref.at[rows], out_ref.at[rows], sems.at[j]))
        copies[-1].start()
    for copy in copies:
        copy.wait()


def more_sizes(more):
    return [0] + [size for size in (16, 32, 48, 64, 80, 96, 128, 160) if size < more] + [more]


def place_kernel(size, *refs):
    count = (len(refs) - 1) // 2
    sems = refs[-1]
    copies = [
        pltpu.make_async_copy(refs[i], refs[count + i].at[pl.ds(0, size)], sems.at[i])
        for i in range(count)
    ]
    for copy in copies:
        copy.start()
    for copy in copies:
        copy.wait()


def more_rows(size, blocks):
    members = lax.axis_size("fsdp")
    if size == blocks[0].shape[0]:
        return [turned(block, i + 1) for i, block in enumerate(blocks)]
    if size == 0:
        return list(blocks)
    anywhere = pl.BlockSpec(memory_space=pl.ANY)
    placed = pl.pallas_call(
        functools.partial(place_kernel, size),
        in_specs=[anywhere] * (members - 1),
        out_specs=[anywhere] * (members - 1),
        out_shape=[jax.ShapeDtypeStruct(block.shape, block.dtype) for block in blocks],
        scratch_shapes=[pltpu.SemaphoreType.DMA((members - 1,))],
    )(*[turned(block[:size], i + 1) for i, block in enumerate(blocks)])
    return list(placed)


def local(activations, targets, weights, lengths):
    features = activations[0]
    wanted = targets[0]
    master = weights[0]
    tokens_here = features.shape[0]
    local_rows, columns = master.shape
    members = lax.axis_size("fsdp")
    distance_bit = STEP % (lax.axis_size("replica").bit_length() - 1)
    share = tokens_here // 2
    first = -(-(share + 32) // MORE) * MORE
    more = -(-(tokens_here + ALIGN - first) // MORE) * MORE
    scale = features.shape[1] ** (-0.5)
    places = members * share + first + more

    vmem = pl.BlockSpec(memory_space=pltpu.VMEM)
    anywhere = pl.BlockSpec(memory_space=pl.ANY)
    smem = pl.BlockSpec(memory_space=pltpu.SMEM)
    params = pltpu.CompilerParams(vmem_limit_bytes=40 * 2**20)

    def array(rows, width, dtype):
        return jax.ShapeDtypeStruct((rows, width), dtype)

    def cost(flops, moved):
        return pl.CostEstimate(flops=flops, bytes_accessed=moved, transcendentals=0)

    first_shape = array(first, local_rows, jnp.bfloat16)
    more_shape = array(more, local_rows, jnp.bfloat16)
    block_scratch = [
        pltpu.VMEM((tokens_here, local_rows), jnp.bfloat16),
        pltpu.SemaphoreType.DMA((max(1, local_rows // 256),)),
    ]

    sent_more, held_first = [], []
    for i in range(1, members):
        sent, rest = pl.pallas_call(
            functools.partial(sent_kernel, members, i),
            in_specs=[smem, anywhere],
            out_specs=[vmem] * 2,
            out_shape=[first_shape, more_shape],
            scratch_shapes=block_scratch,
            compiler_params=pltpu.CompilerParams(vmem_limit_bytes=56 * 2**20),
            cost_estimate=cost(
                2 * first * tokens_here * local_rows, 2 * (tokens_here + first) * local_rows
            ),
        )(lengths, features)
        held_first.append(turned(sent, i))
        sent_more.append(rest)

    partner_master = swapped(master, "replica", distance_bit)
    own_rows, own_wanted, low, halves, choice = pl.pallas_call(
        functools.partial(own_kernel, members, first, more),
        in_specs=[smem, anywhere, vmem, vmem, vmem],
        out_specs=[vmem] * 4 + [smem],
        out_shape=[
            array(places, local_rows, jnp.bfloat16),
            array(first + more, columns, jnp.float32),
            array(local_rows, columns, jnp.bfloat16),
            array(local_rows, columns, jnp.float32),
            jax.ShapeDtypeStruct((1,), jnp.int32),
        ],
        scratch_shapes=block_scratch,
        compiler_params=params,
        cost_estimate=cost(
            2 * (first + more) * tokens_here * (local_rows + columns), 20 * local_rows * columns
        ),
    )(lengths, features, wanted, master, partner_master)

    choice, held_first[0] = lax.optimization_barrier((choice, held_first[0]))
    held_more = lax.switch(
        choice[0], [functools.partial(more_rows, size) for size in more_sizes(more)], sent_more
    )
    held = [array for pair in zip(held_first, held_more) for array in pair]

    *sums, rows = pl.pallas_call(
        functools.partial(keys_kernel, members, scale),
        in_specs=[smem, vmem, vmem, vmem] + [vmem, anywhere] * (members - 1),
        out_specs=[vmem] * (members + 1),
        out_shape=[
            array(share, columns, jnp.bfloat16 if i else jnp.float32) for i in range(members)
        ]
        + [array(places, local_rows, jnp.bfloat16)],
        input_output_aliases={3: members},
        scratch_shapes=[
            pltpu.VMEM((places, columns), jnp.float32),
            pltpu.VMEM((more, local_rows), jnp.bfloat16),
            pltpu.SemaphoreType.DMA((members - 1,)),
        ],
        compiler_params=params,
        cost_estimate=cost(
            2 * members * share * local_rows * columns, 4 * places * (local_rows + columns)
        ),
    )(lengths, own_wanted, low, own_rows, *held)

    turned_rows = pl.pallas_call(
        turn_kernel,
        in_specs=[vmem],
        out_specs=vmem,
        out_shape=array(local_rows, members * share, jnp.bfloat16),
        compiler_params=params,
        cost_estimate=cost(0, 4 * members * share * local_rows),
    )(rows)

    residual = sums[0]
    for i in range(1, members):
        residual = residual + turned(sums[i], i).astype(jnp.float32)
    residual = residual.astype(jnp.bfloat16)
    residuals = [residual] + [turned(residual, i) for i in range(1, members)]

    gradient, low_gradient, squares = pl.pallas_call(
        functools.partial(gradient_kernel, members),
        in_specs=[vmem] + [vmem] * members,
        out_specs=[vmem] * 3,
        out_shape=[
            array(local_rows, columns, jnp.float32),
            array(local_rows, columns, jnp.bfloat16),
            array(8, 128, jnp.float32),
        ],
        scratch_shapes=[pltpu.VMEM((members * share, columns), jnp.bfloat16)],
        compiler_params=params,
        cost_estimate=cost(
            2 * members * share * local_rows * columns, 8 * local_rows * columns
        ),
    )(turned_rows, *residuals)

    partner_gradient = swapped(low_gradient, "replica", distance_bit)
    total = squares
    for bit in range(members.bit_length() - 1):
        total = total + swapped(total, "fsdp", bit)
    partner_total = swapped(total, "replica", distance_bit)

    averaged = pl.pallas_call(
        functools.partial(average_kernel, members * local_rows * columns),
        in_specs=[vmem] * 5,
        out_specs=anywhere,
        out_shape=array(local_rows, columns, jnp.float32),
        scratch_shapes=[
            pltpu.VMEM((local_rows, columns), jnp.float32),
            pltpu.SemaphoreType.DMA((4,)),
        ],
        compiler_params=params,
    )(total, partner_total, halves, gradient, partner_gradient)
    return averaged[None]


def solution(mesh):
    return jax.shard_map(
        local,
        mesh=mesh,
        in_specs=(
            P("replica", "fsdp", None),
            P("replica", "fsdp", None),
            P("replica", "fsdp", None),
            P("replica", None),
        ),
        out_specs=P("replica", "fsdp", None),
        check_vma=False,
    )
```

```python
import functools

import jax
import jax.numpy as jnp
from jax import lax
from jax.experimental import pallas as pl
from jax.experimental.pallas import tpu as pltpu
from jax.sharding import PartitionSpec as P

SLOT = 64
STEP = 3
ALIGN = 16

learning_rate = 0.1
epsilon = 1e-06


def swapped(value, axis, bit):
    mask = 2**bit
    pairs = [(source, source ^ mask) for source in range(lax.axis_size(axis))]
    return lax.ppermute(value, axis, pairs)


def turned(value, distance):
    members = lax.axis_size("fsdp")
    ring = [(source, (source + distance) % members) for source in range(members)]
    return lax.ppermute(value, "fsdp", ring)


def live_before(lengths_ref, members):
    sequences = lengths_ref.shape[1] // members
    totals = [jnp.int32(0)]
    for member in range(members):
        total = totals[-1]
        for q in range(sequences):
            total = total + lengths_ref[0, member * sequences + q]
        totals.append(total)
    return totals


def chosen(values, index):
    value = values[0]
    for i in range(1, len(values)):
        value = jnp.where(index == i, values[i], value)
    return value


def aligned(place):
    return pl.multiple_of(place // ALIGN * ALIGN, ALIGN)


def token_places(lengths_ref, member, before, tokens):
    sequences = tokens // SLOT
    place = before % ALIGN
    slot = lax.broadcasted_iota(jnp.int32, (1, tokens), 1)
    places = jnp.full((1, tokens), -1, jnp.int32)
    for s in range(sequences):
        length = lengths_ref[0, member * sequences + s]
        position = slot - s * SLOT
        places = jnp.where((position >= 0) & (position < length), position + place, places)
        place = place + length
    return places


def picking(places, start, rows):
    row = lax.broadcasted_iota(jnp.int32, (rows, places.shape[1]), 0) + start
    return jnp.where(row == places, 1.0, 0.0).astype(jnp.bfloat16)


class Block:
    def __init__(self, features_ref, member, block_ref, sems):
        self.block_ref, self.width = block_ref, block_ref.shape[1] // sems.shape[0]
        start = member * block_ref.shape[1]
        self.copies = []
        for j in range(sems.shape[0]):
            there = pl.ds(pl.multiple_of(start + j * self.width, 128), self.width)
            here = pl.ds(j * self.width, self.width)
            copy = pltpu.make_async_copy(
                features_ref.at[:, there], block_ref.at[:, here], sems.at[j]
            )
            copy.start()
            self.copies.append(copy)

    def picked(self, pick, store, wait):
        for j, copy in enumerate(self.copies):
            if wait:
                copy.wait()
            here = slice(j * self.width, (j + 1) * self.width)
            rows = jnp.dot(pick, self.block_ref[:, here], preferred_element_type=jnp.float32)
            store(here, rows.astype(jnp.bfloat16))


def sent_kernel(members, lengths_ref, features_ref, *refs):
    parts, (block_ref, sems) = refs[:-2], refs[-2:]
    index = lax.axis_index("fsdp")
    blocks = [
        Block(
            features_ref, lax.rem(index + i, members), block_ref.at[i - 1], sems.at[i - 1]
        )
        for i in range(1, members)
    ]
    totals = live_before(lengths_ref, members)
    before, end = chosen(totals[:-1], index), chosen(totals[1:], index)
    places = token_places(lengths_ref, index, before, block_ref.shape[1])
    used = end - aligned(before)

    def fill(refs, start, wait):
        pick = picking(places, start, refs[0].shape[0])
        for block, ref in zip(blocks, refs):

            def store(here, rows, ref=ref):
                ref[:, here] = rows

            block.picked(pick, store, wait)

    start = 0
    for j in range(3):
        group = parts[j * (members - 1) : (j + 1) * (members - 1)]
        if j:
            pl.when(used > start)(functools.partial(fill, group, start, False))
        else:
            fill(group, start, True)
        start = start + group[0].shape[0]


def own_kernel(
    members,
    first,
    sizes,
    lengths_ref,
    features_ref,
    targets_ref,
    master_ref,
    partner_ref,
    rows_ref,
    wanted_ref,
    low_ref,
    halves_ref,
    choice_ref,
    block_ref,
    sems,
):
    index = lax.axis_index("fsdp")
    block = Block(features_ref, index, block_ref, sems)
    rows_ref[...] = jnp.zeros_like(rows_ref)
    low_ref[...] = master_ref[...].astype(jnp.bfloat16)
    halves_ref[...] = 0.5 * (master_ref[...] + partner_ref[...])
    totals = live_before(lengths_ref, members)
    longest = jnp.int32(0)
    for member in range(members):
        longest = jnp.maximum(longest, totals[member + 1] - aligned(totals[member]))
    choice = jnp.int32(0)
    for size in sizes[:-1]:
        choice = choice + jnp.where(longest > first + size, 1, 0)
    choice_ref[0] = choice
    choice_ref[1] = jnp.where(longest > first + sizes[-1], 1, 0)
    before = chosen(totals[:-1], index)
    places = token_places(lengths_ref, index, before, block_ref.shape[0])
    pick = picking(places, 0, wanted_ref.shape[0])
    wanted_ref[...] = jnp.dot(pick, targets_ref[...], preferred_element_type=jnp.float32)

    def store(here, rows):
        rows_ref[pl.ds(aligned(before), wanted_ref.shape[0]), here] = rows

    block.picked(pick, store, True)


def keys_kernel(members, scale, lengths_ref, wanted_ref, low_ref, rows_ref, *refs):
    others = members - 1
    held, sums = refs[: 3 * others], refs[3 * others : 3 * others + members]
    all_ref, total_ref, first_ref, *rest_refs, first_sems, rest_sems = refs[3 * others + members :]
    del rows_ref
    index = lax.axis_index("fsdp")
    share = sums[0].shape[0]
    totals = live_before(lengths_ref, members)
    copies = [
        pltpu.make_async_copy(held[3 * i], first_ref.at[i], first_sems.at[i]) for i in range(others)
    ]
    for copy in copies:
        copy.start()
    for i in range(others):
        member = lax.rem(index + members - 1 - i, members)
        begin = aligned(chosen(totals[:-1], member))
        used = chosen(totals[1:], member) - begin
        copies[i].wait()
        start = first_ref.shape[1]
        all_ref[pl.ds(begin, start)] += first_ref[i]
        for j in range(2):
            part_ref = rest_refs[j]

            @pl.when(used > start)
            def _(i=i, j=j, begin=begin, used=used, start=start, part_ref=part_ref):
                copy = pltpu.make_async_copy(held[3 * i + 1 + j], part_ref, rest_sems.at[2 * i + j])
                copy.start()
                copy.wait()
                for k in range(0, part_ref.shape[0], ALIGN):

                    @pl.when(used > start + k)
                    def _(k=k):
                        all_ref[pl.ds(begin + start + k, ALIGN)] += part_ref[k : k + ALIGN]

            start = start + part_ref.shape[0]

    @pl.loop(0, members)
    def _(j):
        rows = pl.ds(pl.multiple_of(j * share, ALIGN), share)
        total_ref[rows] = (
            jnp.dot(all_ref[rows], low_ref[...], preferred_element_type=jnp.float32) * scale
        )

    own_start = aligned(chosen(totals[:-1], index))
    total_ref[pl.ds(own_start, wanted_ref.shape[0])] -= wanted_ref[...]
    for i in range(members):
        owner = lax.rem(index + i, members)
        block = total_ref[pl.ds(pl.multiple_of(owner * share, ALIGN), share)]
        sums[i][...] = block.astype(sums[i].dtype)


def turn_kernel(all_ref, turned_ref):
    for start in range(0, turned_ref.shape[1], 128):
        turned_ref[:, start : start + 128] = all_ref[start : start + 128, :].T


def gradient_kernel(members, turned_ref, *refs):
    residuals, (gradient_ref, low_ref, squares_ref, all_ref) = refs[:members], refs[members:]
    index = lax.axis_index("fsdp")
    share = residuals[0].shape[0]
    for i in range(members):
        owner = lax.rem(index + members - i, members)
        all_ref[pl.ds(pl.multiple_of(owner * share, ALIGN), share)] = residuals[i][...]
    squares_ref[...] = jnp.zeros_like(squares_ref)
    height = min(256, turned_ref.shape[0])

    @pl.loop(0, turned_ref.shape[0] // height)
    def _(j):
        rows = pl.ds(pl.multiple_of(j * height, height), height)
        gradient = jnp.dot(turned_ref[rows], all_ref[...], preferred_element_type=jnp.float32)
        gradient_ref[rows] = gradient
        low_ref[rows] = gradient.astype(low_ref.dtype)
        squares = jnp.sum((gradient * gradient).reshape(-1, 8, gradient.shape[1]), axis=0)
        lanes = squares.shape[1] // 128
        squares_ref[...] += sum(squares[:, 128 * k : 128 * (k + 1)] for k in range(lanes))


def average_kernel(entries, own_ref, other_ref, halves_ref, gradient_ref, partner_ref, out_ref, done_ref, sems):
    half = 0.5 * learning_rate
    own = half * lax.rsqrt(jnp.sum(own_ref[...], keepdims=True) / entries + epsilon)
    other = half * lax.rsqrt(jnp.sum(other_ref[...], keepdims=True) / entries + epsilon)
    pieces = sems.shape[0]
    height = done_ref.shape[0] // pieces
    copies = []
    for j in range(pieces):
        rows = pl.ds(j * height, height)
        done_ref[rows] = (
            halves_ref[rows]
            - gradient_ref[rows] * own
            - partner_ref[rows].astype(jnp.float32) * other
        )
        copies.append(pltpu.make_async_copy(done_ref.at[rows], out_ref.at[rows], sems.at[j]))
        copies[-1].start()
    for copy in copies:
        copy.wait()


def more_rows(size, blocks):
    if size == 0:
        return list(blocks)
    moved = [turned(block[:size], i + 1) for i, block in enumerate(blocks)]
    return [jnp.pad(m, ((0, b.shape[0] - size), (0, 0))) for m, b in zip(moved, blocks)]


def local(activations, targets, weights, lengths):
    features = activations[0]
    wanted = targets[0]
    master = weights[0]
    tokens_here = features.shape[0]
    local_rows, columns = master.shape
    members = lax.axis_size("fsdp")
    distance_bit = STEP % (lax.axis_size("replica").bit_length() - 1)
    share = tokens_here // 2
    first = -(-(share + 32) // ALIGN) * ALIGN
    sizes = list(range(0, 97, ALIGN))
    parts = [first, sizes[-1], -(-(tokens_here + ALIGN - first - sizes[-1]) // ALIGN) * ALIGN]
    most = sum(parts)
    scale = features.shape[1] ** (-0.5)
    places = members * share + most

    vmem = pl.BlockSpec(memory_space=pltpu.VMEM)
    anywhere = pl.BlockSpec(memory_space=pl.ANY)
    smem = pl.BlockSpec(memory_space=pltpu.SMEM)
    params = pltpu.CompilerParams(vmem_limit_bytes=40 * 2**20)

    def array(rows, width, dtype):
        return jax.ShapeDtypeStruct((rows, width), dtype)

    def cost(flops, moved):
        return pl.CostEstimate(flops=flops, bytes_accessed=moved, transcendentals=0)

    def block_scratch(*count):
        return [
            pltpu.VMEM((*count, tokens_here, local_rows), jnp.bfloat16),
            pltpu.SemaphoreType.DMA((*count, max(1, local_rows // 256))),
        ]

    sent = pl.pallas_call(
        functools.partial(sent_kernel, members),
        in_specs=[smem, anywhere],
        out_specs=[vmem] * (3 * members - 3),
        out_shape=[
            array(rows, local_rows, jnp.bfloat16) for rows in parts for _ in range(members - 1)
        ],
        scratch_shapes=block_scratch(members - 1),
        compiler_params=pltpu.CompilerParams(vmem_limit_bytes=56 * 2**20),
    )(lengths, features)
    sent = [list(sent[j * (members - 1) : (j + 1) * (members - 1)]) for j in range(3)]
    held_first = [None] + [turned(sent[0][i - 1], i) for i in range(2, members)]

    partner_master = swapped(master, "replica", distance_bit)
    own_rows, own_wanted, low, halves, choice = pl.pallas_call(
        functools.partial(own_kernel, members, first, sizes),
        in_specs=[smem, anywhere, vmem, vmem, vmem],
        out_specs=[vmem] * 4 + [smem],
        out_shape=[
            array(places, local_rows, jnp.bfloat16),
            array(most, columns, jnp.float32),
            array(local_rows, columns, jnp.bfloat16),
            array(local_rows, columns, jnp.float32),
            jax.ShapeDtypeStruct((2,), jnp.int32),
        ],
        scratch_shapes=block_scratch(),
        compiler_params=params,
        cost_estimate=cost(
            2 * most * tokens_here * (local_rows + columns), 20 * local_rows * columns
        ),
    )(lengths, features, wanted, master, partner_master)

    held_more = lax.switch(
        choice[0], [functools.partial(more_rows, size) for size in sizes], sent[1]
    )
    held_rest = lax.cond(
        choice[1] > 0, functools.partial(more_rows, parts[2]), functools.partial(more_rows, 0), sent[2]
    )
    last, held_more, held_rest = lax.optimization_barrier((sent[0][0], held_more, held_rest))
    held_first[0] = turned(last, 1)
    held = [array for group in zip(held_first, held_more, held_rest) for array in group]

    *sums, rows = pl.pallas_call(
        functools.partial(keys_kernel, members, scale),
        in_specs=[smem, vmem, vmem, vmem] + [anywhere] * (3 * members - 3),
        out_specs=[vmem] * (members + 1),
        out_shape=[
            array(share, columns, jnp.bfloat16 if i else jnp.float32) for i in range(members)
        ]
        + [array(places, local_rows, jnp.bfloat16)],
        input_output_aliases={3: members},
        scratch_shapes=[
            pltpu.VMEM((places, columns), jnp.float32),
            pltpu.VMEM((members - 1, first, local_rows), jnp.bfloat16),
            pltpu.VMEM((parts[1], local_rows), jnp.bfloat16),
            pltpu.VMEM((parts[2], local_rows), jnp.bfloat16),
            pltpu.SemaphoreType.DMA((members - 1,)),
            pltpu.SemaphoreType.DMA((2 * members - 2,)),
        ],
        compiler_params=params,
        cost_estimate=cost(
            2 * members * share * local_rows * columns, 4 * places * (local_rows + columns)
        ),
    )(lengths, own_wanted, low, own_rows, *held)

    turned_rows = pl.pallas_call(
        turn_kernel,
        in_specs=[vmem],
        out_specs=vmem,
        out_shape=array(local_rows, members * share, jnp.bfloat16),
        compiler_params=params,
        cost_estimate=cost(0, 4 * members * share * local_rows),
    )(rows)

    residual = sums[0]
    for i in range(1, members):
        residual = residual + turned(sums[i], i).astype(jnp.float32)
    residual = residual.astype(jnp.bfloat16)
    residuals = [residual] + [turned(residual, i) for i in range(1, members)]

    gradient, low_gradient, squares = pl.pallas_call(
        functools.partial(gradient_kernel, members),
        in_specs=[vmem] + [vmem] * members,
        out_specs=[vmem] * 3,
        out_shape=[
            array(local_rows, columns, jnp.float32),
            array(local_rows, columns, jnp.bfloat16),
            array(8, 128, jnp.float32),
        ],
        scratch_shapes=[pltpu.VMEM((members * share, columns), jnp.bfloat16)],
        compiler_params=params,
        cost_estimate=cost(
            2 * members * share * local_rows * columns, 8 * local_rows * columns
        ),
    )(turned_rows, *residuals)

    partner_gradient = swapped(low_gradient, "replica", distance_bit)
    total = squares
    for i in range(1, members):
        total = total + turned(squares, i)
    partner_total = swapped(total, "replica", distance_bit)

    averaged = pl.pallas_call(
        functools.partial(average_kernel, members * local_rows * columns),
        in_specs=[vmem] * 5,
        out_specs=anywhere,
        out_shape=array(local_rows, columns, jnp.float32),
        scratch_shapes=[
            pltpu.VMEM((local_rows, columns), jnp.float32),
            pltpu.SemaphoreType.DMA((4,)),
        ],
        compiler_params=params,
    )(total, partner_total, halves, gradient, partner_gradient)
    return averaged[None]


def solution(mesh):
    return jax.shard_map(
        local,
        mesh=mesh,
        in_specs=(
            P("replica", "fsdp", None),
            P("replica", "fsdp", None),
            P("replica", "fsdp", None),
            P("replica", None),
        ),
        out_specs=P("replica", "fsdp", None),
        check_vma=False,
    )
```

```python
import functools

import jax
import jax.numpy as jnp
from jax import lax
from jax.experimental import pallas as pl
from jax.experimental.pallas import tpu as pltpu
from jax.sharding import PartitionSpec as P

SLOT = 64
STEP = 3
ALIGN = 16
HALVES = 2

learning_rate = 0.1
epsilon = 1e-06


def swapped(value, axis, bit):
    mask = 2**bit
    pairs = [(source, source ^ mask) for source in range(lax.axis_size(axis))]
    return lax.ppermute(value, axis, pairs)


def turned(value, distance):
    members = lax.axis_size("fsdp")
    ring = [(source, (source + distance) % members) for source in range(members)]
    return lax.ppermute(value, "fsdp", ring)


def live_before(lengths_ref, members):
    sequences = lengths_ref.shape[1] // members
    totals = [jnp.int32(0)]
    for member in range(members):
        total = totals[-1]
        for q in range(sequences):
            total = total + lengths_ref[0, member * sequences + q]
        totals.append(total)
    return totals


def chosen(values, index):
    value = values[0]
    for i in range(1, len(values)):
        value = jnp.where(index == i, values[i], value)
    return value


def aligned(place):
    return pl.multiple_of(place // ALIGN * ALIGN, ALIGN)


def token_places(lengths_ref, member, before, tokens):
    sequences = tokens // SLOT
    place = before % ALIGN
    slot = lax.broadcasted_iota(jnp.int32, (1, tokens), 1)
    places = jnp.full((1, tokens), -1, jnp.int32)
    for s in range(sequences):
        length = lengths_ref[0, member * sequences + s]
        position = slot - s * SLOT
        places = jnp.where((position >= 0) & (position < length), position + place, places)
        place = place + length
    return places


def picking(places, start, rows):
    row = lax.broadcasted_iota(jnp.int32, (rows, places.shape[1]), 0) + start
    return jnp.where(row == places, 1.0, 0.0).astype(jnp.bfloat16)


class Block:
    def __init__(self, features_ref, member, block_ref, sems):
        self.block_ref, self.width = block_ref, block_ref.shape[1] // sems.shape[0]
        start = member * block_ref.shape[1]
        self.copies = []
        for j in range(sems.shape[0]):
            there = pl.ds(pl.multiple_of(start + j * self.width, 128), self.width)
            here = pl.ds(j * self.width, self.width)
            copy = pltpu.make_async_copy(
                features_ref.at[:, there], block_ref.at[:, here], sems.at[j]
            )
            copy.start()
            self.copies.append(copy)

    def picked(self, pick, store, wait):
        for j, copy in enumerate(self.copies):
            if wait:
                copy.wait()
            here = slice(j * self.width, (j + 1) * self.width)
            rows = jnp.dot(pick, self.block_ref[:, here], preferred_element_type=jnp.float32)
            store(here, rows.astype(jnp.bfloat16))


def sent_kernel(members, offsets, sizes, lengths_ref, features_ref, *refs):
    parts, (choice_ref, block_ref, sems) = refs[:-3], refs[-3:]
    count = len(offsets)
    index = lax.axis_index("fsdp")
    blocks = [
        Block(features_ref, lax.rem(index + i, members), block_ref.at[n], sems.at[n])
        for n, i in enumerate(offsets)
    ]
    totals = live_before(lengths_ref, members)
    longest = jnp.int32(0)
    for member in range(members):
        longest = jnp.maximum(longest, totals[member + 1] - aligned(totals[member]))
    first = parts[0].shape[0]
    choice = jnp.int32(0)
    for size in sizes[:-1]:
        choice = choice + jnp.where(longest > first + size, 1, 0)
    choice_ref[0] = choice
    choice_ref[1] = jnp.where(longest > first + sizes[-1], 1, 0)
    before, end = chosen(totals[:-1], index), chosen(totals[1:], index)
    places = token_places(lengths_ref, index, before, block_ref.shape[1])
    used = end - aligned(before)

    def fill(refs, start, wait):
        pick = picking(places, start, refs[0].shape[0])
        for block, ref in zip(blocks, refs):

            def store(here, rows, ref=ref):
                ref[:, here] = rows

            block.picked(pick, store, wait)

    start = 0
    for j in range(3):
        group = parts[j * count : (j + 1) * count]
        if j:
            pl.when(used > start)(functools.partial(fill, group, start, False))
        else:
            fill(group, start, True)
        start = start + group[0].shape[0]


def own_kernel(
    members,
    lengths_ref,
    features_ref,
    targets_ref,
    master_ref,
    partner_ref,
    rows_ref,
    wanted_ref,
    low_ref,
    halves_ref,
    block_ref,
    sems,
):
    index = lax.axis_index("fsdp")
    block = Block(features_ref, index, block_ref, sems)
    rows_ref[...] = jnp.zeros_like(rows_ref)
    low_ref[...] = master_ref[...].astype(jnp.bfloat16)
    halves_ref[...] = 0.5 * (master_ref[...] + partner_ref[...])
    totals = live_before(lengths_ref, members)
    before = chosen(totals[:-1], index)
    places = token_places(lengths_ref, index, before, block_ref.shape[0])
    pick = picking(places, 0, wanted_ref.shape[0])
    wanted_ref[...] = jnp.dot(pick, targets_ref[...], preferred_element_type=jnp.float32)

    def store(here, rows):
        rows_ref[pl.ds(aligned(before), wanted_ref.shape[0]), here] = rows

    block.picked(pick, store, True)


def half_keys(members, half, scale, lengths_ref, wanted_ref, low_ref, rows_ref, sums, total_ref):
    index = lax.axis_index("fsdp")
    share, width = sums[0].shape
    here = slice(half * width, (half + 1) * width)

    @pl.loop(0, members)
    def _(j):
        rows = pl.ds(pl.multiple_of(j * share, ALIGN), share)
        total_ref[rows] = (
            jnp.dot(rows_ref[rows], low_ref[:, here], preferred_element_type=jnp.float32) * scale
        )

    own_start = aligned(chosen(live_before(lengths_ref, members)[:-1], index))
    total_ref[pl.ds(own_start, wanted_ref.shape[0])] -= wanted_ref[:, here]
    for i in range(members):
        owner = lax.rem(index + i, members)
        block = total_ref[pl.ds(pl.multiple_of(owner * share, ALIGN), share)]
        sums[i][...] = block.astype(sums[i].dtype)


def keys_kernel(members, offsets, scale, lengths_ref, wanted_ref, low_ref, rows_ref, *refs):
    others = members - 1
    held, sums = refs[: 3 * others], refs[3 * others : 3 * others + HALVES * members]
    all_ref, total_ref, first_ref, *rest_refs, first_sems, rest_sems = refs[
        3 * others + HALVES * members :
    ]
    del rows_ref
    index = lax.axis_index("fsdp")
    share = sums[0].shape[0]
    totals = live_before(lengths_ref, members)
    copies = [
        pltpu.make_async_copy(held[3 * i], first_ref.at[i], first_sems.at[i]) for i in range(others)
    ]
    for copy in copies:
        copy.start()
    for i in range(others):
        member = lax.rem(index + members - offsets[i], members)
        begin = aligned(chosen(totals[:-1], member))
        used = chosen(totals[1:], member) - begin
        copies[i].wait()
        start = first_ref.shape[1]
        all_ref[pl.ds(begin, start)] += first_ref[i]
        for j in range(2):
            part_ref = rest_refs[j]

            @pl.when(used > start)
            def _(i=i, j=j, begin=begin, used=used, start=start, part_ref=part_ref):
                copy = pltpu.make_async_copy(held[3 * i + 1 + j], part_ref, rest_sems.at[2 * i + j])
                copy.start()
                copy.wait()
                for k in range(0, part_ref.shape[0], ALIGN):

                    @pl.when(used > start + k)
                    def _(k=k):
                        all_ref[pl.ds(begin + start + k, ALIGN)] += part_ref[k : k + ALIGN]

            start = start + part_ref.shape[0]

    for half in range(HALVES):
        here = sums[half * members : (half + 1) * members]
        half_keys(members, half, scale, lengths_ref, wanted_ref, low_ref, all_ref, here, total_ref)


def turn_kernel(all_ref, turned_ref):
    for start in range(0, turned_ref.shape[1], 128):
        turned_ref[:, start : start + 128] = all_ref[start : start + 128, :].T


def gradient_kernel(members, turned_ref, *refs):
    residuals, (gradient_ref, low_ref, squares_ref, all_ref) = refs[:members], refs[members:]
    index = lax.axis_index("fsdp")
    share = residuals[0].shape[0]
    for i in range(members):
        owner = lax.rem(index + members - i, members)
        all_ref[pl.ds(pl.multiple_of(owner * share, ALIGN), share)] = residuals[i][...]
    squares_ref[...] = jnp.zeros_like(squares_ref)
    height = min(256, turned_ref.shape[0])

    @pl.loop(0, turned_ref.shape[0] // height)
    def _(j):
        rows = pl.ds(pl.multiple_of(j * height, height), height)
        gradient = jnp.dot(turned_ref[rows], all_ref[...], preferred_element_type=jnp.float32)
        gradient_ref[rows] = gradient
        low_ref[rows] = gradient.astype(low_ref.dtype)
        squares = jnp.sum((gradient * gradient).reshape(-1, 8, gradient.shape[1]), axis=0)
        lanes = squares.shape[1] // 128
        squares_ref[...] += sum(squares[:, 128 * k : 128 * (k + 1)] for k in range(lanes))


def average_kernel(entries, own_ref, other_ref, halves_ref, *refs):
    gradients, partners, (out_ref, done_ref, sems) = refs[:HALVES], refs[HALVES:-3], refs[-3:]
    rate = 0.5 * learning_rate
    own = rate * lax.rsqrt(jnp.sum(own_ref[...], keepdims=True) / entries + epsilon)
    other = rate * lax.rsqrt(jnp.sum(other_ref[...], keepdims=True) / entries + epsilon)
    pieces = sems.shape[0]
    height = done_ref.shape[0] // pieces
    width = done_ref.shape[1] // HALVES
    copies = []
    for j in range(pieces):
        rows = pl.ds(j * height, height)
        for half in range(HALVES):
            here = slice(half * width, (half + 1) * width)
            done_ref[rows, here] = (
                halves_ref[rows, here]
                - gradients[half][rows] * own
                - partners[half][rows].astype(jnp.float32) * other
            )
        copies.append(pltpu.make_async_copy(done_ref.at[rows], out_ref.at[rows], sems.at[j]))
        copies[-1].start()
    for copy in copies:
        copy.wait()


def more_rows(size, offsets, blocks):
    if size == 0:
        return list(blocks)
    moved = [turned(block[:size], i) for i, block in zip(offsets, blocks)]
    return [jnp.pad(m, ((0, b.shape[0] - size), (0, 0))) for m, b in zip(moved, blocks)]


def local(activations, targets, weights, lengths):
    features = activations[0]
    wanted = targets[0]
    master = weights[0]
    tokens_here = features.shape[0]
    local_rows, columns = master.shape
    members = lax.axis_size("fsdp")
    distance_bit = STEP % (lax.axis_size("replica").bit_length() - 1)
    share = tokens_here // 2
    first = -(-(share + 32) // ALIGN) * ALIGN
    sizes = list(range(0, 97, ALIGN))
    parts = [first, sizes[-1], -(-(tokens_here + ALIGN - first - sizes[-1]) // ALIGN) * ALIGN]
    most = sum(parts)
    scale = features.shape[1] ** (-0.5)
    places = members * share + most

    vmem = pl.BlockSpec(memory_space=pltpu.VMEM)
    anywhere = pl.BlockSpec(memory_space=pl.ANY)
    smem = pl.BlockSpec(memory_space=pltpu.SMEM)
    params = pltpu.CompilerParams(vmem_limit_bytes=40 * 2**20)
    large = pltpu.CompilerParams(vmem_limit_bytes=56 * 2**20)

    def array(rows, width, dtype):
        return jax.ShapeDtypeStruct((rows, width), dtype)

    def cost(flops, moved):
        return pl.CostEstimate(flops=flops, bytes_accessed=moved, transcendentals=0)

    def block_scratch(*count):
        return [
            pltpu.VMEM((*count, tokens_here, local_rows), jnp.bfloat16),
            pltpu.SemaphoreType.DMA((*count, max(1, local_rows // 256))),
        ]

    def sent_to(offsets):
        count = len(offsets)
        *arrays, choice = pl.pallas_call(
            functools.partial(sent_kernel, members, offsets, sizes),
            in_specs=[smem, anywhere],
            out_specs=[vmem] * (3 * count) + [smem],
            out_shape=[array(rows, local_rows, jnp.bfloat16) for rows in parts for _ in offsets]
            + [jax.ShapeDtypeStruct((2,), jnp.int32)],
            scratch_shapes=block_scratch(count),
            compiler_params=large,
            cost_estimate=cost(
                2 * count * first * tokens_here * local_rows,
                2 * count * (tokens_here + first) * local_rows,
            ),
        )(lengths, features)
        return [arrays[j * count : (j + 1) * count] for j in range(3)], choice

    far = members // 2
    near = [i for i in range(1, members) if i != far]
    far_parts, choice = sent_to([far])
    near_parts, _ = sent_to(near)
    held_far = turned(far_parts[0][0], far)
    offsets = [far] + near
    held_more = lax.switch(
        choice[0],
        [functools.partial(more_rows, size, offsets) for size in sizes],
        far_parts[1] + near_parts[1],
    )
    held_rest = lax.cond(
        choice[1] > 0,
        functools.partial(more_rows, parts[2], offsets),
        functools.partial(more_rows, 0, offsets),
        far_parts[2] + near_parts[2],
    )
    near_first, held_more, held_rest, late_lengths = lax.optimization_barrier(
        (near_parts[0], held_more, held_rest, lengths)
    )
    held_first = [held_far] + [turned(block, i) for i, block in zip(near, near_first)]
    held = [part for group in zip(held_first, held_more, held_rest) for part in group]

    partner_master = swapped(master, "replica", distance_bit)
    own_rows, own_wanted, low, halves = pl.pallas_call(
        functools.partial(own_kernel, members),
        in_specs=[smem, anywhere, vmem, vmem, vmem],
        out_specs=[vmem] * 4,
        out_shape=[
            array(places, local_rows, jnp.bfloat16),
            array(most, columns, jnp.float32),
            array(local_rows, columns, jnp.bfloat16),
            array(local_rows, columns, jnp.float32),
        ],
        scratch_shapes=block_scratch(),
        compiler_params=params,
        cost_estimate=cost(
            2 * most * tokens_here * (local_rows + columns), 20 * local_rows * columns
        ),
    )(late_lengths, features, wanted, master, partner_master)

    width = columns // HALVES
    sum_shapes = [array(share, width, jnp.bfloat16 if i else jnp.float32) for i in range(members)]
    *sums, rows = pl.pallas_call(
        functools.partial(keys_kernel, members, offsets, scale),
        in_specs=[smem, vmem, vmem, vmem] + [anywhere] * (3 * members - 3),
        out_specs=[vmem] * (HALVES * members + 1),
        out_shape=sum_shapes * HALVES + [array(places, local_rows, jnp.bfloat16)],
        input_output_aliases={3: HALVES * members},
        scratch_shapes=[
            pltpu.VMEM((places, width), jnp.float32),
            pltpu.VMEM((members - 1, first, local_rows), jnp.bfloat16),
            pltpu.VMEM((parts[1], local_rows), jnp.bfloat16),
            pltpu.VMEM((parts[2], local_rows), jnp.bfloat16),
            pltpu.SemaphoreType.DMA((members - 1,)),
            pltpu.SemaphoreType.DMA((2 * members - 2,)),
        ],
        compiler_params=params,
        cost_estimate=cost(
            2 * members * share * local_rows * columns, 4 * places * (local_rows + columns)
        ),
    )(lengths, own_wanted, low, own_rows, *held)
    sums = [sums[half * members : (half + 1) * members] for half in range(HALVES)]

    turned_rows = pl.pallas_call(
        turn_kernel,
        in_specs=[vmem],
        out_specs=vmem,
        out_shape=array(local_rows, members * share, jnp.bfloat16),
        compiler_params=params,
        cost_estimate=cost(0, 4 * members * share * local_rows),
    )(rows)

    gradients, partners, squares = [], [], 0.0
    for half in range(HALVES):
        residual = sums[half][0]
        for i in range(1, members):
            residual = residual + turned(sums[half][i], i).astype(jnp.float32)
        residual = residual.astype(jnp.bfloat16)
        residuals = [residual] + [turned(residual, i) for i in range(1, members)]
        gradient, low_gradient, own_squares = pl.pallas_call(
            functools.partial(gradient_kernel, members),
            in_specs=[vmem] + [vmem] * members,
            out_specs=[vmem] * 3,
            out_shape=[
                array(local_rows, width, jnp.float32),
                array(local_rows, width, jnp.bfloat16),
                array(8, 128, jnp.float32),
            ],
            scratch_shapes=[pltpu.VMEM((members * share, width), jnp.bfloat16)],
            compiler_params=params,
            cost_estimate=cost(
                2 * members * share * local_rows * width, 8 * local_rows * width
            ),
        )(turned_rows, *residuals)
        gradients.append(gradient)
        partners.append(swapped(low_gradient, "replica", distance_bit))
        squares = squares + own_squares

    total = squares
    for i in range(1, members):
        total = total + turned(squares, i)
    partner_total = swapped(total, "replica", distance_bit)

    averaged = pl.pallas_call(
        functools.partial(average_kernel, members * local_rows * columns),
        in_specs=[vmem] * (3 + 2 * HALVES),
        out_specs=anywhere,
        out_shape=array(local_rows, columns, jnp.float32),
        scratch_shapes=[
            pltpu.VMEM((local_rows, columns), jnp.float32),
            pltpu.SemaphoreType.DMA((4,)),
        ],
        compiler_params=params,
    )(total, partner_total, halves, *gradients, *partners)
    return averaged[None]


def solution(mesh):
    return jax.shard_map(
        local,
        mesh=mesh,
        in_specs=(
            P("replica", "fsdp", None),
            P("replica", "fsdp", None),
            P("replica", "fsdp", None),
            P("replica", None),
        ),
        out_specs=P("replica", "fsdp", None),
        check_vma=False,
    )
```

```python
import functools

import jax
import jax.numpy as jnp
from jax import lax
from jax.experimental import pallas as pl
from jax.experimental.pallas import tpu as pltpu
from jax.sharding import PartitionSpec as P

SLOT = 64
STEP = 3
ALIGN = 16
HALVES = 2

learning_rate = 0.1
epsilon = 1e-06


def swapped(value, axis, bit):
    mask = 2**bit
    pairs = [(source, source ^ mask) for source in range(lax.axis_size(axis))]
    return lax.ppermute(value, axis, pairs)


def turned(value, distance):
    members = lax.axis_size("fsdp")
    ring = [(source, (source + distance) % members) for source in range(members)]
    return lax.ppermute(value, "fsdp", ring)


def live_before(lengths_ref, members):
    sequences = lengths_ref.shape[1] // members
    totals = [jnp.int32(0)]
    for member in range(members):
        total = totals[-1]
        for q in range(sequences):
            total = total + lengths_ref[0, member * sequences + q]
        totals.append(total)
    return totals


def chosen(values, index):
    value = values[0]
    for i in range(1, len(values)):
        value = jnp.where(index == i, values[i], value)
    return value


def aligned(place):
    return pl.multiple_of(place // ALIGN * ALIGN, ALIGN)


def token_places(lengths_ref, member, before, tokens):
    sequences = tokens // SLOT
    place = before % ALIGN
    slot = lax.broadcasted_iota(jnp.int32, (1, tokens), 1)
    places = jnp.full((1, tokens), -1, jnp.int32)
    for s in range(sequences):
        length = lengths_ref[0, member * sequences + s]
        position = slot - s * SLOT
        places = jnp.where((position >= 0) & (position < length), position + place, places)
        place = place + length
    return places


def picking(places, start, rows):
    row = lax.broadcasted_iota(jnp.int32, (rows, places.shape[1]), 0) + start
    return jnp.where(row == places, 1.0, 0.0).astype(jnp.bfloat16)


class Block:
    def __init__(self, features_ref, member, block_ref, sems):
        self.block_ref, self.width = block_ref, block_ref.shape[1] // sems.shape[0]
        start = member * block_ref.shape[1]
        self.copies = []
        for j in range(sems.shape[0]):
            there = pl.ds(pl.multiple_of(start + j * self.width, 128), self.width)
            here = pl.ds(j * self.width, self.width)
            copy = pltpu.make_async_copy(
                features_ref.at[:, there], block_ref.at[:, here], sems.at[j]
            )
            copy.start()
            self.copies.append(copy)

    def picked(self, pick, store, wait):
        for j, copy in enumerate(self.copies):
            if wait:
                copy.wait()
            here = slice(j * self.width, (j + 1) * self.width)
            rows = jnp.dot(pick, self.block_ref[:, here], preferred_element_type=jnp.float32)
            store(here, rows.astype(jnp.bfloat16))


def used_places(totals, first, sizes):
    choices = []
    for member in range(len(totals) - 1):
        used = totals[member + 1] - aligned(totals[member])
        choice = jnp.int32(0)
        for size in sizes[:-1]:
            choice = choice + jnp.where(used > first + size, 1, 0)
        choices.append(choice)
    return choices


def sent_kernel(members, offsets, sizes, lengths_ref, features_ref, *refs):
    count = len(offsets)
    outs, choice_ref = refs[: 2 * count], refs[2 * count]
    block_ref, first_ref, more_ref, sems, out_sems, more_sems = refs[2 * count + 1 :]
    index = lax.axis_index("fsdp")
    blocks = [
        Block(features_ref, lax.rem(index + i, members), block_ref.at[n], sems.at[n])
        for n, i in enumerate(offsets)
    ]
    totals = live_before(lengths_ref, members)
    before, end = chosen(totals[:-1], index), chosen(totals[1:], index)
    places = token_places(lengths_ref, index, before, block_ref.shape[1])
    first, more = first_ref.shape[1], more_ref.shape[1]
    pick = picking(places, 0, first)
    copies = []
    for n, block in enumerate(blocks):

        def store(here, rows, n=n):
            first_ref[n, :, here] = rows
            copy = pltpu.make_async_copy(
                first_ref.at[n, :, here],
                outs[n].at[:, here],
                out_sems.at[n, here.start // (here.stop - here.start)],
            )
            copy.start()
            copies.append(copy)

        block.picked(pick, store, True)

    @pl.when(end - aligned(before) > first)
    def _():
        further = picking(places, first, more)
        for n, block in enumerate(blocks):

            def store(here, rows, n=n):
                more_ref[n, :, here] = rows

            block.picked(further, store, False)
            copy = pltpu.make_async_copy(more_ref.at[n], outs[count + n], more_sems.at[n])
            copy.start()
            copy.wait()

    for member, choice in enumerate(used_places(totals, first, sizes)):
        choice_ref[member] = choice
    for copy in copies:
        copy.wait()


def own_kernel(
    members,
    far,
    scale,
    lengths_ref,
    features_ref,
    targets_ref,
    master_ref,
    partner_ref,
    far_ref,
    *refs,
):
    held_more = refs[:members]
    rows_ref, keys_ref, low_ref, halves_ref = refs[members : members + 4]
    block_ref, first_ref, more_ref, sems, first_sem, more_sems = refs[members + 4 :]
    index = lax.axis_index("fsdp")
    block = Block(features_ref, index, block_ref, sems)
    far_copy = pltpu.make_async_copy(far_ref, first_ref, first_sem)
    far_copy.start()
    rows_ref[...] = jnp.zeros_like(rows_ref)
    low_ref[...] = master_ref[...].astype(jnp.bfloat16)
    halves_ref[...] = 0.5 * (master_ref[...] + partner_ref[...])
    totals = live_before(lengths_ref, members)
    before = chosen(totals[:-1], index)
    first, more = first_ref.shape[0], more_ref.shape[0]
    places = token_places(lengths_ref, index, before, block_ref.shape[0])
    pick = picking(places, 0, first + more)

    def store(here, rows):
        rows_ref[pl.ds(aligned(before), first + more), here] = rows

    block.picked(pick, store, True)
    far_start = aligned(chosen(totals[:-1], lax.rem(index + members - far, members)))
    far_copy.wait()
    rows_ref[pl.ds(far_start, first)] += first_ref[...]
    for member in range(members):
        start = aligned(totals[member])
        used = totals[member + 1] - start

        @pl.when((member != index) & (used > first))
        def _(member=member, start=start, used=used):
            copy = pltpu.make_async_copy(held_more[member], more_ref, more_sems.at[member])
            copy.start()
            copy.wait()
            for k in range(0, more, ALIGN):

                @pl.when(used > first + k)
                def _(k=k):
                    rows_ref[pl.ds(start + first + k, ALIGN)] += more_ref[k : k + ALIGN]

    height = (rows_ref.shape[0] - first - more) // members

    @pl.loop(0, members)
    def _(j):
        here = pl.ds(pl.multiple_of(j * height, ALIGN), height)
        keys_ref[here] = (
            jnp.dot(rows_ref[here], low_ref[...], preferred_element_type=jnp.float32) * scale
        )

    keys_ref[pl.ds(aligned(before), first + more)] -= jnp.dot(
        pick, targets_ref[...], preferred_element_type=jnp.float32
    )


def keys_kernel(members, near, scale, lengths_ref, low_ref, keys_ref, *refs):
    blocks, sums, total_ref = refs[: len(near)], refs[len(near) : -1], refs[-1]
    del keys_ref
    index = lax.axis_index("fsdp")
    totals = live_before(lengths_ref, members)
    for i, block_ref in zip(near, blocks):
        start = aligned(chosen(totals[:-1], lax.rem(index + members - i, members)))
        total_ref[pl.ds(start, block_ref.shape[0])] += (
            jnp.dot(block_ref[...], low_ref[...], preferred_element_type=jnp.float32) * scale
        )
    share, width = sums[0].shape
    for half in range(HALVES):
        for i in range(members):
            owner = lax.rem(index + i, members)
            rows = pl.ds(pl.multiple_of(owner * share, ALIGN), share)
            out_ref = sums[half * members + i]
            here = slice(half * width, (half + 1) * width)
            out_ref[...] = total_ref[rows, here].astype(out_ref.dtype)


def turn_kernel(members, near, lengths_ref, rows_ref, *refs):
    blocks, (turned_ref, all_ref) = refs[: len(near)], refs[len(near) :]
    index = lax.axis_index("fsdp")
    totals = live_before(lengths_ref, members)
    all_ref[...] = rows_ref[...]
    for i, block_ref in zip(near, blocks):
        start = aligned(chosen(totals[:-1], lax.rem(index + members - i, members)))
        all_ref[pl.ds(start, block_ref.shape[0])] += block_ref[...]
    for start in range(0, turned_ref.shape[1], 128):
        turned_ref[:, start : start + 128] = all_ref[start : start + 128, :].T


def gradient_kernel(members, turned_ref, *refs):
    residuals, (gradient_ref, low_ref, squares_ref, all_ref) = refs[:members], refs[members:]
    index = lax.axis_index("fsdp")
    share = residuals[0].shape[0]
    for i in range(members):
        owner = lax.rem(index + members - i, members)
        all_ref[pl.ds(pl.multiple_of(owner * share, ALIGN), share)] = residuals[i][...]
    squares_ref[...] = jnp.zeros_like(squares_ref)
    height = min(256, turned_ref.shape[0])

    @pl.loop(0, turned_ref.shape[0] // height)
    def _(j):
        rows = pl.ds(pl.multiple_of(j * height, height), height)
        gradient = jnp.dot(turned_ref[rows], all_ref[...], preferred_element_type=jnp.float32)
        gradient_ref[rows] = gradient
        low_ref[rows] = gradient.astype(low_ref.dtype)
        squares = jnp.sum((gradient * gradient).reshape(-1, 8, gradient.shape[1]), axis=0)
        lanes = squares.shape[1] // 128
        squares_ref[...] += sum(squares[:, 128 * k : 128 * (k + 1)] for k in range(lanes))


def average_kernel(entries, own_ref, other_ref, halves_ref, *refs):
    gradients, partners, (out_ref, done_ref, sems) = refs[:HALVES], refs[HALVES:-3], refs[-3:]
    rate = 0.5 * learning_rate
    own = rate * lax.rsqrt(jnp.sum(own_ref[...], keepdims=True) / entries + epsilon)
    other = rate * lax.rsqrt(jnp.sum(other_ref[...], keepdims=True) / entries + epsilon)
    pieces = sems.shape[0]
    height = done_ref.shape[0] // pieces
    width = done_ref.shape[1] // HALVES
    copies = []
    for j in range(pieces):
        rows = pl.ds(j * height, height)
        for half in range(HALVES):
            here = slice(half * width, (half + 1) * width)
            done_ref[rows, here] = (
                halves_ref[rows, here]
                - gradients[half][rows] * own
                - partners[half][rows].astype(jnp.float32) * other
            )
        copies.append(pltpu.make_async_copy(done_ref.at[rows], out_ref.at[rows], sems.at[j]))
        copies[-1].start()
    for copy in copies:
        copy.wait()


def more_rows(size, source, offsets, blocks):
    if size == 0:
        return blocks[0]
    members = lax.axis_size("fsdp")
    moved = [
        lax.ppermute(block[:size], "fsdp", [(source, (source + i) % members)])
        for i, block in zip(offsets, blocks)
    ]
    return jnp.pad(sum(moved[1:], moved[0]), ((0, blocks[0].shape[0] - size), (0, 0)))


def local(activations, targets, weights, lengths):
    features = activations[0]
    wanted = targets[0]
    master = weights[0]
    tokens_here = features.shape[0]
    local_rows, columns = master.shape
    members = lax.axis_size("fsdp")
    distance_bit = STEP % (lax.axis_size("replica").bit_length() - 1)
    share = tokens_here // 2
    first = -(-(share + 32) // ALIGN) * ALIGN
    more = -(-(tokens_here + ALIGN - first) // ALIGN) * ALIGN
    steps = (16, 32, 48, 64, 80, 96, 128) if members <= 4 else (96,)
    sizes = [0] + [size for size in steps if size < more] + [more]
    most = first + more
    scale = features.shape[1] ** (-0.5)
    places = members * share + most

    vmem = pl.BlockSpec(memory_space=pltpu.VMEM)
    anywhere = pl.BlockSpec(memory_space=pl.ANY)
    smem = pl.BlockSpec(memory_space=pltpu.SMEM)
    params = pltpu.CompilerParams(vmem_limit_bytes=40 * 2**20)
    large = pltpu.CompilerParams(vmem_limit_bytes=56 * 2**20)

    def array(rows, width, dtype):
        return jax.ShapeDtypeStruct((rows, width), dtype)

    def cost(flops, moved):
        return pl.CostEstimate(flops=flops, bytes_accessed=moved, transcendentals=0)

    def sent_to(offsets):
        count = len(offsets)
        pieces = max(1, local_rows // 256)
        *arrays, choice = pl.pallas_call(
            functools.partial(sent_kernel, members, offsets, sizes),
            in_specs=[smem, anywhere],
            out_specs=[anywhere] * (2 * count) + [smem],
            out_shape=[
                array(rows, local_rows, jnp.bfloat16) for rows in (first, more) for _ in offsets
            ]
            + [jax.ShapeDtypeStruct((members,), jnp.int32)],
            scratch_shapes=[
                pltpu.VMEM((count, tokens_here, local_rows), jnp.bfloat16),
                pltpu.VMEM((count, first, local_rows), jnp.bfloat16),
                pltpu.VMEM((count, more, local_rows), jnp.bfloat16),
                pltpu.SemaphoreType.DMA((count, pieces)),
                pltpu.SemaphoreType.DMA((count, pieces)),
                pltpu.SemaphoreType.DMA((count,)),
            ],
            compiler_params=large,
            cost_estimate=cost(
                2 * count * first * tokens_here * local_rows,
                2 * count * (tokens_here + first) * local_rows,
            ),
        )(lengths, features)
        return arrays[:count], arrays[count:], choice

    far = members // 2
    near = [i for i in range(1, members) if i != far]
    far_first, far_more, choice = sent_to([far])
    near_first, near_more, _ = sent_to(near)
    held_far = turned(far_first[0], far)
    offsets = [far] + near
    held_more = [
        lax.switch(
            choice[source],
            [functools.partial(more_rows, size, source, offsets) for size in sizes],
            far_more + near_more,
        )
        for source in range(members)
    ]
    near_first, held_more, late_lengths = lax.optimization_barrier((near_first, held_more, lengths))
    held = [turned(block, i) for i, block in zip(near, near_first)]

    partner_master = swapped(master, "replica", distance_bit)
    rows, keys, low, halves = pl.pallas_call(
        functools.partial(own_kernel, members, far, scale),
        in_specs=[smem, anywhere, vmem, vmem, vmem, anywhere] + [anywhere] * members,
        out_specs=[vmem] * 4,
        out_shape=[
            array(places, local_rows, jnp.bfloat16),
            array(places, columns, jnp.float32),
            array(local_rows, columns, jnp.bfloat16),
            array(local_rows, columns, jnp.float32),
        ],
        scratch_shapes=[
            pltpu.VMEM((tokens_here, local_rows), jnp.bfloat16),
            pltpu.VMEM((first, local_rows), jnp.bfloat16),
            pltpu.VMEM((more, local_rows), jnp.bfloat16),
            pltpu.SemaphoreType.DMA((max(1, local_rows // 256),)),
            pltpu.SemaphoreType.DMA,
            pltpu.SemaphoreType.DMA((members,)),
        ],
        compiler_params=params,
        cost_estimate=cost(
            2 * (most * tokens_here + members * share * columns) * (local_rows + columns),
            20 * local_rows * columns,
        ),
    )(late_lengths, features, wanted, master, partner_master, held_far, *held_more)

    width = columns // HALVES
    sum_shapes = [array(share, width, jnp.bfloat16 if i else jnp.float32) for i in range(members)]
    *sums, _ = pl.pallas_call(
        functools.partial(keys_kernel, members, near, scale),
        in_specs=[smem, vmem, vmem] + [vmem] * len(near),
        out_specs=[vmem] * (HALVES * members + 1),
        out_shape=sum_shapes * HALVES + [array(places, columns, jnp.float32)],
        input_output_aliases={2: HALVES * members},
        compiler_params=params,
        cost_estimate=cost(
            2 * len(near) * first * local_rows * columns, 8 * places * columns
        ),
    )(lengths, low, keys, *held)
    sums = [sums[half * members : (half + 1) * members] for half in range(HALVES)]

    turned_rows = pl.pallas_call(
        functools.partial(turn_kernel, members, near),
        in_specs=[smem, vmem] + [vmem] * len(near),
        out_specs=vmem,
        out_shape=array(local_rows, members * share, jnp.bfloat16),
        scratch_shapes=[pltpu.VMEM((places, local_rows), jnp.bfloat16)],
        compiler_params=params,
        cost_estimate=cost(0, 4 * members * share * local_rows),
    )(lengths, rows, *held)

    gradients, partners, squares = [], [], 0.0
    for half in range(HALVES):
        residual = sums[half][0]
        for i in range(1, members):
            residual = residual + turned(sums[half][i], i).astype(jnp.float32)
        residual = residual.astype(jnp.bfloat16)
        residuals = [residual] + [turned(residual, i) for i in range(1, members)]
        gradient, low_gradient, own_squares = pl.pallas_call(
            functools.partial(gradient_kernel, members),
            in_specs=[vmem] + [vmem] * members,
            out_specs=[vmem] * 3,
            out_shape=[
                array(local_rows, width, jnp.float32),
                array(local_rows, width, jnp.bfloat16),
                array(8, 128, jnp.float32),
            ],
            scratch_shapes=[pltpu.VMEM((members * share, width), jnp.bfloat16)],
            compiler_params=params,
            cost_estimate=cost(
                2 * members * share * local_rows * width, 8 * local_rows * width
            ),
        )(turned_rows, *residuals)
        gradients.append(gradient)
        partners.append(swapped(low_gradient, "replica", distance_bit))
        squares = squares + own_squares

    total = squares
    for i in range(1, members):
        total = total + turned(squares, i)
    partner_total = swapped(total, "replica", distance_bit)

    averaged = pl.pallas_call(
        functools.partial(average_kernel, members * local_rows * columns),
        in_specs=[vmem] * (3 + 2 * HALVES),
        out_specs=anywhere,
        out_shape=array(local_rows, columns, jnp.float32),
        scratch_shapes=[
            pltpu.VMEM((local_rows, columns), jnp.float32),
            pltpu.SemaphoreType.DMA((4,)),
        ],
        compiler_params=params,
    )(total, partner_total, halves, *gradients, *partners)
    return averaged[None]


def solution(mesh):
    return jax.shard_map(
        local,
        mesh=mesh,
        in_specs=(
            P("replica", "fsdp", None),
            P("replica", "fsdp", None),
            P("replica", "fsdp", None),
            P("replica", None),
        ),
        out_specs=P("replica", "fsdp", None),
        check_vma=False,
    )
```

```python
import functools

import jax
import jax.numpy as jnp
from jax import lax
from jax.experimental import pallas as pl
from jax.experimental.pallas import tpu as pltpu
from jax.sharding import PartitionSpec as P

SLOT = 64
STEP = 3
ALIGN = 16
HALVES = 2

learning_rate = 0.1
epsilon = 1e-06


def swapped(value, axis, bit):
    mask = 2**bit
    pairs = [(source, source ^ mask) for source in range(lax.axis_size(axis))]
    return lax.ppermute(value, axis, pairs)


def turned(value, distance):
    members = lax.axis_size("fsdp")
    ring = [(source, (source + distance) % members) for source in range(members)]
    return lax.ppermute(value, "fsdp", ring)


def live_before(lengths_ref, members):
    sequences = lengths_ref.shape[1] // members
    totals = [jnp.int32(0)]
    for member in range(members):
        total = totals[-1]
        for q in range(sequences):
            total = total + lengths_ref[0, member * sequences + q]
        totals.append(total)
    return totals


def chosen(values, index):
    value = values[0]
    for i in range(1, len(values)):
        value = jnp.where(index == i, values[i], value)
    return value


def aligned(place):
    return pl.multiple_of(place // ALIGN * ALIGN, ALIGN)


def token_places(lengths_ref, member, before, tokens):
    sequences = tokens // SLOT
    place = before % ALIGN
    slot = lax.broadcasted_iota(jnp.int32, (1, tokens), 1)
    places = jnp.full((1, tokens), -1, jnp.int32)
    for s in range(sequences):
        length = lengths_ref[0, member * sequences + s]
        position = slot - s * SLOT
        places = jnp.where((position >= 0) & (position < length), position + place, places)
        place = place + length
    return places


def picking(places, start, rows):
    row = lax.broadcasted_iota(jnp.int32, (rows, places.shape[1]), 0) + start
    return jnp.where(row == places, 1.0, 0.0).astype(jnp.bfloat16)


def other_half(index):
    half = index // 2
    return [2 - half, 3 - 3 * half]


class Block:
    def __init__(self, features_ref, member, block_ref, sems):
        self.block_ref, self.width = block_ref, block_ref.shape[1] // sems.shape[0]
        start = member * block_ref.shape[1]
        self.copies = []
        for j in range(sems.shape[0]):
            there = pl.ds(pl.multiple_of(start + j * self.width, 128), self.width)
            here = pl.ds(j * self.width, self.width)
            copy = pltpu.make_async_copy(
                features_ref.at[:, there], block_ref.at[:, here], sems.at[j]
            )
            copy.start()
            self.copies.append(copy)

    def picked(self, pick, store, wait):
        for j, copy in enumerate(self.copies):
            if wait:
                copy.wait()
            here = slice(j * self.width, (j + 1) * self.width)
            rows = jnp.dot(pick, self.block_ref[:, here], preferred_element_type=jnp.float32)
            store(here, rows.astype(jnp.bfloat16))


def used_places(totals, first, sizes):
    choices = []
    for member in range(len(totals) - 1):
        used = totals[member + 1] - aligned(totals[member])
        choice = jnp.int32(0)
        for size in sizes[:-1]:
            choice = choice + jnp.where(used > first + size, 1, 0)
        choices.append(choice)
    return choices


def sent_kernel(members, offsets, sizes, lengths_ref, features_ref, *refs):
    count = len(offsets)
    outs, choice_ref = refs[: 2 * count], refs[2 * count]
    block_ref, first_ref, more_ref, sems, out_sems, more_sems = refs[2 * count + 1 :]
    index = lax.axis_index("fsdp")
    blocks = [
        Block(features_ref, lax.rem(index + i, members), block_ref.at[n], sems.at[n])
        for n, i in enumerate(offsets)
    ]
    totals = live_before(lengths_ref, members)
    before, end = chosen(totals[:-1], index), chosen(totals[1:], index)
    places = token_places(lengths_ref, index, before, block_ref.shape[1])
    first, more = first_ref.shape[1], more_ref.shape[1]
    pick = picking(places, 0, first)
    copies = []
    for n, block in enumerate(blocks):

        def store(here, rows, n=n):
            first_ref[n, :, here] = rows
            copy = pltpu.make_async_copy(
                first_ref.at[n, :, here],
                outs[n].at[:, here],
                out_sems.at[n, here.start // (here.stop - here.start)],
            )
            copy.start()
            copies.append(copy)

        block.picked(pick, store, True)

    @pl.when(end - aligned(before) > first)
    def _():
        further = picking(places, first, more)
        for n, block in enumerate(blocks):

            def store(here, rows, n=n):
                more_ref[n, :, here] = rows

            block.picked(further, store, False)
            copy = pltpu.make_async_copy(more_ref.at[n], outs[count + n], more_sems.at[n])
            copy.start()
            copy.wait()

    for member, choice in enumerate(used_places(totals, first, sizes)):
        choice_ref[member] = choice
    for copy in copies:
        copy.wait()


def own_kernel(
    members,
    far,
    scale,
    lengths_ref,
    features_ref,
    targets_ref,
    master_ref,
    partner_ref,
    far_ref,
    *refs,
):
    held_more = refs[:members]
    rows_ref, keys_ref, low_ref, halves_ref = refs[members : members + 4]
    block_ref, first_ref, more_ref, sems, first_sem, more_sems = refs[members + 4 :]
    index = lax.axis_index("fsdp")
    block = Block(features_ref, index, block_ref, sems)
    far_copy = pltpu.make_async_copy(far_ref, first_ref, first_sem)
    far_copy.start()
    rows_ref[...] = jnp.zeros_like(rows_ref)
    low_ref[...] = master_ref[...].astype(jnp.bfloat16)
    halves_ref[...] = 0.5 * (master_ref[...] + partner_ref[...])
    totals = live_before(lengths_ref, members)
    before = chosen(totals[:-1], index)
    first, more = first_ref.shape[0], more_ref.shape[0]
    places = token_places(lengths_ref, index, before, block_ref.shape[0])
    pick = picking(places, 0, first + more)

    def store(here, rows):
        rows_ref[pl.ds(aligned(before), first + more), here] = rows

    block.picked(pick, store, True)
    far_start = aligned(chosen(totals[:-1], lax.rem(index + members - far, members)))
    far_copy.wait()
    rows_ref[pl.ds(far_start, first)] += first_ref[...]
    for member in range(members):
        start = aligned(totals[member])
        used = totals[member + 1] - start

        @pl.when((member != index) & (used > first))
        def _(member=member, start=start, used=used):
            copy = pltpu.make_async_copy(held_more[member], more_ref, more_sems.at[member])
            copy.start()
            copy.wait()
            for k in range(0, more, ALIGN):

                @pl.when(used > first + k)
                def _(k=k):
                    rows_ref[pl.ds(start + first + k, ALIGN)] += more_ref[k : k + ALIGN]

    height = (rows_ref.shape[0] - first - more) // members

    @pl.loop(0, members)
    def _(j):
        here = pl.ds(pl.multiple_of(j * height, ALIGN), height)
        keys_ref[here] = (
            jnp.dot(rows_ref[here], low_ref[...], preferred_element_type=jnp.float32) * scale
        )

    keys_ref[pl.ds(aligned(before), first + more)] -= jnp.dot(
        pick, targets_ref[...], preferred_element_type=jnp.float32
    )


def keys_kernel(members, near, scale, lengths_ref, low_ref, keys_ref, *refs):
    blocks, sums, total_ref = refs[: len(near)], refs[len(near) : -1], refs[-1]
    del keys_ref
    index = lax.axis_index("fsdp")
    totals = live_before(lengths_ref, members)
    for i, block_ref in zip(near, blocks):
        start = aligned(chosen(totals[:-1], lax.rem(index + members - i, members)))
        total_ref[pl.ds(start, block_ref.shape[0])] += (
            jnp.dot(block_ref[...], low_ref[...], preferred_element_type=jnp.float32) * scale
        )
    share, width = sums[0].shape
    count = len(sums) // HALVES
    if members == 4:
        owners = [[index], [jnp.bitwise_xor(index, 1)], other_half(index)]
    else:
        owners = [[lax.rem(index + i, members)] for i in range(members)]
    for half in range(HALVES):
        here = slice(half * width, (half + 1) * width)
        for out_ref, group in zip(sums[half * count : (half + 1) * count], owners):
            for n, owner in enumerate(group):
                rows = pl.ds(pl.multiple_of(owner * share, ALIGN), share)
                out_ref[n * share : (n + 1) * share] = total_ref[rows, here].astype(out_ref.dtype)


def turn_kernel(members, near, lengths_ref, rows_ref, *refs):
    blocks, (turned_ref, all_ref) = refs[: len(near)], refs[len(near) :]
    index = lax.axis_index("fsdp")
    totals = live_before(lengths_ref, members)
    all_ref[...] = rows_ref[...]
    for i, block_ref in zip(near, blocks):
        start = aligned(chosen(totals[:-1], lax.rem(index + members - i, members)))
        all_ref[pl.ds(start, block_ref.shape[0])] += block_ref[...]
    for start in range(0, turned_ref.shape[1], 128):
        turned_ref[:, start : start + 128] = all_ref[start : start + 128, :].T


def gradient_kernel(members, turned_ref, *refs):
    residuals, (gradient_ref, low_ref, squares_ref, all_ref) = refs[:-4], refs[-4:]
    index = lax.axis_index("fsdp")
    share = residuals[0].shape[0]

    def put(owner, block):
        all_ref[pl.ds(pl.multiple_of(owner * share, ALIGN), share)] = block

    if members == 4:
        own_ref, left_ref, right_ref, two_ref, pair_ref = residuals
        inner, outer = other_half(index)
        put(index, own_ref[...])
        pl.when(index > 0)(lambda: put(index - 1, left_ref[...]))
        pl.when(index < 3)(lambda: put(index + 1, right_ref[...]))

        @pl.when((index == 1) | (index == 2))
        def _():
            put(outer, two_ref[...])

        @pl.when((index == 0) | (index == 3))
        def _():
            put(inner, pair_ref[:share])
            put(outer, pair_ref[share:])
    else:
        for i in range(members):
            put(lax.rem(index + members - i, members), residuals[i][...])
    squares_ref[...] = jnp.zeros_like(squares_ref)
    height = min(256, turned_ref.shape[0])

    @pl.loop(0, turned_ref.shape[0] // height)
    def _(j):
        rows = pl.ds(pl.multiple_of(j * height, height), height)
        gradient = jnp.dot(turned_ref[rows], all_ref[...], preferred_element_type=jnp.float32)
        gradient_ref[rows] = gradient
        low_ref[rows] = gradient.astype(low_ref.dtype)
        squares = jnp.sum((gradient * gradient).reshape(-1, 8, gradient.shape[1]), axis=0)
        lanes = squares.shape[1] // 128
        squares_ref[...] += sum(squares[:, 128 * k : 128 * (k + 1)] for k in range(lanes))


def average_kernel(entries, own_ref, other_ref, halves_ref, *refs):
    gradients, partners, (out_ref, done_ref, sems) = refs[:HALVES], refs[HALVES:-3], refs[-3:]
    rate = 0.5 * learning_rate
    own = rate * lax.rsqrt(jnp.sum(own_ref[...], keepdims=True) / entries + epsilon)
    other = rate * lax.rsqrt(jnp.sum(other_ref[...], keepdims=True) / entries + epsilon)
    pieces = sems.shape[0]
    height = done_ref.shape[0] // pieces
    width = done_ref.shape[1] // HALVES
    copies = []
    for j in range(pieces):
        rows = pl.ds(j * height, height)
        for half in range(HALVES):
            here = slice(half * width, (half + 1) * width)
            done_ref[rows, here] = (
                halves_ref[rows, here]
                - gradients[half][rows] * own
                - partners[half][rows].astype(jnp.float32) * other
            )
        copies.append(pltpu.make_async_copy(done_ref.at[rows], out_ref.at[rows], sems.at[j]))
        copies[-1].start()
    for copy in copies:
        copy.wait()


def more_rows(size, source, offsets, blocks):
    if size == 0:
        return blocks[0]
    members = lax.axis_size("fsdp")
    moved = [
        lax.ppermute(block[:size], "fsdp", [(source, (source + i) % members)])
        for i, block in zip(offsets, blocks)
    ]
    return jnp.pad(sum(moved[1:], moved[0]), ((0, blocks[0].shape[0] - size), (0, 0)))


def sent_along(value, *pairs):
    return lax.ppermute(value, "fsdp", pairs)


def own_residual(sums):
    members = lax.axis_size("fsdp")
    if members == 4:
        own, near, far = sums
        share = own.shape[0]
        handed = sent_along(far, (0, 1), (3, 2)).astype(jnp.float32)
        far = (far.astype(jnp.float32) + handed).astype(far.dtype)
        received = [
            sent_along(far[:share], (1, 2), (2, 1)),
            sent_along(far[share:], (1, 3), (2, 0)),
            sent_along(near, (0, 1), (1, 0), (2, 3), (3, 2)),
        ]
    else:
        own = sums[0]
        received = [turned(sums[i], i) for i in range(1, members)]
    for part in received:
        own = own + part.astype(jnp.float32)
    return own.astype(jnp.bfloat16)


def all_residuals(residual):
    members = lax.axis_size("fsdp")
    if members == 4:
        left = sent_along(residual, (0, 1), (1, 2), (2, 3))
        right = sent_along(residual, (1, 0), (2, 1), (3, 2))
        two = sent_along(residual, (0, 2), (3, 1))
        inner = jnp.where(lax.axis_index("fsdp") < 2, right, left)
        pair = sent_along(jnp.concatenate([inner, two]), (1, 0), (2, 3))
        return [residual, left, right, two, pair]
    return [residual] + [turned(residual, i) for i in range(1, members)]


def local(activations, targets, weights, lengths):
    features = activations[0]
    wanted = targets[0]
    master = weights[0]
    tokens_here = features.shape[0]
    local_rows, columns = master.shape
    members = lax.axis_size("fsdp")
    distance_bit = STEP % (lax.axis_size("replica").bit_length() - 1)
    share = tokens_here // 2
    first = -(-(share + 32) // ALIGN) * ALIGN
    more = -(-(tokens_here + ALIGN - first) // ALIGN) * ALIGN
    steps = (16, 32, 48, 64, 80, 96, 128) if members <= 4 else (96,)
    sizes = [0] + [size for size in steps if size < more] + [more]
    most = first + more
    scale = features.shape[1] ** (-0.5)
    places = members * share + most

    vmem = pl.BlockSpec(memory_space=pltpu.VMEM)
    anywhere = pl.BlockSpec(memory_space=pl.ANY)
    smem = pl.BlockSpec(memory_space=pltpu.SMEM)
    params = pltpu.CompilerParams(vmem_limit_bytes=40 * 2**20)
    large = pltpu.CompilerParams(vmem_limit_bytes=56 * 2**20)

    def array(rows, width, dtype):
        return jax.ShapeDtypeStruct((rows, width), dtype)

    def cost(flops, moved):
        return pl.CostEstimate(flops=flops, bytes_accessed=moved, transcendentals=0)

    def sent_to(offsets):
        count = len(offsets)
        pieces = max(1, local_rows // 256)
        *arrays, choice = pl.pallas_call(
            functools.partial(sent_kernel, members, offsets, sizes),
            in_specs=[smem, anywhere],
            out_specs=[anywhere] * (2 * count) + [smem],
            out_shape=[
                array(rows, local_rows, jnp.bfloat16) for rows in (first, more) for _ in offsets
            ]
            + [jax.ShapeDtypeStruct((members,), jnp.int32)],
            scratch_shapes=[
                pltpu.VMEM((count, tokens_here, local_rows), jnp.bfloat16),
                pltpu.VMEM((count, first, local_rows), jnp.bfloat16),
                pltpu.VMEM((count, more, local_rows), jnp.bfloat16),
                pltpu.SemaphoreType.DMA((count, pieces)),
                pltpu.SemaphoreType.DMA((count, pieces)),
                pltpu.SemaphoreType.DMA((count,)),
            ],
            compiler_params=large,
            cost_estimate=cost(
                2 * count * first * tokens_here * local_rows,
                2 * count * (tokens_here + first) * local_rows,
            ),
        )(lengths, features)
        return arrays[:count], arrays[count:], choice

    far = members // 2
    near = [i for i in range(1, members) if i != far]
    far_first, far_more, choice = sent_to([far])
    near_first, near_more, _ = sent_to(near)
    held_far = turned(far_first[0], far)
    offsets = [far] + near
    held_more = [
        lax.switch(
            choice[source],
            [functools.partial(more_rows, size, source, offsets) for size in sizes],
            far_more + near_more,
        )
        for source in range(members)
    ]
    near_first, held_more, late_lengths = lax.optimization_barrier((near_first, held_more, lengths))
    held = [turned(block, i) for i, block in zip(near, near_first)]

    partner_master = swapped(master, "replica", distance_bit)
    rows, keys, low, halves = pl.pallas_call(
        functools.partial(own_kernel, members, far, scale),
        in_specs=[smem, anywhere, vmem, vmem, vmem, anywhere] + [anywhere] * members,
        out_specs=[vmem] * 4,
        out_shape=[
            array(places, local_rows, jnp.bfloat16),
            array(places, columns, jnp.float32),
            array(local_rows, columns, jnp.bfloat16),
            array(local_rows, columns, jnp.float32),
        ],
        scratch_shapes=[
            pltpu.VMEM((tokens_here, local_rows), jnp.bfloat16),
            pltpu.VMEM((first, local_rows), jnp.bfloat16),
            pltpu.VMEM((more, local_rows), jnp.bfloat16),
            pltpu.SemaphoreType.DMA((max(1, local_rows // 256),)),
            pltpu.SemaphoreType.DMA,
            pltpu.SemaphoreType.DMA((members,)),
        ],
        compiler_params=params,
        cost_estimate=cost(
            2 * (most * tokens_here + members * share * columns) * (local_rows + columns),
            20 * local_rows * columns,
        ),
    )(late_lengths, features, wanted, master, partner_master, held_far, *held_more)

    width = columns // HALVES
    counts = [1, 1, 2] if members == 4 else [1] * members
    sum_shapes = [
        array(n * share, width, jnp.bfloat16 if i else jnp.float32) for i, n in enumerate(counts)
    ]
    *sums, _ = pl.pallas_call(
        functools.partial(keys_kernel, members, near, scale),
        in_specs=[smem, vmem, vmem] + [vmem] * len(near),
        out_specs=[vmem] * (HALVES * len(counts) + 1),
        out_shape=sum_shapes * HALVES + [array(places, columns, jnp.float32)],
        input_output_aliases={2: HALVES * len(counts)},
        compiler_params=params,
        cost_estimate=cost(
            2 * len(near) * first * local_rows * columns, 8 * places * columns
        ),
    )(lengths, low, keys, *held)
    sums = [sums[half * len(counts) : (half + 1) * len(counts)] for half in range(HALVES)]

    turned_rows = pl.pallas_call(
        functools.partial(turn_kernel, members, near),
        in_specs=[smem, vmem] + [vmem] * len(near),
        out_specs=vmem,
        out_shape=array(local_rows, members * share, jnp.bfloat16),
        scratch_shapes=[pltpu.VMEM((places, local_rows), jnp.bfloat16)],
        compiler_params=params,
        cost_estimate=cost(0, 4 * members * share * local_rows),
    )(lengths, rows, *held)

    gradients, partners, squares = [], [], 0.0
    for half in range(HALVES):
        residuals = all_residuals(own_residual(sums[half]))
        gradient, low_gradient, own_squares = pl.pallas_call(
            functools.partial(gradient_kernel, members),
            in_specs=[vmem] * (1 + len(residuals)),
            out_specs=[vmem] * 3,
            out_shape=[
                array(local_rows, width, jnp.float32),
                array(local_rows, width, jnp.bfloat16),
                array(8, 128, jnp.float32),
            ],
            scratch_shapes=[pltpu.VMEM((members * share, width), jnp.bfloat16)],
            compiler_params=params,
            cost_estimate=cost(
                2 * members * share * local_rows * width, 8 * local_rows * width
            ),
        )(turned_rows, *residuals)
        gradients.append(gradient)
        partners.append(swapped(low_gradient, "replica", distance_bit))
        squares = squares + own_squares

    total = squares
    for i in range(1, members):
        total = total + turned(squares, i)
    partner_total = swapped(total, "replica", distance_bit)

    averaged = pl.pallas_call(
        functools.partial(average_kernel, members * local_rows * columns),
        in_specs=[vmem] * (3 + 2 * HALVES),
        out_specs=anywhere,
        out_shape=array(local_rows, columns, jnp.float32),
        scratch_shapes=[
            pltpu.VMEM((local_rows, columns), jnp.float32),
            pltpu.SemaphoreType.DMA((4,)),
        ],
        compiler_params=params,
    )(total, partner_total, halves, *gradients, *partners)
    return averaged[None]


def solution(mesh):
    return jax.shard_map(
        local,
        mesh=mesh,
        in_specs=(
            P("replica", "fsdp", None),
            P("replica", "fsdp", None),
            P("replica", "fsdp", None),
            P("replica", None),
        ),
        out_specs=P("replica", "fsdp", None),
        check_vma=False,
    )
```

```python
import functools

import jax
import jax.numpy as jnp
from jax import lax
from jax.experimental import pallas as pl
from jax.experimental.pallas import tpu as pltpu
from jax.sharding import PartitionSpec as P

SLOT = 64
STEP = 3
ALIGN = 16
HALVES = 2

learning_rate = 0.1
epsilon = 1e-06


def swapped(value, axis, bit):
    mask = 2**bit
    pairs = [(source, source ^ mask) for source in range(lax.axis_size(axis))]
    return lax.ppermute(value, axis, pairs)


def turned(value, distance):
    members = lax.axis_size("fsdp")
    ring = [(source, (source + distance) % members) for source in range(members)]
    return lax.ppermute(value, "fsdp", ring)


def live_before(lengths_ref, members):
    sequences = lengths_ref.shape[1] // members
    totals = [jnp.int32(0)]
    for member in range(members):
        total = totals[-1]
        for q in range(sequences):
            total = total + lengths_ref[0, member * sequences + q]
        totals.append(total)
    return totals


def chosen(values, index):
    value = values[0]
    for i in range(1, len(values)):
        value = jnp.where(index == i, values[i], value)
    return value


def aligned(place):
    return pl.multiple_of(place // ALIGN * ALIGN, ALIGN)


def token_places(lengths_ref, member, before, tokens):
    sequences = tokens // SLOT
    place = before % ALIGN
    slot = lax.broadcasted_iota(jnp.int32, (1, tokens), 1)
    places = jnp.full((1, tokens), -1, jnp.int32)
    for s in range(sequences):
        length = lengths_ref[0, member * sequences + s]
        position = slot - s * SLOT
        places = jnp.where((position >= 0) & (position < length), position + place, places)
        place = place + length
    return places


def picking(places, start, rows):
    row = lax.broadcasted_iota(jnp.int32, (rows, places.shape[1]), 0) + start
    return jnp.where(row == places, 1.0, 0.0).astype(jnp.bfloat16)


class Block:
    def __init__(self, features_ref, member, block_ref, sems):
        self.block_ref, self.width = block_ref, block_ref.shape[1] // sems.shape[0]
        start = member * block_ref.shape[1]
        self.copies = []
        for j in range(sems.shape[0]):
            there = pl.ds(pl.multiple_of(start + j * self.width, 128), self.width)
            here = pl.ds(j * self.width, self.width)
            copy = pltpu.make_async_copy(
                features_ref.at[:, there], block_ref.at[:, here], sems.at[j]
            )
            copy.start()
            self.copies.append(copy)

    def picked(self, pick, store, wait):
        for j, copy in enumerate(self.copies):
            if wait:
                copy.wait()
            here = slice(j * self.width, (j + 1) * self.width)
            rows = jnp.dot(pick, self.block_ref[:, here], preferred_element_type=jnp.float32)
            store(here, rows.astype(jnp.bfloat16))


def used_places(totals, first, sizes):
    choices = []
    for member in range(len(totals) - 1):
        used = totals[member + 1] - aligned(totals[member])
        choice = jnp.int32(0)
        for size in sizes[:-1]:
            choice = choice + jnp.where(used > first + size, 1, 0)
        choices.append(choice)
    return choices


def sent_kernel(members, offsets, sizes, lengths_ref, features_ref, *refs):
    count = len(offsets)
    outs, choice_ref = refs[: 2 * count], refs[2 * count]
    block_ref, first_ref, more_ref, sems, out_sems, more_sems = refs[2 * count + 1 :]
    index = lax.axis_index("fsdp")
    blocks = [
        Block(features_ref, lax.rem(index + i, members), block_ref.at[n], sems.at[n])
        for n, i in enumerate(offsets)
    ]
    totals = live_before(lengths_ref, members)
    before, end = chosen(totals[:-1], index), chosen(totals[1:], index)
    places = token_places(lengths_ref, index, before, block_ref.shape[1])
    first, more = first_ref.shape[1], more_ref.shape[1]
    pick = picking(places, 0, first)
    copies = []
    for n, block in enumerate(blocks):

        def store(here, rows, n=n):
            first_ref[n, :, here] = rows
            copy = pltpu.make_async_copy(
                first_ref.at[n, :, here],
                outs[n].at[:, here],
                out_sems.at[n, here.start // (here.stop - here.start)],
            )
            copy.start()
            copies.append(copy)

        block.picked(pick, store, True)

    @pl.when(end - aligned(before) > first)
    def _():
        further = picking(places, first, more)
        for n, block in enumerate(blocks):

            def store(here, rows, n=n):
                more_ref[n, :, here] = rows

            block.picked(further, store, False)
            copy = pltpu.make_async_copy(more_ref.at[n], outs[count + n], more_sems.at[n])
            copy.start()
            copy.wait()

    for member, choice in enumerate(used_places(totals, first, sizes)):
        choice_ref[member] = choice
    for copy in copies:
        copy.wait()


def own_kernel(
    members,
    early,
    scale,
    lengths_ref,
    features_ref,
    targets_ref,
    master_ref,
    partner_ref,
    early_ref,
    *refs,
):
    held_more = refs[:members]
    rows_ref, keys_ref, low_ref, halves_ref = refs[members : members + 4]
    block_ref, first_ref, more_ref, sems, first_sem, more_sems = refs[members + 4 :]
    index = lax.axis_index("fsdp")
    block = Block(features_ref, index, block_ref, sems)
    early_copy = pltpu.make_async_copy(early_ref, first_ref, first_sem)
    early_copy.start()
    rows_ref[...] = jnp.zeros_like(rows_ref)
    low_ref[...] = master_ref[...].astype(jnp.bfloat16)
    halves_ref[...] = 0.5 * (master_ref[...] + partner_ref[...])
    totals = live_before(lengths_ref, members)
    before = chosen(totals[:-1], index)
    first, more = first_ref.shape[0], more_ref.shape[0]
    places = token_places(lengths_ref, index, before, block_ref.shape[0])
    pick = picking(places, 0, first + more)

    def store(here, rows):
        rows_ref[pl.ds(aligned(before), first + more), here] = rows

    block.picked(pick, store, True)
    early_start = aligned(chosen(totals[:-1], lax.rem(index + members - early, members)))
    early_copy.wait()
    rows_ref[pl.ds(early_start, first)] += first_ref[...]
    for member in range(members):
        start = aligned(totals[member])
        used = totals[member + 1] - start

        @pl.when((member != index) & (used > first))
        def _(member=member, start=start, used=used):
            copy = pltpu.make_async_copy(held_more[member], more_ref, more_sems.at[member])
            copy.start()
            copy.wait()
            for k in range(0, more, ALIGN):

                @pl.when(used > first + k)
                def _(k=k):
                    rows_ref[pl.ds(start + first + k, ALIGN)] += more_ref[k : k + ALIGN]

    height = (rows_ref.shape[0] - first - more) // members

    @pl.loop(0, members)
    def _(j):
        here = pl.ds(pl.multiple_of(j * height, ALIGN), height)
        keys_ref[here] = (
            jnp.dot(rows_ref[here], low_ref[...], preferred_element_type=jnp.float32) * scale
        )

    keys_ref[pl.ds(aligned(before), first + more)] -= jnp.dot(
        pick, targets_ref[...], preferred_element_type=jnp.float32
    )


def keys_kernel(members, late, scale, lengths_ref, low_ref, keys_ref, *refs):
    blocks, sums, total_ref = refs[: len(late)], refs[len(late) : -1], refs[-1]
    del keys_ref
    index = lax.axis_index("fsdp")
    totals = live_before(lengths_ref, members)
    for i, block_ref in zip(late, blocks):
        start = aligned(chosen(totals[:-1], lax.rem(index + members - i, members)))
        total_ref[pl.ds(start, block_ref.shape[0])] += (
            jnp.dot(block_ref[...], low_ref[...], preferred_element_type=jnp.float32) * scale
        )
    share, width = sums[0].shape
    for half in range(HALVES):
        for i in range(members):
            owner = lax.rem(index + i, members)
            rows = pl.ds(pl.multiple_of(owner * share, ALIGN), share)
            out_ref = sums[half * members + i]
            here = slice(half * width, (half + 1) * width)
            out_ref[...] = total_ref[rows, here].astype(out_ref.dtype)


def turn_kernel(members, late, lengths_ref, rows_ref, *refs):
    blocks, (turned_ref, all_ref) = refs[: len(late)], refs[len(late) :]
    index = lax.axis_index("fsdp")
    totals = live_before(lengths_ref, members)
    all_ref[...] = rows_ref[...]
    for i, block_ref in zip(late, blocks):
        start = aligned(chosen(totals[:-1], lax.rem(index + members - i, members)))
        all_ref[pl.ds(start, block_ref.shape[0])] += block_ref[...]
    for start in range(0, turned_ref.shape[1], 128):
        turned_ref[:, start : start + 128] = all_ref[start : start + 128, :].T


def gradient_kernel(members, turned_ref, *refs):
    residuals, (gradient_ref, low_ref, squares_ref, all_ref) = refs[:members], refs[members:]
    index = lax.axis_index("fsdp")
    share = residuals[0].shape[0]
    for i in range(members):
        owner = lax.rem(index + members - i, members)
        all_ref[pl.ds(pl.multiple_of(owner * share, ALIGN), share)] = residuals[i][...]
    squares_ref[...] = jnp.zeros_like(squares_ref)
    height = min(256, turned_ref.shape[0])

    @pl.loop(0, turned_ref.shape[0] // height)
    def _(j):
        rows = pl.ds(pl.multiple_of(j * height, height), height)
        gradient = jnp.dot(turned_ref[rows], all_ref[...], preferred_element_type=jnp.float32)
        gradient_ref[rows] = gradient
        low_ref[rows] = gradient.astype(low_ref.dtype)
        squares = jnp.sum((gradient * gradient).reshape(-1, 8, gradient.shape[1]), axis=0)
        lanes = squares.shape[1] // 128
        squares_ref[...] += sum(squares[:, 128 * k : 128 * (k + 1)] for k in range(lanes))


def average_kernel(entries, own_ref, other_ref, halves_ref, *refs):
    gradients, partners, (out_ref, done_ref, sems) = refs[:HALVES], refs[HALVES:-3], refs[-3:]
    rate = 0.5 * learning_rate
    own = rate * lax.rsqrt(jnp.sum(own_ref[...], keepdims=True) / entries + epsilon)
    other = rate * lax.rsqrt(jnp.sum(other_ref[...], keepdims=True) / entries + epsilon)
    pieces = sems.shape[0]
    height = done_ref.shape[0] // pieces
    width = done_ref.shape[1] // HALVES
    copies = []
    for j in range(pieces):
        rows = pl.ds(j * height, height)
        for half in range(HALVES):
            here = slice(half * width, (half + 1) * width)
            done_ref[rows, here] = (
                halves_ref[rows, here]
                - gradients[half][rows] * own
                - partners[half][rows].astype(jnp.float32) * other
            )
        copies.append(pltpu.make_async_copy(done_ref.at[rows], out_ref.at[rows], sems.at[j]))
        copies[-1].start()
    for copy in copies:
        copy.wait()


def more_rows(size, source, offsets, blocks):
    if size == 0:
        return blocks[0]
    members = lax.axis_size("fsdp")
    moved = [
        lax.ppermute(block[:size], "fsdp", [(source, (source + i) % members)])
        for i, block in zip(offsets, blocks)
    ]
    return jnp.pad(sum(moved[1:], moved[0]), ((0, blocks[0].shape[0] - size), (0, 0)))


def local(activations, targets, weights, lengths):
    features = activations[0]
    wanted = targets[0]
    master = weights[0]
    tokens_here = features.shape[0]
    local_rows, columns = master.shape
    members = lax.axis_size("fsdp")
    distance_bit = STEP % (lax.axis_size("replica").bit_length() - 1)
    share = tokens_here // 2
    first = -(-(share + 32) // ALIGN) * ALIGN
    more = -(-(tokens_here + ALIGN - first) // ALIGN) * ALIGN
    steps = (16, 32, 48, 64, 80, 96, 128) if members <= 4 else (96,)
    sizes = [0] + [size for size in steps if size < more] + [more]
    most = first + more
    scale = features.shape[1] ** (-0.5)
    places = members * share + most

    vmem = pl.BlockSpec(memory_space=pltpu.VMEM)
    anywhere = pl.BlockSpec(memory_space=pl.ANY)
    smem = pl.BlockSpec(memory_space=pltpu.SMEM)
    params = pltpu.CompilerParams(vmem_limit_bytes=40 * 2**20)
    large = pltpu.CompilerParams(vmem_limit_bytes=56 * 2**20)

    def array(rows, width, dtype):
        return jax.ShapeDtypeStruct((rows, width), dtype)

    def cost(flops, moved):
        return pl.CostEstimate(flops=flops, bytes_accessed=moved, transcendentals=0)

    def sent_to(offsets):
        count = len(offsets)
        pieces = max(1, local_rows // 256)
        *arrays, choice = pl.pallas_call(
            functools.partial(sent_kernel, members, offsets, sizes),
            in_specs=[smem, anywhere],
            out_specs=[anywhere] * (2 * count) + [smem],
            out_shape=[
                array(rows, local_rows, jnp.bfloat16) for rows in (first, more) for _ in offsets
            ]
            + [jax.ShapeDtypeStruct((members,), jnp.int32)],
            scratch_shapes=[
                pltpu.VMEM((count, tokens_here, local_rows), jnp.bfloat16),
                pltpu.VMEM((count, first, local_rows), jnp.bfloat16),
                pltpu.VMEM((count, more, local_rows), jnp.bfloat16),
                pltpu.SemaphoreType.DMA((count, pieces)),
                pltpu.SemaphoreType.DMA((count, pieces)),
                pltpu.SemaphoreType.DMA((count,)),
            ],
            compiler_params=large,
            cost_estimate=cost(
                2 * count * first * tokens_here * local_rows,
                2 * count * (tokens_here + first) * local_rows,
            ),
        )(lengths, features)
        return arrays[:count], arrays[count:], choice

    early = 1
    late = list(range(2, members))
    early_first, early_more, choice = sent_to([early])
    late_first, late_more, _ = sent_to(late)
    held_early = turned(early_first[0], early)
    offsets = [early] + late
    held_more = [
        lax.switch(
            choice[source],
            [functools.partial(more_rows, size, source, offsets) for size in sizes],
            early_more + late_more,
        )
        for source in range(members)
    ]
    late_first, held_more, late_lengths = lax.optimization_barrier((late_first, held_more, lengths))
    held = [turned(block, i) for i, block in zip(late, late_first)]

    partner_master = swapped(master, "replica", distance_bit)
    rows, keys, low, halves = pl.pallas_call(
        functools.partial(own_kernel, members, early, scale),
        in_specs=[smem, anywhere, vmem, vmem, vmem, anywhere] + [anywhere] * members,
        out_specs=[vmem] * 4,
        out_shape=[
            array(places, local_rows, jnp.bfloat16),
            array(places, columns, jnp.float32),
            array(local_rows, columns, jnp.bfloat16),
            array(local_rows, columns, jnp.float32),
        ],
        scratch_shapes=[
            pltpu.VMEM((tokens_here, local_rows), jnp.bfloat16),
            pltpu.VMEM((first, local_rows), jnp.bfloat16),
            pltpu.VMEM((more, local_rows), jnp.bfloat16),
            pltpu.SemaphoreType.DMA((max(1, local_rows // 256),)),
            pltpu.SemaphoreType.DMA,
            pltpu.SemaphoreType.DMA((members,)),
        ],
        compiler_params=params,
        cost_estimate=cost(
            2 * (most * tokens_here + members * share * columns) * (local_rows + columns),
            20 * local_rows * columns,
        ),
    )(late_lengths, features, wanted, master, partner_master, held_early, *held_more)

    width = columns // HALVES
    sum_shapes = [array(share, width, jnp.bfloat16 if i else jnp.float32) for i in range(members)]
    *sums, _ = pl.pallas_call(
        functools.partial(keys_kernel, members, late, scale),
        in_specs=[smem, vmem, vmem] + [vmem] * len(late),
        out_specs=[vmem] * (HALVES * members + 1),
        out_shape=sum_shapes * HALVES + [array(places, columns, jnp.float32)],
        input_output_aliases={2: HALVES * members},
        compiler_params=params,
        cost_estimate=cost(
            2 * len(late) * first * local_rows * columns, 8 * places * columns
        ),
    )(lengths, low, keys, *held)
    sums = [sums[half * members : (half + 1) * members] for half in range(HALVES)]

    turned_rows = pl.pallas_call(
        functools.partial(turn_kernel, members, late),
        in_specs=[smem, vmem] + [vmem] * len(late),
        out_specs=vmem,
        out_shape=array(local_rows, members * share, jnp.bfloat16),
        scratch_shapes=[pltpu.VMEM((places, local_rows), jnp.bfloat16)],
        compiler_params=params,
        cost_estimate=cost(0, 4 * members * share * local_rows),
    )(lengths, rows, *held)

    gradients, partners, squares = [], [], 0.0
    for half in range(HALVES):
        residual = sums[half][0]
        for i in range(1, members):
            residual = residual + turned(sums[half][i], i).astype(jnp.float32)
        residual = residual.astype(jnp.bfloat16)
        residuals = [residual] + [turned(residual, i) for i in range(1, members)]
        gradient, low_gradient, own_squares = pl.pallas_call(
            functools.partial(gradient_kernel, members),
            in_specs=[vmem] + [vmem] * members,
            out_specs=[vmem] * 3,
            out_shape=[
                array(local_rows, width, jnp.float32),
                array(local_rows, width, jnp.bfloat16),
                array(8, 128, jnp.float32),
            ],
            scratch_shapes=[pltpu.VMEM((members * share, width), jnp.bfloat16)],
            compiler_params=params,
            cost_estimate=cost(
                2 * members * share * local_rows * width, 8 * local_rows * width
            ),
        )(turned_rows, *residuals)
        gradients.append(gradient)
        partners.append(swapped(low_gradient, "replica", distance_bit))
        squares = squares + own_squares

    total = squares
    for i in range(1, members):
        total = total + turned(squares, i)
    partner_total = swapped(total, "replica", distance_bit)

    averaged = pl.pallas_call(
        functools.partial(average_kernel, members * local_rows * columns),
        in_specs=[vmem] * (3 + 2 * HALVES),
        out_specs=anywhere,
        out_shape=array(local_rows, columns, jnp.float32),
        scratch_shapes=[
            pltpu.VMEM((local_rows, columns), jnp.float32),
            pltpu.SemaphoreType.DMA((4,)),
        ],
        compiler_params=params,
    )(total, partner_total, halves, *gradients, *partners)
    return averaged[None]


def solution(mesh):
    return jax.shard_map(
        local,
        mesh=mesh,
        in_specs=(
            P("replica", "fsdp", None),
            P("replica", "fsdp", None),
            P("replica", "fsdp", None),
            P("replica", None),
        ),
        out_specs=P("replica", "fsdp", None),
        check_vma=False,
    )
```

```python
import functools

import jax
import jax.numpy as jnp
from jax import lax
from jax.experimental import pallas as pl
from jax.experimental.pallas import tpu as pltpu
from jax.sharding import PartitionSpec as P

SLOT = 64
STEP = 3
ALIGN = 16
HALVES = 2

learning_rate = 0.1
epsilon = 1e-06


def swapped(value, axis, bit):
    mask = 2**bit
    pairs = [(source, source ^ mask) for source in range(lax.axis_size(axis))]
    return lax.ppermute(value, axis, pairs)


def turned(value, distance):
    members = lax.axis_size("fsdp")
    ring = [(source, (source + distance) % members) for source in range(members)]
    return lax.ppermute(value, "fsdp", ring)


def sent_across(value, bit, distance):
    members = lax.axis_size("fsdp")
    pairs = [
        (
            replica * members + member,
            (replica ^ 2**bit) * members + (member + distance) % members,
        )
        for replica in range(lax.axis_size("replica"))
        for member in range(members)
    ]
    return lax.ppermute(value, ("replica", "fsdp"), pairs)


def live_before(lengths_ref, members):
    sequences = lengths_ref.shape[1] // members
    totals = [jnp.int32(0)]
    for member in range(members):
        total = totals[-1]
        for q in range(sequences):
            total = total + lengths_ref[0, member * sequences + q]
        totals.append(total)
    return totals


def chosen(values, index):
    value = values[0]
    for i in range(1, len(values)):
        value = jnp.where(index == i, values[i], value)
    return value


def aligned(place):
    return pl.multiple_of(place // ALIGN * ALIGN, ALIGN)


def token_places(lengths_ref, member, before, tokens):
    sequences = tokens // SLOT
    place = before % ALIGN
    slot = lax.broadcasted_iota(jnp.int32, (1, tokens), 1)
    places = jnp.full((1, tokens), -1, jnp.int32)
    for s in range(sequences):
        length = lengths_ref[0, member * sequences + s]
        position = slot - s * SLOT
        places = jnp.where((position >= 0) & (position < length), position + place, places)
        place = place + length
    return places


def picking(places, start, rows):
    row = lax.broadcasted_iota(jnp.int32, (rows, places.shape[1]), 0) + start
    return jnp.where(row == places, 1.0, 0.0).astype(jnp.bfloat16)


class Block:
    def __init__(self, features_ref, member, block_ref, sems):
        self.block_ref, self.width = block_ref, block_ref.shape[1] // sems.shape[0]
        start = member * block_ref.shape[1]
        self.copies = []
        for j in range(sems.shape[0]):
            there = pl.ds(pl.multiple_of(start + j * self.width, 128), self.width)
            here = pl.ds(j * self.width, self.width)
            copy = pltpu.make_async_copy(
                features_ref.at[:, there], block_ref.at[:, here], sems.at[j]
            )
            copy.start()
            self.copies.append(copy)

    def picked(self, pick, store, wait):
        for j, copy in enumerate(self.copies):
            if wait:
                copy.wait()
            here = slice(j * self.width, (j + 1) * self.width)
            rows = jnp.dot(pick, self.block_ref[:, here], preferred_element_type=jnp.float32)
            store(here, rows.astype(jnp.bfloat16))


def used_places(totals, first, sizes):
    choices = []
    for member in range(len(totals) - 1):
        used = totals[member + 1] - aligned(totals[member])
        choice = jnp.int32(0)
        for size in sizes[:-1]:
            choice = choice + jnp.where(used > first + size, 1, 0)
        choices.append(choice)
    return choices


def sent_kernel(members, offsets, sizes, lengths_ref, features_ref, *refs):
    count = len(offsets)
    outs, choice_refs = refs[: 2 * count], refs[2 * count : -6]
    block_ref, first_ref, more_ref, sems, out_sems, more_sems = refs[-6:]
    index = lax.axis_index("fsdp")
    blocks = [
        Block(features_ref, lax.rem(index + i, members), block_ref.at[n], sems.at[n])
        for n, i in enumerate(offsets)
    ]
    totals = live_before(lengths_ref, members)
    before, end = chosen(totals[:-1], index), chosen(totals[1:], index)
    places = token_places(lengths_ref, index, before, block_ref.shape[1])
    first, more = first_ref.shape[1], more_ref.shape[1]
    pick = picking(places, 0, first)
    copies = []
    for n, block in enumerate(blocks):

        def store(here, rows, n=n):
            first_ref[n, :, here] = rows
            copy = pltpu.make_async_copy(
                first_ref.at[n, :, here],
                outs[n].at[:, here],
                out_sems.at[n, here.start // (here.stop - here.start)],
            )
            copy.start()
            copies.append(copy)

        block.picked(pick, store, True)

    @pl.when(end - aligned(before) > first)
    def _():
        further = picking(places, first, more)
        for n, block in enumerate(blocks):

            def store(here, rows, n=n):
                more_ref[n, :, here] = rows

            block.picked(further, store, False)
            copy = pltpu.make_async_copy(more_ref.at[n], outs[count + n], more_sems.at[n])
            copy.start()
            copy.wait()

    for choice_ref, choice in zip(choice_refs, used_places(totals, first, sizes)):
        choice_ref[0] = choice
    for copy in copies:
        copy.wait()


def own_kernel(
    members,
    far,
    scale,
    lengths_ref,
    features_ref,
    targets_ref,
    master_ref,
    partner_ref,
    far_ref,
    *refs,
):
    held_more = refs[:members]
    rows_ref, keys_ref, low_ref, halves_ref = refs[members : members + 4]
    block_ref, first_ref, more_ref, sems, first_sem, more_sems = refs[members + 4 :]
    index = lax.axis_index("fsdp")
    block = Block(features_ref, index, block_ref, sems)
    far_copy = pltpu.make_async_copy(far_ref, first_ref, first_sem)
    far_copy.start()
    rows_ref[...] = jnp.zeros_like(rows_ref)
    low_ref[...] = master_ref[...].astype(jnp.bfloat16)
    halves_ref[...] = 0.5 * (master_ref[...] + partner_ref[...])
    totals = live_before(lengths_ref, members)
    before = chosen(totals[:-1], index)
    first, more = first_ref.shape[0], more_ref.shape[0]
    places = token_places(lengths_ref, index, before, block_ref.shape[0])
    pick = picking(places, 0, first + more)

    def store(here, rows):
        rows_ref[pl.ds(aligned(before), first + more), here] = rows

    block.picked(pick, store, True)
    far_start = aligned(chosen(totals[:-1], lax.rem(index + members - far, members)))
    far_copy.wait()
    rows_ref[pl.ds(far_start, first)] += first_ref[...]
    for member in range(members):
        start = aligned(totals[member])
        used = totals[member + 1] - start

        @pl.when((member != index) & (used > first))
        def _(member=member, start=start, used=used):
            copy = pltpu.make_async_copy(held_more[member], more_ref, more_sems.at[member])
            copy.start()
            copy.wait()
            for k in range(0, more, ALIGN):

                @pl.when(used > first + k)
                def _(k=k):
                    rows_ref[pl.ds(start + first + k, ALIGN)] += more_ref[k : k + ALIGN]

    height = (rows_ref.shape[0] - first - more) // members

    @pl.loop(0, members)
    def _(j):
        here = pl.ds(pl.multiple_of(j * height, ALIGN), height)
        keys_ref[here] = (
            jnp.dot(rows_ref[here], low_ref[...], preferred_element_type=jnp.float32) * scale
        )

    keys_ref[pl.ds(aligned(before), first + more)] -= jnp.dot(
        pick, targets_ref[...], preferred_element_type=jnp.float32
    )


def keys_kernel(members, near, scale, lengths_ref, low_ref, keys_ref, *refs):
    blocks, sums, total_ref = refs[: len(near)], refs[len(near) : -1], refs[-1]
    del keys_ref
    index = lax.axis_index("fsdp")
    totals = live_before(lengths_ref, members)
    for i, block_ref in zip(near, blocks):
        start = aligned(chosen(totals[:-1], lax.rem(index + members - i, members)))
        total_ref[pl.ds(start, block_ref.shape[0])] += (
            jnp.dot(block_ref[...], low_ref[...], preferred_element_type=jnp.float32) * scale
        )
    share, width = sums[0].shape
    for half in range(HALVES):
        for i in range(members):
            owner = lax.rem(index + i, members)
            rows = pl.ds(pl.multiple_of(owner * share, ALIGN), share)
            out_ref = sums[half * members + i]
            here = slice(half * width, (half + 1) * width)
            out_ref[...] = total_ref[rows, here].astype(out_ref.dtype)


def turn_kernel(members, near, lengths_ref, rows_ref, *refs):
    blocks, (turned_ref, all_ref) = refs[: len(near)], refs[len(near) :]
    index = lax.axis_index("fsdp")
    totals = live_before(lengths_ref, members)
    all_ref[...] = rows_ref[...]
    for i, block_ref in zip(near, blocks):
        start = aligned(chosen(totals[:-1], lax.rem(index + members - i, members)))
        all_ref[pl.ds(start, block_ref.shape[0])] += block_ref[...]
    for start in range(0, turned_ref.shape[1], 128):
        turned_ref[:, start : start + 128] = all_ref[start : start + 128, :].T


def gradient_kernel(members, turned_ref, *refs):
    residuals, (gradient_ref, low_ref, squares_ref, all_ref) = refs[:members], refs[members:]
    index = lax.axis_index("fsdp")
    share = residuals[0].shape[0]
    for i in range(members):
        owner = lax.rem(index + members - i, members)
        all_ref[pl.ds(pl.multiple_of(owner * share, ALIGN), share)] = residuals[i][...]
    squares_ref[...] = jnp.zeros_like(squares_ref)
    height = min(256, turned_ref.shape[0])

    @pl.loop(0, turned_ref.shape[0] // height)
    def _(j):
        rows = pl.ds(pl.multiple_of(j * height, height), height)
        gradient = jnp.dot(turned_ref[rows], all_ref[...], preferred_element_type=jnp.float32)
        gradient_ref[rows] = gradient
        low_ref[rows] = gradient.astype(low_ref.dtype)
        squares = jnp.sum((gradient * gradient).reshape(-1, 8, gradient.shape[1]), axis=0)
        lanes = squares.shape[1] // 128
        squares_ref[...] += sum(squares[:, 128 * k : 128 * (k + 1)] for k in range(lanes))


def average_kernel(entries, own_ref, other_ref, halves_ref, *refs):
    gradients, partners, (out_ref, done_ref, sems) = refs[:HALVES], refs[HALVES:-3], refs[-3:]
    rate = 0.5 * learning_rate
    own = rate * lax.rsqrt(jnp.sum(own_ref[...], keepdims=True) / entries + epsilon)
    other = rate * lax.rsqrt(jnp.sum(other_ref[...], keepdims=True) / entries + epsilon)
    pieces = sems.shape[0]
    height = done_ref.shape[0] // pieces
    width = done_ref.shape[1] // HALVES
    copies = []
    for j in range(pieces):
        rows = pl.ds(j * height, height)
        for half in range(HALVES):
            here = slice(half * width, (half + 1) * width)
            done_ref[rows, here] = (
                halves_ref[rows, here]
                - gradients[half][rows] * own
                - partners[half][rows].astype(jnp.float32) * other
            )
        copies.append(pltpu.make_async_copy(done_ref.at[rows], out_ref.at[rows], sems.at[j]))
        copies[-1].start()
    for copy in copies:
        copy.wait()


def more_rows(size, source, offsets, blocks):
    if size == 0:
        return blocks[0]
    members = lax.axis_size("fsdp")
    moved = [
        lax.ppermute(block[:size], "fsdp", [(source, (source + i) % members)])
        for i, block in zip(offsets, blocks)
    ]
    return jnp.pad(sum(moved[1:], moved[0]), ((0, blocks[0].shape[0] - size), (0, 0)))


def local(activations, targets, weights, lengths):
    features = activations[0]
    wanted = targets[0]
    master = weights[0]
    tokens_here = features.shape[0]
    local_rows, columns = master.shape
    members = lax.axis_size("fsdp")
    distance_bit = STEP % (lax.axis_size("replica").bit_length() - 1)
    share = tokens_here // 2
    first = -(-(share + 32) // ALIGN) * ALIGN
    more = -(-(tokens_here + ALIGN - first) // ALIGN) * ALIGN
    steps = (16, 32, 48, 64, 80, 96, 128) if members <= 4 else (96,)
    sizes = [0] + [size for size in steps if size < more] + [more]
    most = first + more
    scale = features.shape[1] ** (-0.5)
    places = members * share + most

    vmem = pl.BlockSpec(memory_space=pltpu.VMEM)
    anywhere = pl.BlockSpec(memory_space=pl.ANY)
    smem = pl.BlockSpec(memory_space=pltpu.SMEM)
    params = pltpu.CompilerParams(vmem_limit_bytes=40 * 2**20)
    large = pltpu.CompilerParams(vmem_limit_bytes=56 * 2**20)

    def array(rows, width, dtype):
        return jax.ShapeDtypeStruct((rows, width), dtype)

    def cost(flops, moved):
        return pl.CostEstimate(flops=flops, bytes_accessed=moved, transcendentals=0)

    def sent_to(offsets, choices):
        count = len(offsets)
        pieces = max(1, local_rows // 256)
        arrays = pl.pallas_call(
            functools.partial(sent_kernel, members, offsets, sizes),
            in_specs=[smem, anywhere],
            out_specs=[anywhere] * (2 * count) + [smem] * choices,
            out_shape=[
                array(rows, local_rows, jnp.bfloat16) for rows in (first, more) for _ in offsets
            ]
            + [jax.ShapeDtypeStruct((1,), jnp.int32)] * choices,
            scratch_shapes=[
                pltpu.VMEM((count, tokens_here, local_rows), jnp.bfloat16),
                pltpu.VMEM((count, first, local_rows), jnp.bfloat16),
                pltpu.VMEM((count, more, local_rows), jnp.bfloat16),
                pltpu.SemaphoreType.DMA((count, pieces)),
                pltpu.SemaphoreType.DMA((count, pieces)),
                pltpu.SemaphoreType.DMA((count,)),
            ],
            compiler_params=large,
            cost_estimate=cost(
                2 * count * first * tokens_here * local_rows,
                2 * count * (tokens_here + first) * local_rows,
            ),
        )(lengths, features)
        return arrays[:count], arrays[count : 2 * count], arrays[2 * count :]

    far = members // 2
    near = [i for i in range(1, members) if i != far]
    far_first, far_more, choice = sent_to([far], members)
    near_first, near_more, _ = sent_to(near, 0)
    held_far = turned(far_first[0], far)
    offsets = [far] + near
    held_more = [
        lax.switch(
            choice[source][0],
            [functools.partial(more_rows, size, source, offsets) for size in sizes],
            far_more + near_more,
        )
        for source in range(members)
    ]
    near_first, held_more, late_lengths = lax.optimization_barrier((near_first, held_more, lengths))
    held = [turned(block, i) for i, block in zip(near, near_first)]

    partner_master = swapped(master, "replica", distance_bit)
    rows, keys, low, halves = pl.pallas_call(
        functools.partial(own_kernel, members, far, scale),
        in_specs=[smem, anywhere, vmem, vmem, vmem, anywhere] + [anywhere] * members,
        out_specs=[vmem] * 4,
        out_shape=[
            array(places, local_rows, jnp.bfloat16),
            array(places, columns, jnp.float32),
            array(local_rows, columns, jnp.bfloat16),
            array(local_rows, columns, jnp.float32),
        ],
        scratch_shapes=[
            pltpu.VMEM((tokens_here, local_rows), jnp.bfloat16),
            pltpu.VMEM((first, local_rows), jnp.bfloat16),
            pltpu.VMEM((more, local_rows), jnp.bfloat16),
            pltpu.SemaphoreType.DMA((max(1, local_rows // 256),)),
            pltpu.SemaphoreType.DMA,
            pltpu.SemaphoreType.DMA((members,)),
        ],
        compiler_params=params,
        cost_estimate=cost(
            2 * (most * tokens_here + members * share * columns) * (local_rows + columns),
            20 * local_rows * columns,
        ),
    )(late_lengths, features, wanted, master, partner_master, held_far, *held_more)

    width = columns // HALVES
    sum_shapes = [array(share, width, jnp.bfloat16 if i else jnp.float32) for i in range(members)]
    *sums, _ = pl.pallas_call(
        functools.partial(keys_kernel, members, near, scale),
        in_specs=[smem, vmem, vmem] + [vmem] * len(near),
        out_specs=[vmem] * (HALVES * members + 1),
        out_shape=sum_shapes * HALVES + [array(places, columns, jnp.float32)],
        input_output_aliases={2: HALVES * members},
        compiler_params=params,
        cost_estimate=cost(
            2 * len(near) * first * local_rows * columns, 8 * places * columns
        ),
    )(lengths, low, keys, *held)
    sums = [sums[half * members : (half + 1) * members] for half in range(HALVES)]

    turned_rows = pl.pallas_call(
        functools.partial(turn_kernel, members, near),
        in_specs=[smem, vmem] + [vmem] * len(near),
        out_specs=vmem,
        out_shape=array(local_rows, members * share, jnp.bfloat16),
        scratch_shapes=[pltpu.VMEM((places, local_rows), jnp.bfloat16)],
        compiler_params=params,
        cost_estimate=cost(0, 4 * members * share * local_rows),
    )(lengths, rows, *held)

    gradients, partners, squares = [], [], 0.0
    for half in range(HALVES):
        residual = sums[half][0]
        for i in range(1, members):
            residual = residual + turned(sums[half][i], i).astype(jnp.float32)
        residual = residual.astype(jnp.bfloat16)
        residuals = [residual] + [turned(residual, i) for i in range(1, members)]
        gradient, low_gradient, own_squares = pl.pallas_call(
            functools.partial(gradient_kernel, members),
            in_specs=[vmem] + [vmem] * members,
            out_specs=[vmem] * 3,
            out_shape=[
                array(local_rows, width, jnp.float32),
                array(local_rows, width, jnp.bfloat16),
                array(8, 128, jnp.float32),
            ],
            scratch_shapes=[pltpu.VMEM((members * share, width), jnp.bfloat16)],
            compiler_params=params,
            cost_estimate=cost(
                2 * members * share * local_rows * width, 8 * local_rows * width
            ),
        )(turned_rows, *residuals)
        gradients.append(gradient)
        partners.append(swapped(low_gradient, "replica", distance_bit))
        squares = squares + own_squares

    total, partner_total = squares, 0.0
    for i in range(members):
        if i:
            total = total + turned(squares, i)
        partner_total = partner_total + sent_across(squares, distance_bit, i)

    averaged = pl.pallas_call(
        functools.partial(average_kernel, members * local_rows * columns),
        in_specs=[vmem] * (3 + 2 * HALVES),
        out_specs=anywhere,
        out_shape=array(local_rows, columns, jnp.float32),
        scratch_shapes=[
            pltpu.VMEM((local_rows, columns), jnp.float32),
            pltpu.SemaphoreType.DMA((4,)),
        ],
        compiler_params=params,
    )(total, partner_total, halves, *gradients, *partners)
    return averaged[None]


def solution(mesh):
    return jax.shard_map(
        local,
        mesh=mesh,
        in_specs=(
            P("replica", "fsdp", None),
            P("replica", "fsdp", None),
            P("replica", "fsdp", None),
            P("replica", None),
        ),
        out_specs=P("replica", "fsdp", None),
        check_vma=False,
    )
```

```python
import functools

import jax
import jax.numpy as jnp
from jax import lax
from jax.experimental import pallas as pl
from jax.experimental.pallas import tpu as pltpu
from jax.sharding import PartitionSpec as P

SLOT = 64
STEP = 3
ALIGN = 16
HALVES = 2

learning_rate = 0.1
epsilon = 1e-06


def swapped(value, axis, bit):
    mask = 2**bit
    pairs = [(source, source ^ mask) for source in range(lax.axis_size(axis))]
    return lax.ppermute(value, axis, pairs)


def turned(value, distance):
    members = lax.axis_size("fsdp")
    ring = [(source, (source + distance) % members) for source in range(members)]
    return lax.ppermute(value, "fsdp", ring)


def live_before(lengths_ref, members):
    sequences = lengths_ref.shape[1] // members
    totals = [jnp.int32(0)]
    for member in range(members):
        total = totals[-1]
        for q in range(sequences):
            total = total + lengths_ref[0, member * sequences + q]
        totals.append(total)
    return totals


def chosen(values, index):
    value = values[0]
    for i in range(1, len(values)):
        value = jnp.where(index == i, values[i], value)
    return value


def aligned(place):
    return pl.multiple_of(place // ALIGN * ALIGN, ALIGN)


def token_places(lengths_ref, member, before, tokens):
    sequences = tokens // SLOT
    place = before % ALIGN
    slot = lax.broadcasted_iota(jnp.int32, (1, tokens), 1)
    places = jnp.full((1, tokens), -1, jnp.int32)
    for s in range(sequences):
        length = lengths_ref[0, member * sequences + s]
        position = slot - s * SLOT
        places = jnp.where((position >= 0) & (position < length), position + place, places)
        place = place + length
    return places


def picking(places, start, rows):
    row = lax.broadcasted_iota(jnp.int32, (rows, places.shape[1]), 0) + start
    return jnp.where(row == places, 1.0, 0.0).astype(jnp.bfloat16)


def other_half(index):
    half = index // 2
    return [2 - half, 3 - 3 * half]


class Block:
    def __init__(self, features_ref, member, block_ref, sems):
        self.block_ref, self.width = block_ref, block_ref.shape[1] // sems.shape[0]
        start = member * block_ref.shape[1]
        self.copies = []
        for j in range(sems.shape[0]):
            there = pl.ds(pl.multiple_of(start + j * self.width, 128), self.width)
            here = pl.ds(j * self.width, self.width)
            copy = pltpu.make_async_copy(
                features_ref.at[:, there], block_ref.at[:, here], sems.at[j]
            )
            copy.start()
            self.copies.append(copy)

    def picked(self, pick, store, wait):
        for j, copy in enumerate(self.copies):
            if wait:
                copy.wait()
            here = slice(j * self.width, (j + 1) * self.width)
            rows = jnp.dot(pick, self.block_ref[:, here], preferred_element_type=jnp.float32)
            store(here, rows.astype(jnp.bfloat16))


def used_places(totals, first, sizes):
    choices = []
    for member in range(len(totals) - 1):
        used = totals[member + 1] - aligned(totals[member])
        choice = jnp.int32(0)
        for size in sizes[:-1]:
            choice = choice + jnp.where(used > first + size, 1, 0)
        choices.append(choice)
    return choices


def choice_bits(sizes):
    return (len(sizes) - 1).bit_length()


def sent_kernel(members, offsets, sizes, lengths_ref, features_ref, *refs):
    count = len(offsets)
    outs, choice_ref = refs[: 2 * count], refs[2 * count]
    block_ref, first_ref, more_ref, sems, out_sems, more_sems = refs[2 * count + 1 :]
    index = lax.axis_index("fsdp")
    blocks = [
        Block(features_ref, lax.rem(index + i, members), block_ref.at[n], sems.at[n])
        for n, i in enumerate(offsets)
    ]
    totals = live_before(lengths_ref, members)
    before, end = chosen(totals[:-1], index), chosen(totals[1:], index)
    places = token_places(lengths_ref, index, before, block_ref.shape[1])
    first, more = first_ref.shape[1], more_ref.shape[1]
    pick = picking(places, 0, first)
    copies = []
    for n, block in enumerate(blocks):

        def store(here, rows, n=n):
            first_ref[n, :, here] = rows
            copy = pltpu.make_async_copy(
                first_ref.at[n, :, here],
                outs[n].at[:, here],
                out_sems.at[n, here.start // (here.stop - here.start)],
            )
            copy.start()
            copies.append(copy)

        block.picked(pick, store, True)

    @pl.when(end - aligned(before) > first)
    def _():
        further = picking(places, first, more)
        for n, block in enumerate(blocks):

            def store(here, rows, n=n):
                more_ref[n, :, here] = rows

            block.picked(further, store, False)
            copy = pltpu.make_async_copy(more_ref.at[n], outs[count + n], more_sems.at[n])
            copy.start()
            copy.wait()

    packed = jnp.int32(0)
    for member, choice in enumerate(used_places(totals, first, sizes)):
        packed = packed | (choice << (member * choice_bits(sizes)))
    choice_ref[0] = packed
    for copy in copies:
        copy.wait()


def own_kernel(
    members,
    far,
    scale,
    lengths_ref,
    features_ref,
    targets_ref,
    master_ref,
    partner_ref,
    far_ref,
    *refs,
):
    held_more = refs[:members]
    rows_ref, keys_ref, low_ref, halves_ref = refs[members : members + 4]
    block_ref, first_ref, more_ref, sems, first_sem, more_sems = refs[members + 4 :]
    index = lax.axis_index("fsdp")
    block = Block(features_ref, index, block_ref, sems)
    far_copy = pltpu.make_async_copy(far_ref, first_ref, first_sem)
    far_copy.start()
    rows_ref[...] = jnp.zeros_like(rows_ref)
    low_ref[...] = master_ref[...].astype(jnp.bfloat16)
    halves_ref[...] = 0.5 * (master_ref[...] + partner_ref[...])
    totals = live_before(lengths_ref, members)
    before = chosen(totals[:-1], index)
    first, more = first_ref.shape[0], more_ref.shape[0]
    places = token_places(lengths_ref, index, before, block_ref.shape[0])
    pick = picking(places, 0, first + more)

    def store(here, rows):
        rows_ref[pl.ds(aligned(before), first + more), here] = rows

    block.picked(pick, store, True)
    far_start = aligned(chosen(totals[:-1], lax.rem(index + members - far, members)))
    far_copy.wait()
    rows_ref[pl.ds(far_start, first)] += first_ref[...]
    for member in range(members):
        start = aligned(totals[member])
        used = totals[member + 1] - start

        @pl.when((member != index) & (used > first))
        def _(member=member, start=start, used=used):
            copy = pltpu.make_async_copy(held_more[member], more_ref, more_sems.at[member])
            copy.start()
            copy.wait()
            for k in range(0, more, ALIGN):

                @pl.when(used > first + k)
                def _(k=k):
                    rows_ref[pl.ds(start + first + k, ALIGN)] += more_ref[k : k + ALIGN]

    height = (rows_ref.shape[0] - first - more) // members

    @pl.loop(0, members)
    def _(j):
        here = pl.ds(pl.multiple_of(j * height, ALIGN), height)
        keys_ref[here] = (
            jnp.dot(rows_ref[here], low_ref[...], preferred_element_type=jnp.float32) * scale
        )

    keys_ref[pl.ds(aligned(before), first + more)] -= jnp.dot(
        pick, targets_ref[...], preferred_element_type=jnp.float32
    )


def keys_kernel(members, near, scale, lengths_ref, low_ref, keys_ref, *refs):
    blocks, sums, total_ref = refs[: len(near)], refs[len(near) : -1], refs[-1]
    del keys_ref
    index = lax.axis_index("fsdp")
    totals = live_before(lengths_ref, members)
    for i, block_ref in zip(near, blocks):
        start = aligned(chosen(totals[:-1], lax.rem(index + members - i, members)))
        total_ref[pl.ds(start, block_ref.shape[0])] += (
            jnp.dot(block_ref[...], low_ref[...], preferred_element_type=jnp.float32) * scale
        )
    share, width = sums[0].shape
    for half in range(HALVES):
        for i in range(members):
            owner = lax.rem(index + i, members)
            rows = pl.ds(pl.multiple_of(owner * share, ALIGN), share)
            out_ref = sums[half * members + i]
            here = slice(half * width, (half + 1) * width)
            out_ref[...] = total_ref[rows, here].astype(out_ref.dtype)


def turn_kernel(members, near, lengths_ref, rows_ref, *refs):
    blocks, (turned_ref, all_ref) = refs[: len(near)], refs[len(near) :]
    index = lax.axis_index("fsdp")
    totals = live_before(lengths_ref, members)
    all_ref[...] = rows_ref[...]
    for i, block_ref in zip(near, blocks):
        start = aligned(chosen(totals[:-1], lax.rem(index + members - i, members)))
        all_ref[pl.ds(start, block_ref.shape[0])] += block_ref[...]
    for start in range(0, turned_ref.shape[1], 128):
        turned_ref[:, start : start + 128] = all_ref[start : start + 128, :].T


def gradient_kernel(members, turned_ref, *refs):
    residuals, (gradient_ref, low_ref, squares_ref, all_ref) = refs[:-4], refs[-4:]
    index = lax.axis_index("fsdp")
    share = residuals[0].shape[0]

    def put(owner, block):
        all_ref[pl.ds(pl.multiple_of(owner * share, ALIGN), share)] = block

    if len(residuals) > members:
        own_ref, left_ref, right_ref, two_ref, pair_ref = residuals
        inner, outer = other_half(index)
        put(index, own_ref[...])
        pl.when(index > 0)(lambda: put(index - 1, left_ref[...]))
        pl.when(index < 3)(lambda: put(index + 1, right_ref[...]))

        @pl.when((index == 1) | (index == 2))
        def _():
            put(outer, two_ref[...])

        @pl.when((index == 0) | (index == 3))
        def _():
            put(inner, pair_ref[:share])
            put(outer, pair_ref[share:])
    else:
        for i in range(members):
            put(lax.rem(index + members - i, members), residuals[i][...])
    squares_ref[...] = jnp.zeros_like(squares_ref)
    height = min(256, turned_ref.shape[0])

    @pl.loop(0, turned_ref.shape[0] // height)
    def _(j):
        rows = pl.ds(pl.multiple_of(j * height, height), height)
        gradient = jnp.dot(turned_ref[rows], all_ref[...], preferred_element_type=jnp.float32)
        gradient_ref[rows] = gradient
        low_ref[rows] = gradient.astype(low_ref.dtype)
        squares = jnp.sum((gradient * gradient).reshape(-1, 8, gradient.shape[1]), axis=0)
        lanes = squares.shape[1] // 128
        squares_ref[...] += sum(squares[:, 128 * k : 128 * (k + 1)] for k in range(lanes))


def average_kernel(entries, own_ref, other_ref, halves_ref, *refs):
    gradients, partners, (out_ref, done_ref, sems) = refs[:HALVES], refs[HALVES:-3], refs[-3:]
    rate = 0.5 * learning_rate
    own = rate * lax.rsqrt(jnp.sum(own_ref[...], keepdims=True) / entries + epsilon)
    other = rate * lax.rsqrt(jnp.sum(other_ref[...], keepdims=True) / entries + epsilon)
    pieces = sems.shape[0]
    height = done_ref.shape[0] // pieces
    width = done_ref.shape[1] // HALVES
    copies = []
    for j in range(pieces):
        rows = pl.ds(j * height, height)
        for half in range(HALVES):
            here = slice(half * width, (half + 1) * width)
            done_ref[rows, here] = (
                halves_ref[rows, here]
                - gradients[half][rows] * own
                - partners[half][rows].astype(jnp.float32) * other
            )
        copies.append(pltpu.make_async_copy(done_ref.at[rows], out_ref.at[rows], sems.at[j]))
        copies[-1].start()
    for copy in copies:
        copy.wait()


def more_rows(size, source, offsets, blocks):
    if size == 0:
        return blocks[0]
    members = lax.axis_size("fsdp")
    moved = [
        lax.ppermute(block[:size], "fsdp", [(source, (source + i) % members)])
        for i, block in zip(offsets, blocks)
    ]
    return jnp.pad(sum(moved[1:], moved[0]), ((0, blocks[0].shape[0] - size), (0, 0)))


def sent_along(value, *pairs):
    return lax.ppermute(value, "fsdp", pairs)


def all_residuals(residual, last):
    members = lax.axis_size("fsdp")
    if members == 4 and not last:
        left = sent_along(residual, (0, 1), (1, 2), (2, 3))
        right = sent_along(residual, (1, 0), (2, 1), (3, 2))
        two = sent_along(residual, (0, 2), (3, 1))
        inner = jnp.where(lax.axis_index("fsdp") < 2, right, left)
        pair = sent_along(jnp.concatenate([inner, two]), (1, 0), (2, 3))
        return [residual, left, right, two, pair]
    return [residual] + [turned(residual, i) for i in range(1, members)]


def local(activations, targets, weights, lengths):
    features = activations[0]
    wanted = targets[0]
    master = weights[0]
    tokens_here = features.shape[0]
    local_rows, columns = master.shape
    members = lax.axis_size("fsdp")
    distance_bit = STEP % (lax.axis_size("replica").bit_length() - 1)
    share = tokens_here // 2
    first = -(-(share + 32) // ALIGN) * ALIGN
    more = -(-(tokens_here + ALIGN - first) // ALIGN) * ALIGN
    steps = (16, 32, 48, 64, 80, 96, 128) if members <= 4 else (96,)
    sizes = [0] + [size for size in steps if size < more] + [more]
    most = first + more
    scale = features.shape[1] ** (-0.5)
    places = members * share + most

    vmem = pl.BlockSpec(memory_space=pltpu.VMEM)
    anywhere = pl.BlockSpec(memory_space=pl.ANY)
    smem = pl.BlockSpec(memory_space=pltpu.SMEM)
    params = pltpu.CompilerParams(vmem_limit_bytes=40 * 2**20)
    large = pltpu.CompilerParams(vmem_limit_bytes=56 * 2**20)

    def array(rows, width, dtype):
        return jax.ShapeDtypeStruct((rows, width), dtype)

    def cost(flops, moved):
        return pl.CostEstimate(flops=flops, bytes_accessed=moved, transcendentals=0)

    def sent_to(offsets):
        count = len(offsets)
        pieces = max(1, local_rows // 256)
        *arrays, choice = pl.pallas_call(
            functools.partial(sent_kernel, members, offsets, sizes),
            in_specs=[smem, anywhere],
            out_specs=[anywhere] * (2 * count) + [smem],
            out_shape=[
                array(rows, local_rows, jnp.bfloat16) for rows in (first, more) for _ in offsets
            ]
            + [jax.ShapeDtypeStruct((1,), jnp.int32)],
            scratch_shapes=[
                pltpu.VMEM((count, tokens_here, local_rows), jnp.bfloat16),
                pltpu.VMEM((count, first, local_rows), jnp.bfloat16),
                pltpu.VMEM((count, more, local_rows), jnp.bfloat16),
                pltpu.SemaphoreType.DMA((count, pieces)),
                pltpu.SemaphoreType.DMA((count, pieces)),
                pltpu.SemaphoreType.DMA((count,)),
            ],
            compiler_params=large,
            cost_estimate=cost(
                2 * count * first * tokens_here * local_rows,
                2 * count * (tokens_here + first) * local_rows,
            ),
        )(lengths, features)
        return arrays[:count], arrays[count:], choice

    far = members // 2
    near = [i for i in range(1, members) if i != far]
    far_first, far_more, choice = sent_to([far])
    near_first, near_more, _ = sent_to(near)
    held_far = turned(far_first[0], far)
    offsets = [far] + near
    bits = choice_bits(sizes)
    held_more = [
        lax.switch(
            lax.shift_right_logical(choice[0], jnp.int32(source * bits)) & (2**bits - 1),
            [functools.partial(more_rows, size, source, offsets) for size in sizes],
            far_more + near_more,
        )
        for source in range(members)
    ]
    near_first, held_more, late_lengths = lax.optimization_barrier((near_first, held_more, lengths))
    held = [turned(block, i) for i, block in zip(near, near_first)]

    partner_master = swapped(master, "replica", distance_bit)
    rows, keys, low, halves = pl.pallas_call(
        functools.partial(own_kernel, members, far, scale),
        in_specs=[smem, anywhere, vmem, vmem, vmem, anywhere] + [anywhere] * members,
        out_specs=[vmem] * 4,
        out_shape=[
            array(places, local_rows, jnp.bfloat16),
            array(places, columns, jnp.float32),
            array(local_rows, columns, jnp.bfloat16),
            array(local_rows, columns, jnp.float32),
        ],
        scratch_shapes=[
            pltpu.VMEM((tokens_here, local_rows), jnp.bfloat16),
            pltpu.VMEM((first, local_rows), jnp.bfloat16),
            pltpu.VMEM((more, local_rows), jnp.bfloat16),
            pltpu.SemaphoreType.DMA((max(1, local_rows // 256),)),
            pltpu.SemaphoreType.DMA,
            pltpu.SemaphoreType.DMA((members,)),
        ],
        compiler_params=params,
        cost_estimate=cost(
            2 * (most * tokens_here + members * share * columns) * (local_rows + columns),
            20 * local_rows * columns,
        ),
    )(late_lengths, features, wanted, master, partner_master, held_far, *held_more)

    width = columns // HALVES
    sum_shapes = [array(share, width, jnp.bfloat16 if i else jnp.float32) for i in range(members)]
    *sums, _ = pl.pallas_call(
        functools.partial(keys_kernel, members, near, scale),
        in_specs=[smem, vmem, vmem] + [vmem] * len(near),
        out_specs=[vmem] * (HALVES * members + 1),
        out_shape=sum_shapes * HALVES + [array(places, columns, jnp.float32)],
        input_output_aliases={2: HALVES * members},
        compiler_params=params,
        cost_estimate=cost(
            2 * len(near) * first * local_rows * columns, 8 * places * columns
        ),
    )(lengths, low, keys, *held)
    sums = [sums[half * members : (half + 1) * members] for half in range(HALVES)]

    turned_rows = pl.pallas_call(
        functools.partial(turn_kernel, members, near),
        in_specs=[smem, vmem] + [vmem] * len(near),
        out_specs=vmem,
        out_shape=array(local_rows, members * share, jnp.bfloat16),
        scratch_shapes=[pltpu.VMEM((places, local_rows), jnp.bfloat16)],
        compiler_params=params,
        cost_estimate=cost(0, 4 * members * share * local_rows),
    )(lengths, rows, *held)

    gradients, partners, squares = [], [], 0.0
    for half in range(HALVES):
        residual = sums[half][0]
        for i in range(1, members):
            residual = residual + turned(sums[half][i], i).astype(jnp.float32)
        residual = residual.astype(jnp.bfloat16)
        residuals = all_residuals(residual, half == HALVES - 1)
        gradient, low_gradient, own_squares = pl.pallas_call(
            functools.partial(gradient_kernel, members),
            in_specs=[vmem] * (1 + len(residuals)),
            out_specs=[vmem] * 3,
            out_shape=[
                array(local_rows, width, jnp.float32),
                array(local_rows, width, jnp.bfloat16),
                array(8, 128, jnp.float32),
            ],
            scratch_shapes=[pltpu.VMEM((members * share, width), jnp.bfloat16)],
            compiler_params=params,
            cost_estimate=cost(
                2 * members * share * local_rows * width, 8 * local_rows * width
            ),
        )(turned_rows, *residuals)
        gradients.append(gradient)
        partners.append(swapped(low_gradient, "replica", distance_bit))
        squares = squares + own_squares

    total = squares
    for i in range(1, members):
        total = total + turned(squares, i)
    partner_total = swapped(total, "replica", distance_bit)

    averaged = pl.pallas_call(
        functools.partial(average_kernel, members * local_rows * columns),
        in_specs=[vmem] * (3 + 2 * HALVES),
        out_specs=anywhere,
        out_shape=array(local_rows, columns, jnp.float32),
        scratch_shapes=[
            pltpu.VMEM((local_rows, columns), jnp.float32),
            pltpu.SemaphoreType.DMA((4,)),
        ],
        compiler_params=params,
    )(total, partner_total, halves, *gradients, *partners)
    return averaged[None]


def solution(mesh):
    return jax.shard_map(
        local,
        mesh=mesh,
        in_specs=(
            P("replica", "fsdp", None),
            P("replica", "fsdp", None),
            P("replica", "fsdp", None),
            P("replica", None),
        ),
        out_specs=P("replica", "fsdp", None),
        check_vma=False,
    )
```

```python
import functools

import jax
import jax.numpy as jnp
from jax import lax
from jax.experimental import pallas as pl
from jax.experimental.pallas import tpu as pltpu
from jax.sharding import PartitionSpec as P

SLOT = 64
STEP = 3
ALIGN = 16
HALVES = 2

learning_rate = 0.1
epsilon = 1e-06


def swapped(value, axis, bit):
    mask = 2**bit
    pairs = [(source, source ^ mask) for source in range(lax.axis_size(axis))]
    return lax.ppermute(value, axis, pairs)


def turned(value, distance):
    members = lax.axis_size("fsdp")
    ring = [(source, (source + distance) % members) for source in range(members)]
    return lax.ppermute(value, "fsdp", ring)


def live_before(lengths_ref, members):
    sequences = lengths_ref.shape[1] // members
    totals = [jnp.int32(0)]
    for member in range(members):
        total = totals[-1]
        for q in range(sequences):
            total = total + lengths_ref[0, member * sequences + q]
        totals.append(total)
    return totals


def chosen(values, index):
    value = values[0]
    for i in range(1, len(values)):
        value = jnp.where(index == i, values[i], value)
    return value


def aligned(place):
    return pl.multiple_of(place // ALIGN * ALIGN, ALIGN)


def token_places(lengths_ref, member, before, tokens):
    sequences = tokens // SLOT
    place = before % ALIGN
    slot = lax.broadcasted_iota(jnp.int32, (1, tokens), 1)
    places = jnp.full((1, tokens), -1, jnp.int32)
    for s in range(sequences):
        length = lengths_ref[0, member * sequences + s]
        position = slot - s * SLOT
        places = jnp.where((position >= 0) & (position < length), position + place, places)
        place = place + length
    return places


def picking(places, start, rows):
    row = lax.broadcasted_iota(jnp.int32, (rows, places.shape[1]), 0) + start
    return jnp.where(row == places, 1.0, 0.0).astype(jnp.bfloat16)


class Block:
    def __init__(self, features_ref, member, block_ref, sems):
        self.block_ref, self.width = block_ref, block_ref.shape[1] // sems.shape[0]
        start = member * block_ref.shape[1]
        self.copies = []
        for j in range(sems.shape[0]):
            there = pl.ds(pl.multiple_of(start + j * self.width, 128), self.width)
            here = pl.ds(j * self.width, self.width)
            copy = pltpu.make_async_copy(
                features_ref.at[:, there], block_ref.at[:, here], sems.at[j]
            )
            copy.start()
            self.copies.append(copy)

    def picked(self, pick, store, wait):
        for j, copy in enumerate(self.copies):
            if wait:
                copy.wait()
            here = slice(j * self.width, (j + 1) * self.width)
            rows = jnp.dot(pick, self.block_ref[:, here], preferred_element_type=jnp.float32)
            store(here, rows.astype(jnp.bfloat16))


def used_places(totals, first, sizes):
    choices = []
    for member in range(len(totals) - 1):
        used = totals[member + 1] - aligned(totals[member])
        choice = jnp.int32(0)
        for size in sizes[:-1]:
            choice = choice + jnp.where(used > first + size, 1, 0)
        choices.append(choice)
    return choices


def choice_bits(sizes):
    return (len(sizes) - 1).bit_length()


def sent_kernel(members, offsets, sizes, lengths_ref, features_ref, *refs):
    count = len(offsets)
    outs, choice_ref = refs[: 2 * count], refs[2 * count]
    block_ref, first_ref, more_ref, sems, out_sems, more_sems = refs[2 * count + 1 :]
    index = lax.axis_index("fsdp")
    blocks = [
        Block(features_ref, lax.rem(index + i, members), block_ref.at[n], sems.at[n])
        for n, i in enumerate(offsets)
    ]
    totals = live_before(lengths_ref, members)
    before, end = chosen(totals[:-1], index), chosen(totals[1:], index)
    places = token_places(lengths_ref, index, before, block_ref.shape[1])
    first, more = first_ref.shape[1], more_ref.shape[1]
    pick = picking(places, 0, first)
    copies = []
    for n, block in enumerate(blocks):

        def store(here, rows, n=n):
            first_ref[n, :, here] = rows
            copy = pltpu.make_async_copy(
                first_ref.at[n, :, here],
                outs[n].at[:, here],
                out_sems.at[n, here.start // (here.stop - here.start)],
            )
            copy.start()
            copies.append(copy)

        block.picked(pick, store, True)

    @pl.when(end - aligned(before) > first)
    def _():
        further = picking(places, first, more)
        for n, block in enumerate(blocks):

            def store(here, rows, n=n):
                more_ref[n, :, here] = rows

            block.picked(further, store, False)
            copy = pltpu.make_async_copy(more_ref.at[n], outs[count + n], more_sems.at[n])
            copy.start()
            copy.wait()

    packed = jnp.int32(0)
    for member, choice in enumerate(used_places(totals, first, sizes)):
        packed = packed | (choice << (member * choice_bits(sizes)))
    choice_ref[0] = packed
    for copy in copies:
        copy.wait()


def own_kernel(
    members,
    far,
    scale,
    lengths_ref,
    features_ref,
    targets_ref,
    master_ref,
    partner_ref,
    far_ref,
    *refs,
):
    held_more = refs[:members]
    rows_ref, keys_ref, low_ref, halves_ref = refs[members : members + 4]
    block_ref, first_ref, more_ref, sems, first_sem, more_sems = refs[members + 4 :]
    index = lax.axis_index("fsdp")
    block = Block(features_ref, index, block_ref, sems)
    far_copy = pltpu.make_async_copy(far_ref, first_ref, first_sem)
    far_copy.start()
    rows_ref[...] = jnp.zeros_like(rows_ref)
    low_ref[...] = master_ref[...].astype(jnp.bfloat16)
    halves_ref[...] = 0.5 * (master_ref[...] + partner_ref[...])
    totals = live_before(lengths_ref, members)
    before = chosen(totals[:-1], index)
    first, more = first_ref.shape[0], more_ref.shape[0]
    places = token_places(lengths_ref, index, before, block_ref.shape[0])
    pick = picking(places, 0, first + more)

    def store(here, rows):
        rows_ref[pl.ds(aligned(before), first + more), here] = rows

    block.picked(pick, store, True)
    far_start = aligned(chosen(totals[:-1], lax.rem(index + members - far, members)))
    far_copy.wait()
    rows_ref[pl.ds(far_start, first)] += first_ref[...]
    for member in range(members):
        start = aligned(totals[member])
        used = totals[member + 1] - start

        @pl.when((member != index) & (used > first))
        def _(member=member, start=start, used=used):
            copy = pltpu.make_async_copy(held_more[member], more_ref, more_sems.at[member])
            copy.start()
            copy.wait()
            for k in range(0, more, ALIGN):

                @pl.when(used > first + k)
                def _(k=k):
                    rows_ref[pl.ds(start + first + k, ALIGN)] += more_ref[k : k + ALIGN]

    height = (rows_ref.shape[0] - first - more) // members

    @pl.loop(0, members)
    def _(j):
        here = pl.ds(pl.multiple_of(j * height, ALIGN), height)
        keys_ref[here] = (
            jnp.dot(rows_ref[here], low_ref[...], preferred_element_type=jnp.float32) * scale
        )

    keys_ref[pl.ds(aligned(before), first + more)] -= jnp.dot(
        pick, targets_ref[...], preferred_element_type=jnp.float32
    )


def keys_kernel(members, near, scale, lengths_ref, low_ref, keys_ref, *refs):
    blocks, sums, total_ref = refs[: len(near)], refs[len(near) : -1], refs[-1]
    del keys_ref
    index = lax.axis_index("fsdp")
    totals = live_before(lengths_ref, members)
    for i, block_ref in zip(near, blocks):
        start = aligned(chosen(totals[:-1], lax.rem(index + members - i, members)))
        total_ref[pl.ds(start, block_ref.shape[0])] += (
            jnp.dot(block_ref[...], low_ref[...], preferred_element_type=jnp.float32) * scale
        )
    share, width = sums[0].shape
    for half in range(HALVES):
        for i in range(members):
            owner = lax.rem(index + i, members)
            rows = pl.ds(pl.multiple_of(owner * share, ALIGN), share)
            out_ref = sums[half * members + i]
            here = slice(half * width, (half + 1) * width)
            out_ref[...] = total_ref[rows, here].astype(out_ref.dtype)


def turn_kernel(members, near, lengths_ref, rows_ref, *refs):
    blocks, (turned_ref, all_ref) = refs[: len(near)], refs[len(near) :]
    index = lax.axis_index("fsdp")
    totals = live_before(lengths_ref, members)
    all_ref[...] = rows_ref[...]
    for i, block_ref in zip(near, blocks):
        start = aligned(chosen(totals[:-1], lax.rem(index + members - i, members)))
        all_ref[pl.ds(start, block_ref.shape[0])] += block_ref[...]
    for start in range(0, turned_ref.shape[1], 128):
        turned_ref[:, start : start + 128] = all_ref[start : start + 128, :].T


def gradient_kernel(members, turned_ref, *refs):
    residuals, (gradient_ref, low_ref, squares_ref, all_ref) = refs[:members], refs[members:]
    index = lax.axis_index("fsdp")
    share = residuals[0].shape[0]
    for i in range(members):
        owner = lax.rem(index + members - i, members)
        all_ref[pl.ds(pl.multiple_of(owner * share, ALIGN), share)] = residuals[i][...]
    squares_ref[...] = jnp.zeros_like(squares_ref)
    height = min(256, turned_ref.shape[0])

    @pl.loop(0, turned_ref.shape[0] // height)
    def _(j):
        rows = pl.ds(pl.multiple_of(j * height, height), height)
        gradient = jnp.dot(turned_ref[rows], all_ref[...], preferred_element_type=jnp.float32)
        gradient_ref[rows] = gradient
        low_ref[rows] = gradient.astype(low_ref.dtype)
        squares = jnp.sum((gradient * gradient).reshape(-1, 8, gradient.shape[1]), axis=0)
        lanes = squares.shape[1] // 128
        squares_ref[...] += sum(squares[:, 128 * k : 128 * (k + 1)] for k in range(lanes))


def average_kernel(entries, own_ref, other_ref, halves_ref, *refs):
    gradients, partners, (out_ref, done_ref, sems) = refs[:HALVES], refs[HALVES:-3], refs[-3:]
    rate = 0.5 * learning_rate
    own = rate * lax.rsqrt(jnp.sum(own_ref[...], keepdims=True) / entries + epsilon)
    other = rate * lax.rsqrt(jnp.sum(other_ref[...], keepdims=True) / entries + epsilon)
    pieces = sems.shape[0]
    height = done_ref.shape[0] // pieces
    width = done_ref.shape[1] // HALVES
    copies = []
    for j in range(pieces):
        rows = pl.ds(j * height, height)
        for half in range(HALVES):
            here = slice(half * width, (half + 1) * width)
            done_ref[rows, here] = (
                halves_ref[rows, here]
                - gradients[half][rows] * own
                - partners[half][rows].astype(jnp.float32) * other
            )
        copies.append(pltpu.make_async_copy(done_ref.at[rows], out_ref.at[rows], sems.at[j]))
        copies[-1].start()
    for copy in copies:
        copy.wait()


def more_rows(size, source, offsets, blocks):
    if size == 0:
        return blocks[0]
    members = lax.axis_size("fsdp")
    moved = [
        lax.ppermute(block[:size], "fsdp", [(source, (source + i) % members)])
        for i, block in zip(offsets, blocks)
    ]
    return jnp.pad(sum(moved[1:], moved[0]), ((0, blocks[0].shape[0] - size), (0, 0)))


def local(activations, targets, weights, lengths):
    features = activations[0]
    wanted = targets[0]
    master = weights[0]
    tokens_here = features.shape[0]
    local_rows, columns = master.shape
    members = lax.axis_size("fsdp")
    distance_bit = STEP % (lax.axis_size("replica").bit_length() - 1)
    share = tokens_here // 2
    first = -(-(share + 32) // ALIGN) * ALIGN
    more = -(-(tokens_here + ALIGN - first) // ALIGN) * ALIGN
    steps = (16, 32, 48, 64, 80, 96, 128) if members <= 4 else (96,)
    sizes = [0] + [size for size in steps if size < more] + [more]
    most = first + more
    scale = features.shape[1] ** (-0.5)
    places = members * share + most

    vmem = pl.BlockSpec(memory_space=pltpu.VMEM)
    anywhere = pl.BlockSpec(memory_space=pl.ANY)
    smem = pl.BlockSpec(memory_space=pltpu.SMEM)
    params = pltpu.CompilerParams(vmem_limit_bytes=16 * 2**20)
    middle = pltpu.CompilerParams(vmem_limit_bytes=24 * 2**20)
    large = pltpu.CompilerParams(vmem_limit_bytes=56 * 2**20)

    def array(rows, width, dtype):
        return jax.ShapeDtypeStruct((rows, width), dtype)

    def cost(flops, moved):
        return pl.CostEstimate(flops=flops, bytes_accessed=moved, transcendentals=0)

    def sent_to(offsets):
        count = len(offsets)
        pieces = max(1, local_rows // 256)
        *arrays, choice = pl.pallas_call(
            functools.partial(sent_kernel, members, offsets, sizes),
            in_specs=[smem, anywhere],
            out_specs=[anywhere] * (2 * count) + [smem],
            out_shape=[
                array(rows, local_rows, jnp.bfloat16) for rows in (first, more) for _ in offsets
            ]
            + [jax.ShapeDtypeStruct((1,), jnp.int32)],
            scratch_shapes=[
                pltpu.VMEM((count, tokens_here, local_rows), jnp.bfloat16),
                pltpu.VMEM((count, first, local_rows), jnp.bfloat16),
                pltpu.VMEM((count, more, local_rows), jnp.bfloat16),
                pltpu.SemaphoreType.DMA((count, pieces)),
                pltpu.SemaphoreType.DMA((count, pieces)),
                pltpu.SemaphoreType.DMA((count,)),
            ],
            compiler_params=large,
            cost_estimate=cost(
                2 * count * first * tokens_here * local_rows,
                2 * count * (tokens_here + first) * local_rows,
            ),
        )(lengths, features)
        return arrays[:count], arrays[count:], choice

    far = members // 2
    near = [i for i in range(1, members) if i != far]
    far_first, far_more, choice = sent_to([far])
    near_first, near_more, _ = sent_to(near)
    held_far = turned(far_first[0], far)
    offsets = [far] + near
    bits = choice_bits(sizes)
    held_more = [
        lax.switch(
            lax.shift_right_logical(choice[0], jnp.int32(source * bits)) & (2**bits - 1),
            [functools.partial(more_rows, size, source, offsets) for size in sizes],
            far_more + near_more,
        )
        for source in range(members)
    ]
    near_first, held_more, late_lengths = lax.optimization_barrier((near_first, held_more, lengths))
    held = [turned(block, i) for i, block in zip(near, near_first)]

    partner_master = swapped(master, "replica", distance_bit)
    rows, keys, low, halves = pl.pallas_call(
        functools.partial(own_kernel, members, far, scale),
        in_specs=[smem, anywhere, vmem, vmem, vmem, anywhere] + [anywhere] * members,
        out_specs=[vmem] * 4,
        out_shape=[
            array(places, local_rows, jnp.bfloat16),
            array(places, columns, jnp.float32),
            array(local_rows, columns, jnp.bfloat16),
            array(local_rows, columns, jnp.float32),
        ],
        scratch_shapes=[
            pltpu.VMEM((tokens_here, local_rows), jnp.bfloat16),
            pltpu.VMEM((first, local_rows), jnp.bfloat16),
            pltpu.VMEM((more, local_rows), jnp.bfloat16),
            pltpu.SemaphoreType.DMA((max(1, local_rows // 256),)),
            pltpu.SemaphoreType.DMA,
            pltpu.SemaphoreType.DMA((members,)),
        ],
        compiler_params=middle,
        cost_estimate=cost(
            2 * (most * tokens_here + members * share * columns) * (local_rows + columns),
            20 * local_rows * columns,
        ),
    )(late_lengths, features, wanted, master, partner_master, held_far, *held_more)

    width = columns // HALVES
    sum_shapes = [array(share, width, jnp.bfloat16 if i else jnp.float32) for i in range(members)]
    *sums, _ = pl.pallas_call(
        functools.partial(keys_kernel, members, near, scale),
        in_specs=[smem, vmem, vmem] + [vmem] * len(near),
        out_specs=[vmem] * (HALVES * members + 1),
        out_shape=sum_shapes * HALVES + [array(places, columns, jnp.float32)],
        input_output_aliases={2: HALVES * members},
        compiler_params=params,
        cost_estimate=cost(
            2 * len(near) * first * local_rows * columns, 8 * places * columns
        ),
    )(lengths, low, keys, *held)
    sums = [sums[half * members : (half + 1) * members] for half in range(HALVES)]

    turned_rows = pl.pallas_call(
        functools.partial(turn_kernel, members, near),
        in_specs=[smem, vmem] + [vmem] * len(near),
        out_specs=vmem,
        out_shape=array(local_rows, members * share, jnp.bfloat16),
        scratch_shapes=[pltpu.VMEM((places, local_rows), jnp.bfloat16)],
        compiler_params=params,
        cost_estimate=cost(0, 4 * members * share * local_rows),
    )(lengths, rows, *held)

    gradients, partners, squares = [], [], 0.0
    for half in range(HALVES):
        residual = sums[half][0]
        for i in range(1, members):
            residual = residual + turned(sums[half][i], i).astype(jnp.float32)
        residual = residual.astype(jnp.bfloat16)
        residuals = [residual] + [turned(residual, i) for i in range(1, members)]
        gradient, low_gradient, own_squares = pl.pallas_call(
            functools.partial(gradient_kernel, members),
            in_specs=[vmem] + [vmem] * members,
            out_specs=[vmem] * 3,
            out_shape=[
                array(local_rows, width, jnp.float32),
                array(local_rows, width, jnp.bfloat16),
                array(8, 128, jnp.float32),
            ],
            scratch_shapes=[pltpu.VMEM((members * share, width), jnp.bfloat16)],
            compiler_params=params,
            cost_estimate=cost(
                2 * members * share * local_rows * width, 8 * local_rows * width
            ),
        )(turned_rows, *residuals)
        gradients.append(gradient)
        partners.append(swapped(low_gradient, "replica", distance_bit))
        squares = squares + own_squares

    total = squares
    for i in range(1, members):
        total = total + turned(squares, i)
    partner_total = swapped(total, "replica", distance_bit)

    averaged = pl.pallas_call(
        functools.partial(average_kernel, members * local_rows * columns),
        in_specs=[vmem] * (3 + 2 * HALVES),
        out_specs=anywhere,
        out_shape=array(local_rows, columns, jnp.float32),
        scratch_shapes=[
            pltpu.VMEM((local_rows, columns), jnp.float32),
            pltpu.SemaphoreType.DMA((4,)),
        ],
        compiler_params=params,
    )(total, partner_total, halves, *gradients, *partners)
    return averaged[None]


def solution(mesh):
    return jax.shard_map(
        local,
        mesh=mesh,
        in_specs=(
            P("replica", "fsdp", None),
            P("replica", "fsdp", None),
            P("replica", "fsdp", None),
            P("replica", None),
        ),
        out_specs=P("replica", "fsdp", None),
        check_vma=False,
    )
```

```python
import functools

import jax
import jax.numpy as jnp
from jax import lax
from jax.experimental import pallas as pl
from jax.experimental.pallas import tpu as pltpu
from jax.sharding import PartitionSpec as P

SLOT = 64
STEP = 3
ALIGN = 16
HALVES = 2

learning_rate = 0.1
epsilon = 1e-06


def swapped(value, axis, bit):
    mask = 2**bit
    pairs = [(source, source ^ mask) for source in range(lax.axis_size(axis))]
    return lax.ppermute(value, axis, pairs)


def turned(value, distance):
    members = lax.axis_size("fsdp")
    ring = [(source, (source + distance) % members) for source in range(members)]
    return lax.ppermute(value, "fsdp", ring)


def live_before(lengths_ref, members):
    sequences = lengths_ref.shape[1] // members
    totals = [jnp.int32(0)]
    for member in range(members):
        total = totals[-1]
        for q in range(sequences):
            total = total + lengths_ref[0, member * sequences + q]
        totals.append(total)
    return totals


def chosen(values, index):
    value = values[0]
    for i in range(1, len(values)):
        value = jnp.where(index == i, values[i], value)
    return value


def aligned(place):
    return pl.multiple_of(place // ALIGN * ALIGN, ALIGN)


def token_places(lengths_ref, member, before, tokens):
    sequences = tokens // SLOT
    place = before % ALIGN
    slot = lax.broadcasted_iota(jnp.int32, (1, tokens), 1)
    places = jnp.full((1, tokens), -1, jnp.int32)
    for s in range(sequences):
        length = lengths_ref[0, member * sequences + s]
        position = slot - s * SLOT
        places = jnp.where((position >= 0) & (position < length), position + place, places)
        place = place + length
    return places


def picking(places, start, rows):
    row = lax.broadcasted_iota(jnp.int32, (rows, places.shape[1]), 0) + start
    return jnp.where(row == places, 1.0, 0.0).astype(jnp.bfloat16)


class Block:
    def __init__(self, features_ref, member, block_ref, sems):
        self.block_ref, self.width = block_ref, block_ref.shape[1] // sems.shape[0]
        start = member * block_ref.shape[1]
        self.copies = []
        for j in range(sems.shape[0]):
            there = pl.ds(pl.multiple_of(start + j * self.width, 128), self.width)
            here = pl.ds(j * self.width, self.width)
            copy = pltpu.make_async_copy(
                features_ref.at[:, there], block_ref.at[:, here], sems.at[j]
            )
            copy.start()
            self.copies.append(copy)

    def picked(self, pick, store, wait):
        for j, copy in enumerate(self.copies):
            if wait:
                copy.wait()
            here = slice(j * self.width, (j + 1) * self.width)
            rows = jnp.dot(pick, self.block_ref[:, here], preferred_element_type=jnp.float32)
            store(here, rows.astype(jnp.bfloat16))


def used_places(totals, first, sizes):
    choices = []
    for member in range(len(totals) - 1):
        used = totals[member + 1] - aligned(totals[member])
        choice = jnp.int32(0)
        for size in sizes[:-1]:
            choice = choice + jnp.where(used > first + size, 1, 0)
        choices.append(choice)
    return choices


def choice_bits(sizes):
    return (len(sizes) - 1).bit_length()


def sent_kernel(members, offsets, sizes, lengths_ref, features_ref, *refs):
    count = len(offsets)
    outs, choice_ref = refs[: 2 * count], refs[2 * count]
    block_ref, first_ref, more_ref, sems, out_sems, more_sems = refs[2 * count + 1 :]
    index = lax.axis_index("fsdp")
    blocks = [
        Block(features_ref, lax.rem(index + i, members), block_ref.at[n], sems.at[n])
        for n, i in enumerate(offsets)
    ]
    totals = live_before(lengths_ref, members)
    before, end = chosen(totals[:-1], index), chosen(totals[1:], index)
    places = token_places(lengths_ref, index, before, block_ref.shape[1])
    first, more = first_ref.shape[1], more_ref.shape[1]
    pick = picking(places, 0, first)
    copies = []
    for n, block in enumerate(blocks):

        def store(here, rows, n=n):
            first_ref[n, :, here] = rows
            copy = pltpu.make_async_copy(
                first_ref.at[n, :, here],
                outs[n].at[:, here],
                out_sems.at[n, here.start // (here.stop - here.start)],
            )
            copy.start()
            copies.append(copy)

        block.picked(pick, store, True)

    @pl.when(end - aligned(before) > first)
    def _():
        further = picking(places, first, more)
        for n, block in enumerate(blocks):

            def store(here, rows, n=n):
                more_ref[n, :, here] = rows

            block.picked(further, store, False)
            copy = pltpu.make_async_copy(more_ref.at[n], outs[count + n], more_sems.at[n])
            copy.start()
            copy.wait()

    packed = jnp.int32(0)
    for member, choice in enumerate(used_places(totals, first, sizes)):
        packed = packed | (choice << (member * choice_bits(sizes)))
    choice_ref[0] = packed
    for copy in copies:
        copy.wait()


def own_kernel(
    members,
    first,
    scale,
    lengths_ref,
    features_ref,
    targets_ref,
    master_ref,
    partner_ref,
    *refs,
):
    held_more = refs[:members]
    rows_ref, keys_ref, low_ref, halves_ref = refs[members : members + 4]
    block_ref, more_ref, sems, more_sems = refs[members + 4 :]
    index = lax.axis_index("fsdp")
    block = Block(features_ref, index, block_ref, sems)
    rows_ref[...] = jnp.zeros_like(rows_ref)
    low_ref[...] = master_ref[...].astype(jnp.bfloat16)
    halves_ref[...] = 0.5 * (master_ref[...] + partner_ref[...])
    totals = live_before(lengths_ref, members)
    before = chosen(totals[:-1], index)
    more = more_ref.shape[0]
    places = token_places(lengths_ref, index, before, block_ref.shape[0])
    pick = picking(places, 0, first + more)

    def store(here, rows):
        rows_ref[pl.ds(aligned(before), first + more), here] = rows

    block.picked(pick, store, True)
    for member in range(members):
        start = aligned(totals[member])
        used = totals[member + 1] - start

        @pl.when((member != index) & (used > first))
        def _(member=member, start=start, used=used):
            copy = pltpu.make_async_copy(held_more[member], more_ref, more_sems.at[member])
            copy.start()
            copy.wait()
            for k in range(0, more, ALIGN):

                @pl.when(used > first + k)
                def _(k=k):
                    rows_ref[pl.ds(start + first + k, ALIGN)] += more_ref[k : k + ALIGN]

    height = (rows_ref.shape[0] - first - more) // members

    @pl.loop(0, members)
    def _(j):
        here = pl.ds(pl.multiple_of(j * height, ALIGN), height)
        keys_ref[here] = (
            jnp.dot(rows_ref[here], low_ref[...], preferred_element_type=jnp.float32) * scale
        )

    keys_ref[pl.ds(aligned(before), first + more)] -= jnp.dot(
        pick, targets_ref[...], preferred_element_type=jnp.float32
    )


def copy_owned(members, share, from_ref, to_ref):
    @pl.loop(0, members)
    def _(j):
        rows = pl.ds(pl.multiple_of(j * share, ALIGN), share)
        to_ref[rows] = from_ref[rows]


def far_kernel(
    members,
    far,
    share,
    scale,
    lengths_ref,
    low_ref,
    block_ref,
    keys_ref,
    rows_ref,
    keys_out_ref,
    rows_out_ref,
):
    copy_owned(members, share, keys_ref, keys_out_ref)
    copy_owned(members, share, rows_ref, rows_out_ref)
    index = lax.axis_index("fsdp")
    totals = live_before(lengths_ref, members)
    start = aligned(chosen(totals[:-1], lax.rem(index + members - far, members)))
    here = pl.ds(start, block_ref.shape[0])
    rows_out_ref[here] += block_ref[...]
    keys_out_ref[here] += (
        jnp.dot(block_ref[...], low_ref[...], preferred_element_type=jnp.float32) * scale
    )


def keys_kernel(members, near, scale, lengths_ref, low_ref, keys_ref, *refs):
    blocks, sums, total_ref = refs[: len(near)], refs[len(near) : -1], refs[-1]
    share, width = sums[0].shape
    copy_owned(members, share, keys_ref, total_ref)
    index = lax.axis_index("fsdp")
    totals = live_before(lengths_ref, members)
    for i, block_ref in zip(near, blocks):
        start = aligned(chosen(totals[:-1], lax.rem(index + members - i, members)))
        total_ref[pl.ds(start, block_ref.shape[0])] += (
            jnp.dot(block_ref[...], low_ref[...], preferred_element_type=jnp.float32) * scale
        )
    for half in range(HALVES):
        for i in range(members):
            owner = lax.rem(index + i, members)
            rows = pl.ds(pl.multiple_of(owner * share, ALIGN), share)
            out_ref = sums[half * members + i]
            here = slice(half * width, (half + 1) * width)
            out_ref[...] = total_ref[rows, here].astype(out_ref.dtype)


def turn_kernel(members, near, lengths_ref, rows_ref, *refs):
    blocks, (turned_ref, all_ref) = refs[: len(near)], refs[len(near) :]
    index = lax.axis_index("fsdp")
    totals = live_before(lengths_ref, members)
    all_ref[...] = rows_ref[...]
    for i, block_ref in zip(near, blocks):
        start = aligned(chosen(totals[:-1], lax.rem(index + members - i, members)))
        all_ref[pl.ds(start, block_ref.shape[0])] += block_ref[...]
    for start in range(0, turned_ref.shape[1], 128):
        turned_ref[:, start : start + 128] = all_ref[start : start + 128, :].T


def gradient_kernel(members, turned_ref, *refs):
    residuals, (gradient_ref, low_ref, squares_ref, all_ref) = refs[:members], refs[members:]
    index = lax.axis_index("fsdp")
    share = residuals[0].shape[0]
    for i in range(members):
        owner = lax.rem(index + members - i, members)
        all_ref[pl.ds(pl.multiple_of(owner * share, ALIGN), share)] = residuals[i][...]
    squares_ref[...] = jnp.zeros_like(squares_ref)
    height = min(256, turned_ref.shape[0])

    @pl.loop(0, turned_ref.shape[0] // height)
    def _(j):
        rows = pl.ds(pl.multiple_of(j * height, height), height)
        gradient = jnp.dot(turned_ref[rows], all_ref[...], preferred_element_type=jnp.float32)
        gradient_ref[rows] = gradient
        low_ref[rows] = gradient.astype(low_ref.dtype)
        squares = jnp.sum((gradient * gradient).reshape(-1, 8, gradient.shape[1]), axis=0)
        lanes = squares.shape[1] // 128
        squares_ref[...] += sum(squares[:, 128 * k : 128 * (k + 1)] for k in range(lanes))


def average_kernel(entries, own_ref, other_ref, halves_ref, *refs):
    gradients, partners, (out_ref, done_ref, sems) = refs[:HALVES], refs[HALVES:-3], refs[-3:]
    rate = 0.5 * learning_rate
    own = rate * lax.rsqrt(jnp.sum(own_ref[...], keepdims=True) / entries + epsilon)
    other = rate * lax.rsqrt(jnp.sum(other_ref[...], keepdims=True) / entries + epsilon)
    pieces = sems.shape[0]
    height = done_ref.shape[0] // pieces
    width = done_ref.shape[1] // HALVES
    copies = []
    for j in range(pieces):
        rows = pl.ds(j * height, height)
        for half in range(HALVES):
            here = slice(half * width, (half + 1) * width)
            done_ref[rows, here] = (
                halves_ref[rows, here]
                - gradients[half][rows] * own
                - partners[half][rows].astype(jnp.float32) * other
            )
        copies.append(pltpu.make_async_copy(done_ref.at[rows], out_ref.at[rows], sems.at[j]))
        copies[-1].start()
    for copy in copies:
        copy.wait()


def more_rows(size, source, offsets, blocks):
    if size == 0:
        return blocks[0]
    members = lax.axis_size("fsdp")
    moved = [
        lax.ppermute(block[:size], "fsdp", [(source, (source + i) % members)])
        for i, block in zip(offsets, blocks)
    ]
    return jnp.pad(sum(moved[1:], moved[0]), ((0, blocks[0].shape[0] - size), (0, 0)))


def local(activations, targets, weights, lengths):
    features = activations[0]
    wanted = targets[0]
    master = weights[0]
    tokens_here = features.shape[0]
    local_rows, columns = master.shape
    members = lax.axis_size("fsdp")
    distance_bit = STEP % (lax.axis_size("replica").bit_length() - 1)
    share = tokens_here // 2
    first = -(-(share + 32) // ALIGN) * ALIGN
    more = -(-(tokens_here + ALIGN - first) // ALIGN) * ALIGN
    steps = (16, 32, 48, 64, 80, 96, 128) if members <= 4 else (96,)
    sizes = [0] + [size for size in steps if size < more] + [more]
    most = first + more
    scale = features.shape[1] ** (-0.5)
    places = members * share + most

    vmem = pl.BlockSpec(memory_space=pltpu.VMEM)
    anywhere = pl.BlockSpec(memory_space=pl.ANY)
    smem = pl.BlockSpec(memory_space=pltpu.SMEM)
    params = pltpu.CompilerParams(vmem_limit_bytes=16 * 2**20)
    middle = pltpu.CompilerParams(vmem_limit_bytes=40 * 2**20)
    large = pltpu.CompilerParams(vmem_limit_bytes=56 * 2**20)

    def array(rows, width, dtype):
        return jax.ShapeDtypeStruct((rows, width), dtype)

    def cost(flops, moved):
        return pl.CostEstimate(flops=flops, bytes_accessed=moved, transcendentals=0)

    def sent_to(offsets):
        count = len(offsets)
        pieces = max(1, local_rows // 256)
        *arrays, choice = pl.pallas_call(
            functools.partial(sent_kernel, members, offsets, sizes),
            in_specs=[smem, anywhere],
            out_specs=[anywhere] * (2 * count) + [smem],
            out_shape=[
                array(rows, local_rows, jnp.bfloat16) for rows in (first, more) for _ in offsets
            ]
            + [jax.ShapeDtypeStruct((1,), jnp.int32)],
            scratch_shapes=[
                pltpu.VMEM((count, tokens_here, local_rows), jnp.bfloat16),
                pltpu.VMEM((count, first, local_rows), jnp.bfloat16),
                pltpu.VMEM((count, more, local_rows), jnp.bfloat16),
                pltpu.SemaphoreType.DMA((count, pieces)),
                pltpu.SemaphoreType.DMA((count, pieces)),
                pltpu.SemaphoreType.DMA((count,)),
            ],
            compiler_params=large,
            cost_estimate=cost(
                2 * count * first * tokens_here * local_rows,
                2 * count * (tokens_here + first) * local_rows,
            ),
        )(lengths, features)
        return arrays[:count], arrays[count:], choice

    far = members // 2
    near = [i for i in range(1, members) if i != far]
    far_first, far_more, choice = sent_to([far])
    near_first, near_more, _ = sent_to(near)
    held_far = turned(far_first[0], far)
    offsets = [far] + near
    bits = choice_bits(sizes)
    held_more = [
        lax.switch(
            lax.shift_right_logical(choice[0], jnp.int32(source * bits)) & (2**bits - 1),
            [functools.partial(more_rows, size, source, offsets) for size in sizes],
            far_more + near_more,
        )
        for source in range(members)
    ]
    near_first, held_more, late_lengths = lax.optimization_barrier((near_first, held_more, lengths))
    held = [turned(block, i) for i, block in zip(near, near_first)]

    partner_master = swapped(master, "replica", distance_bit)
    rows, keys, low, halves = pl.pallas_call(
        functools.partial(own_kernel, members, first, scale),
        in_specs=[smem, anywhere, vmem, vmem, vmem] + [anywhere] * members,
        out_specs=[vmem] * 4,
        out_shape=[
            array(places, local_rows, jnp.bfloat16),
            array(places, columns, jnp.float32),
            array(local_rows, columns, jnp.bfloat16),
            array(local_rows, columns, jnp.float32),
        ],
        scratch_shapes=[
            pltpu.VMEM((tokens_here, local_rows), jnp.bfloat16),
            pltpu.VMEM((more, local_rows), jnp.bfloat16),
            pltpu.SemaphoreType.DMA((max(1, local_rows // 256),)),
            pltpu.SemaphoreType.DMA((members,)),
        ],
        compiler_params=middle,
        cost_estimate=cost(
            2 * (most * tokens_here + members * share * columns) * (local_rows + columns),
            20 * local_rows * columns,
        ),
    )(late_lengths, features, wanted, master, partner_master, *held_more)
    keys, rows = pl.pallas_call(
        functools.partial(far_kernel, members, far, share, scale),
        in_specs=[smem] + [vmem] * 4,
        out_specs=[vmem] * 2,
        out_shape=[
            array(places, columns, jnp.float32),
            array(places, local_rows, jnp.bfloat16),
        ],
        input_output_aliases={3: 0, 4: 1},
        compiler_params=params,
        cost_estimate=cost(2 * first * local_rows * columns, 8 * first * (local_rows + columns)),
    )(lengths, low, held_far, keys, rows)

    width = columns // HALVES
    sum_shapes = [array(share, width, jnp.bfloat16 if i else jnp.float32) for i in range(members)]
    *sums, _ = pl.pallas_call(
        functools.partial(keys_kernel, members, near, scale),
        in_specs=[smem, vmem, vmem] + [vmem] * len(near),
        out_specs=[vmem] * (HALVES * members + 1),
        out_shape=sum_shapes * HALVES + [array(places, columns, jnp.float32)],
        input_output_aliases={2: HALVES * members},
        compiler_params=params,
        cost_estimate=cost(
            2 * len(near) * first * local_rows * columns, 8 * places * columns
        ),
    )(lengths, low, keys, *held)
    sums = [sums[half * members : (half + 1) * members] for half in range(HALVES)]

    turned_rows = pl.pallas_call(
        functools.partial(turn_kernel, members, near),
        in_specs=[smem, vmem] + [vmem] * len(near),
        out_specs=vmem,
        out_shape=array(local_rows, members * share, jnp.bfloat16),
        scratch_shapes=[pltpu.VMEM((places, local_rows), jnp.bfloat16)],
        compiler_params=params,
        cost_estimate=cost(0, 4 * members * share * local_rows),
    )(lengths, rows, *held)

    gradients, partners, squares = [], [], 0.0
    for half in range(HALVES):
        residual = sums[half][0]
        for i in range(1, members):
            residual = residual + turned(sums[half][i], i).astype(jnp.float32)
        residual = residual.astype(jnp.bfloat16)
        residuals = [residual] + [turned(residual, i) for i in range(1, members)]
        gradient, low_gradient, own_squares = pl.pallas_call(
            functools.partial(gradient_kernel, members),
            in_specs=[vmem] + [vmem] * members,
            out_specs=[vmem] * 3,
            out_shape=[
                array(local_rows, width, jnp.float32),
                array(local_rows, width, jnp.bfloat16),
                array(8, 128, jnp.float32),
            ],
            scratch_shapes=[pltpu.VMEM((members * share, width), jnp.bfloat16)],
            compiler_params=params,
            cost_estimate=cost(
                2 * members * share * local_rows * width, 8 * local_rows * width
            ),
        )(turned_rows, *residuals)
        gradients.append(gradient)
        partners.append(swapped(low_gradient, "replica", distance_bit))
        squares = squares + own_squares

    total = squares
    for i in range(1, members):
        total = total + turned(squares, i)
    partner_total = swapped(total, "replica", distance_bit)

    averaged = pl.pallas_call(
        functools.partial(average_kernel, members * local_rows * columns),
        in_specs=[vmem] * (3 + 2 * HALVES),
        out_specs=anywhere,
        out_shape=array(local_rows, columns, jnp.float32),
        scratch_shapes=[
            pltpu.VMEM((local_rows, columns), jnp.float32),
            pltpu.SemaphoreType.DMA((4,)),
        ],
        compiler_params=params,
    )(total, partner_total, halves, *gradients, *partners)
    return averaged[None]


def solution(mesh):
    return jax.shard_map(
        local,
        mesh=mesh,
        in_specs=(
            P("replica", "fsdp", None),
            P("replica", "fsdp", None),
            P("replica", "fsdp", None),
            P("replica", None),
        ),
        out_specs=P("replica", "fsdp", None),
        check_vma=False,
    )
```

```python
import functools

import jax
import jax.numpy as jnp
from jax import lax
from jax.experimental import pallas as pl
from jax.experimental.pallas import tpu as pltpu
from jax.sharding import PartitionSpec as P

SLOT = 64
STEP = 3
ALIGN = 16
HALVES = 2

learning_rate = 0.1
epsilon = 1e-06


def swapped(value, axis, bit):
    mask = 2**bit
    pairs = [(source, source ^ mask) for source in range(lax.axis_size(axis))]
    return lax.ppermute(value, axis, pairs)


def turned(value, distance):
    members = lax.axis_size("fsdp")
    ring = [(source, (source + distance) % members) for source in range(members)]
    return lax.ppermute(value, "fsdp", ring)


def live_before(lengths_ref, members):
    sequences = lengths_ref.shape[1] // members
    totals = [jnp.int32(0)]
    for member in range(members):
        total = totals[-1]
        for q in range(sequences):
            total = total + lengths_ref[0, member * sequences + q]
        totals.append(total)
    return totals


def chosen(values, index):
    value = values[0]
    for i in range(1, len(values)):
        value = jnp.where(index == i, values[i], value)
    return value


def aligned(place):
    return pl.multiple_of(place // ALIGN * ALIGN, ALIGN)


def token_places(lengths_ref, member, before, tokens):
    sequences = tokens // SLOT
    place = before % ALIGN
    slot = lax.broadcasted_iota(jnp.int32, (1, tokens), 1)
    places = jnp.full((1, tokens), -1, jnp.int32)
    for s in range(sequences):
        length = lengths_ref[0, member * sequences + s]
        position = slot - s * SLOT
        places = jnp.where((position >= 0) & (position < length), position + place, places)
        place = place + length
    return places


def picking(places, start, rows):
    row = lax.broadcasted_iota(jnp.int32, (rows, places.shape[1]), 0) + start
    return jnp.where(row == places, 1.0, 0.0).astype(jnp.bfloat16)


class Block:
    def __init__(self, features_ref, member, block_ref, sems):
        self.block_ref, self.width = block_ref, block_ref.shape[1] // sems.shape[0]
        start = member * block_ref.shape[1]
        self.copies = []
        for j in range(sems.shape[0]):
            there = pl.ds(pl.multiple_of(start + j * self.width, 128), self.width)
            here = pl.ds(j * self.width, self.width)
            copy = pltpu.make_async_copy(
                features_ref.at[:, there], block_ref.at[:, here], sems.at[j]
            )
            copy.start()
            self.copies.append(copy)

    def picked(self, pick, store, wait):
        for j, copy in enumerate(self.copies):
            if wait:
                copy.wait()
            here = slice(j * self.width, (j + 1) * self.width)
            rows = jnp.dot(pick, self.block_ref[:, here], preferred_element_type=jnp.float32)
            store(here, rows.astype(jnp.bfloat16))


def used_places(totals, first, sizes):
    choices = []
    for member in range(len(totals) - 1):
        used = totals[member + 1] - aligned(totals[member])
        choice = jnp.int32(0)
        for size in sizes[:-1]:
            choice = choice + jnp.where(used > first + size, 1, 0)
        choices.append(choice)
    return choices


def choice_bits(sizes):
    return (len(sizes) - 1).bit_length()


def sent_kernel(members, offsets, sizes, lengths_ref, features_ref, *refs):
    count = len(offsets)
    outs, choice_ref = refs[: 2 * count], refs[2 * count]
    block_ref, first_ref, more_ref, sems, out_sems, more_sems = refs[2 * count + 1 :]
    index = lax.axis_index("fsdp")
    blocks = [
        Block(features_ref, lax.rem(index + i, members), block_ref.at[n], sems.at[n])
        for n, i in enumerate(offsets)
    ]
    totals = live_before(lengths_ref, members)
    before, end = chosen(totals[:-1], index), chosen(totals[1:], index)
    places = token_places(lengths_ref, index, before, block_ref.shape[1])
    first, more = first_ref.shape[1], more_ref.shape[1]
    pick = picking(places, 0, first)
    copies = []
    for n, block in enumerate(blocks):

        def store(here, rows, n=n):
            first_ref[n, :, here] = rows
            copy = pltpu.make_async_copy(
                first_ref.at[n, :, here],
                outs[n].at[:, here],
                out_sems.at[n, here.start // (here.stop - here.start)],
            )
            copy.start()
            copies.append(copy)

        block.picked(pick, store, True)

    @pl.when(end - aligned(before) > first)
    def _():
        further = picking(places, first, more)
        for n, block in enumerate(blocks):

            def store(here, rows, n=n):
                more_ref[n, :, here] = rows

            block.picked(further, store, False)
            copy = pltpu.make_async_copy(more_ref.at[n], outs[count + n], more_sems.at[n])
            copy.start()
            copy.wait()

    packed = jnp.int32(0)
    for member, choice in enumerate(used_places(totals, first, sizes)):
        packed = packed | (choice << (member * choice_bits(sizes)))
    choice_ref[0] = packed
    for copy in copies:
        copy.wait()


def own_kernel(
    members,
    far,
    scale,
    lengths_ref,
    features_ref,
    targets_ref,
    master_ref,
    partner_ref,
    far_ref,
    *refs,
):
    held_more = refs[:members]
    rows_ref, keys_ref, low_ref, halves_ref = refs[members : members + 4]
    block_ref, first_ref, more_ref, sems, first_sem, more_sems = refs[members + 4 :]
    index = lax.axis_index("fsdp")
    block = Block(features_ref, index, block_ref, sems)
    far_copy = pltpu.make_async_copy(far_ref, first_ref, first_sem)
    far_copy.start()
    rows_ref[...] = jnp.zeros_like(rows_ref)
    low_ref[...] = master_ref[...].astype(jnp.bfloat16)
    halves_ref[...] = 0.5 * (master_ref[...] + partner_ref[...])
    totals = live_before(lengths_ref, members)
    before = chosen(totals[:-1], index)
    first, more = first_ref.shape[0], more_ref.shape[0]
    places = token_places(lengths_ref, index, before, block_ref.shape[0])
    pick = picking(places, 0, first + more)

    def store(here, rows):
        rows_ref[pl.ds(aligned(before), first + more), here] = rows

    block.picked(pick, store, True)
    far_start = aligned(chosen(totals[:-1], lax.rem(index + members - far, members)))
    far_copy.wait()
    rows_ref[pl.ds(far_start, first)] += first_ref[...]
    for member in range(members):
        start = aligned(totals[member])
        used = totals[member + 1] - start

        @pl.when((member != index) & (used > first))
        def _(member=member, start=start, used=used):
            copy = pltpu.make_async_copy(held_more[member], more_ref, more_sems.at[member])
            copy.start()
            copy.wait()
            for k in range(0, more, ALIGN):

                @pl.when(used > first + k)
                def _(k=k):
                    rows_ref[pl.ds(start + first + k, ALIGN)] += more_ref[k : k + ALIGN]

    height = (rows_ref.shape[0] - first - more) // members

    @pl.loop(0, members)
    def _(j):
        here = pl.ds(pl.multiple_of(j * height, ALIGN), height)
        keys_ref[here] = (
            jnp.dot(rows_ref[here], low_ref[...], preferred_element_type=jnp.float32) * scale
        )

    keys_ref[pl.ds(aligned(before), first + more)] -= jnp.dot(
        pick, targets_ref[...], preferred_element_type=jnp.float32
    )


def keys_kernel(members, near, scale, lengths_ref, low_ref, keys_ref, *refs):
    blocks, sums, total_ref = refs[: len(near)], refs[len(near) : -1], refs[-1]
    share, width = sums[0].shape

    @pl.loop(0, members)
    def _(j):
        rows = pl.ds(pl.multiple_of(j * share, ALIGN), share)
        total_ref[rows] = keys_ref[rows]

    index = lax.axis_index("fsdp")
    totals = live_before(lengths_ref, members)
    for i, block_ref in zip(near, blocks):
        start = aligned(chosen(totals[:-1], lax.rem(index + members - i, members)))
        total_ref[pl.ds(start, block_ref.shape[0])] += (
            jnp.dot(block_ref[...], low_ref[...], preferred_element_type=jnp.float32) * scale
        )
    for half in range(HALVES):
        for i in range(members):
            owner = lax.rem(index + i, members)
            rows = pl.ds(pl.multiple_of(owner * share, ALIGN), share)
            out_ref = sums[half * members + i]
            here = slice(half * width, (half + 1) * width)
            out_ref[...] = total_ref[rows, here].astype(out_ref.dtype)


def turn_kernel(members, near, lengths_ref, rows_ref, *refs):
    blocks, (turned_ref, all_ref) = refs[: len(near)], refs[len(near) :]
    index = lax.axis_index("fsdp")
    totals = live_before(lengths_ref, members)
    all_ref[...] = rows_ref[...]
    for i, block_ref in zip(near, blocks):
        start = aligned(chosen(totals[:-1], lax.rem(index + members - i, members)))
        all_ref[pl.ds(start, block_ref.shape[0])] += block_ref[...]
    for start in range(0, turned_ref.shape[1], 128):
        turned_ref[:, start : start + 128] = all_ref[start : start + 128, :].T


def gradient_kernel(members, turned_ref, *refs):
    residuals, (gradient_ref, low_ref, squares_ref, all_ref) = refs[:members], refs[members:]
    index = lax.axis_index("fsdp")
    share = residuals[0].shape[0]
    for i in range(members):
        owner = lax.rem(index + members - i, members)
        all_ref[pl.ds(pl.multiple_of(owner * share, ALIGN), share)] = residuals[i][...]
    squares_ref[...] = jnp.zeros_like(squares_ref)
    height = min(256, turned_ref.shape[0])

    @pl.loop(0, turned_ref.shape[0] // height)
    def _(j):
        rows = pl.ds(pl.multiple_of(j * height, height), height)
        gradient = jnp.dot(turned_ref[rows], all_ref[...], preferred_element_type=jnp.float32)
        gradient_ref[rows] = gradient
        low_ref[rows] = gradient.astype(low_ref.dtype)
        squares = jnp.sum((gradient * gradient).reshape(-1, 8, gradient.shape[1]), axis=0)
        lanes = squares.shape[1] // 128
        squares_ref[...] += sum(squares[:, 128 * k : 128 * (k + 1)] for k in range(lanes))


def average_kernel(entries, own_ref, other_ref, halves_ref, *refs):
    gradients, partners, (out_ref, done_ref, sems) = refs[:HALVES], refs[HALVES:-3], refs[-3:]
    rate = 0.5 * learning_rate
    own = rate * lax.rsqrt(jnp.sum(own_ref[...], keepdims=True) / entries + epsilon)
    other = rate * lax.rsqrt(jnp.sum(other_ref[...], keepdims=True) / entries + epsilon)
    pieces = sems.shape[0]
    height = done_ref.shape[0] // pieces
    width = done_ref.shape[1] // HALVES
    copies = []
    for j in range(pieces):
        rows = pl.ds(j * height, height)
        for half in range(HALVES):
            here = slice(half * width, (half + 1) * width)
            done_ref[rows, here] = (
                halves_ref[rows, here]
                - gradients[half][rows] * own
                - partners[half][rows].astype(jnp.float32) * other
            )
        copies.append(pltpu.make_async_copy(done_ref.at[rows], out_ref.at[rows], sems.at[j]))
        copies[-1].start()
    for copy in copies:
        copy.wait()


def more_rows(size, source, offsets, blocks):
    if size == 0:
        return blocks[0]
    members = lax.axis_size("fsdp")
    moved = [
        lax.ppermute(block[:size], "fsdp", [(source, (source + i) % members)])
        for i, block in zip(offsets, blocks)
    ]
    return jnp.pad(sum(moved[1:], moved[0]), ((0, blocks[0].shape[0] - size), (0, 0)))


def local(activations, targets, weights, lengths):
    features = activations[0]
    wanted = targets[0]
    master = weights[0]
    tokens_here = features.shape[0]
    local_rows, columns = master.shape
    members = lax.axis_size("fsdp")
    distance_bit = STEP % (lax.axis_size("replica").bit_length() - 1)
    share = tokens_here // 2
    first = -(-(share + 32) // ALIGN) * ALIGN
    more = -(-(tokens_here + ALIGN - first) // ALIGN) * ALIGN
    steps = (16, 32, 48, 64, 80, 96, 128) if members <= 4 else (96,)
    sizes = [0] + [size for size in steps if size < more] + [more]
    most = first + more
    scale = features.shape[1] ** (-0.5)
    places = members * share + most

    vmem = pl.BlockSpec(memory_space=pltpu.VMEM)
    anywhere = pl.BlockSpec(memory_space=pl.ANY)
    smem = pl.BlockSpec(memory_space=pltpu.SMEM)
    params = pltpu.CompilerParams(vmem_limit_bytes=16 * 2**20)
    middle = pltpu.CompilerParams(vmem_limit_bytes=24 * 2**20)
    large = pltpu.CompilerParams(vmem_limit_bytes=56 * 2**20)

    def array(rows, width, dtype):
        return jax.ShapeDtypeStruct((rows, width), dtype)

    def cost(flops, moved):
        return pl.CostEstimate(flops=flops, bytes_accessed=moved, transcendentals=0)

    def sent_to(offsets):
        count = len(offsets)
        pieces = max(1, local_rows // 256)
        *arrays, choice = pl.pallas_call(
            functools.partial(sent_kernel, members, offsets, sizes),
            in_specs=[smem, anywhere],
            out_specs=[anywhere] * (2 * count) + [smem],
            out_shape=[
                array(rows, local_rows, jnp.bfloat16) for rows in (first, more) for _ in offsets
            ]
            + [jax.ShapeDtypeStruct((1,), jnp.int32)],
            scratch_shapes=[
                pltpu.VMEM((count, tokens_here, local_rows), jnp.bfloat16),
                pltpu.VMEM((count, first, local_rows), jnp.bfloat16),
                pltpu.VMEM((count, more, local_rows), jnp.bfloat16),
                pltpu.SemaphoreType.DMA((count, pieces)),
                pltpu.SemaphoreType.DMA((count, pieces)),
                pltpu.SemaphoreType.DMA((count,)),
            ],
            compiler_params=large,
            cost_estimate=cost(
                2 * count * first * tokens_here * local_rows,
                2 * count * (tokens_here + first) * local_rows,
            ),
        )(lengths, features)
        return arrays[:count], arrays[count:], choice

    far = members // 2
    near = [i for i in range(1, members) if i != far]
    far_first, far_more, choice = sent_to([far])
    near_first, near_more, _ = sent_to(near)
    held_far = turned(far_first[0], far)
    offsets = [far] + near
    bits = choice_bits(sizes)
    held_more = [
        lax.switch(
            lax.shift_right_logical(choice[0], jnp.int32(source * bits)) & (2**bits - 1),
            [functools.partial(more_rows, size, source, offsets) for size in sizes],
            far_more + near_more,
        )
        for source in range(members)
    ]
    near_first, held_more, late_lengths = lax.optimization_barrier((near_first, held_more, lengths))
    held = [turned(block, i) for i, block in zip(near, near_first)]

    partner_master = swapped(master, "replica", distance_bit)
    rows, keys, low, halves = pl.pallas_call(
        functools.partial(own_kernel, members, far, scale),
        in_specs=[smem, anywhere, vmem, vmem, vmem, anywhere] + [anywhere] * members,
        out_specs=[vmem] * 4,
        out_shape=[
            array(places, local_rows, jnp.bfloat16),
            array(places, columns, jnp.float32),
            array(local_rows, columns, jnp.bfloat16),
            array(local_rows, columns, jnp.float32),
        ],
        scratch_shapes=[
            pltpu.VMEM((tokens_here, local_rows), jnp.bfloat16),
            pltpu.VMEM((first, local_rows), jnp.bfloat16),
            pltpu.VMEM((more, local_rows), jnp.bfloat16),
            pltpu.SemaphoreType.DMA((max(1, local_rows // 256),)),
            pltpu.SemaphoreType.DMA,
            pltpu.SemaphoreType.DMA((members,)),
        ],
        compiler_params=middle,
        cost_estimate=cost(
            2 * (most * tokens_here + members * share * columns) * (local_rows + columns),
            20 * local_rows * columns,
        ),
    )(late_lengths, features, wanted, master, partner_master, held_far, *held_more)

    width = columns // HALVES
    sum_shapes = [array(share, width, jnp.bfloat16 if i else jnp.float32) for i in range(members)]
    *sums, _ = pl.pallas_call(
        functools.partial(keys_kernel, members, near, scale),
        in_specs=[smem, vmem, vmem] + [vmem] * len(near),
        out_specs=[vmem] * (HALVES * members + 1),
        out_shape=sum_shapes * HALVES + [array(places, columns, jnp.float32)],
        input_output_aliases={2: HALVES * members},
        compiler_params=params,
        cost_estimate=cost(
            2 * len(near) * first * local_rows * columns, 8 * places * columns
        ),
    )(lengths, low, keys, *held)
    sums = [sums[half * members : (half + 1) * members] for half in range(HALVES)]

    turned_rows = pl.pallas_call(
        functools.partial(turn_kernel, members, near),
        in_specs=[smem, vmem] + [vmem] * len(near),
        out_specs=vmem,
        out_shape=array(local_rows, members * share, jnp.bfloat16),
        scratch_shapes=[pltpu.VMEM((places, local_rows), jnp.bfloat16)],
        compiler_params=params,
        cost_estimate=cost(0, 4 * members * share * local_rows),
    )(lengths, rows, *held)

    gradients, partners, squares = [], [], 0.0
    for half in range(HALVES):
        residual = sums[half][0]
        for i in range(1, members):
            residual = residual + turned(sums[half][i], i).astype(jnp.float32)
        residual = residual.astype(jnp.bfloat16)
        residuals = [residual] + [turned(residual, i) for i in range(1, members)]
        gradient, low_gradient, own_squares = pl.pallas_call(
            functools.partial(gradient_kernel, members),
            in_specs=[vmem] + [vmem] * members,
            out_specs=[vmem] * 3,
            out_shape=[
                array(local_rows, width, jnp.float32),
                array(local_rows, width, jnp.bfloat16),
                array(8, 128, jnp.float32),
            ],
            scratch_shapes=[pltpu.VMEM((members * share, width), jnp.bfloat16)],
            compiler_params=params,
            cost_estimate=cost(
                2 * members * share * local_rows * width, 8 * local_rows * width
            ),
        )(turned_rows, *residuals)
        gradients.append(gradient)
        partners.append(swapped(low_gradient, "replica", distance_bit))
        squares = squares + own_squares

    total = squares
    for i in range(1, members):
        total = total + turned(squares, i)
    partner_total = swapped(total, "replica", distance_bit)

    averaged = pl.pallas_call(
        functools.partial(average_kernel, members * local_rows * columns),
        in_specs=[vmem] * (3 + 2 * HALVES),
        out_specs=anywhere,
        out_shape=array(local_rows, columns, jnp.float32),
        scratch_shapes=[
            pltpu.VMEM((local_rows, columns), jnp.float32),
            pltpu.SemaphoreType.DMA((4,)),
        ],
        compiler_params=params,
    )(total, partner_total, halves, *gradients, *partners)
    return averaged[None]


def solution(mesh):
    return jax.shard_map(
        local,
        mesh=mesh,
        in_specs=(
            P("replica", "fsdp", None),
            P("replica", "fsdp", None),
            P("replica", "fsdp", None),
            P("replica", None),
        ),
        out_specs=P("replica", "fsdp", None),
        check_vma=False,
    )
```

```python
import functools

import jax
import jax.numpy as jnp
from jax import lax
from jax.experimental import pallas as pl
from jax.experimental.pallas import tpu as pltpu
from jax.sharding import PartitionSpec as P

SLOT = 64
STEP = 3
ALIGN = 16
HALVES = 2

learning_rate = 0.1
epsilon = 1e-06


def swapped(value, axis, bit):
    mask = 2**bit
    pairs = [(source, source ^ mask) for source in range(lax.axis_size(axis))]
    return lax.ppermute(value, axis, pairs)


def turned(value, distance):
    members = lax.axis_size("fsdp")
    ring = [(source, (source + distance) % members) for source in range(members)]
    return lax.ppermute(value, "fsdp", ring)


def live_before(lengths_ref, members):
    sequences = lengths_ref.shape[1] // members
    totals = [jnp.int32(0)]
    for member in range(members):
        total = totals[-1]
        for q in range(sequences):
            total = total + lengths_ref[0, member * sequences + q]
        totals.append(total)
    return totals


def chosen(values, index):
    value = values[0]
    for i in range(1, len(values)):
        value = jnp.where(index == i, values[i], value)
    return value


def aligned(place):
    return pl.multiple_of(place // ALIGN * ALIGN, ALIGN)


def token_places(lengths_ref, member, before, tokens):
    sequences = tokens // SLOT
    place = before % ALIGN
    slot = lax.broadcasted_iota(jnp.int32, (1, tokens), 1)
    places = jnp.full((1, tokens), -1, jnp.int32)
    for s in range(sequences):
        length = lengths_ref[0, member * sequences + s]
        position = slot - s * SLOT
        places = jnp.where((position >= 0) & (position < length), position + place, places)
        place = place + length
    return places


def picking(places, start, rows):
    row = lax.broadcasted_iota(jnp.int32, (rows, places.shape[1]), 0) + start
    return jnp.where(row == places, 1.0, 0.0).astype(jnp.bfloat16)


class Block:
    def __init__(self, features_ref, member, block_ref, sems):
        self.block_ref, self.width = block_ref, block_ref.shape[1] // sems.shape[0]
        start = member * block_ref.shape[1]
        self.copies = []
        for j in range(sems.shape[0]):
            there = pl.ds(pl.multiple_of(start + j * self.width, 128), self.width)
            here = pl.ds(j * self.width, self.width)
            copy = pltpu.make_async_copy(
                features_ref.at[:, there], block_ref.at[:, here], sems.at[j]
            )
            copy.start()
            self.copies.append(copy)

    def picked(self, pick, store, wait):
        for j, copy in enumerate(self.copies):
            if wait:
                copy.wait()
            here = slice(j * self.width, (j + 1) * self.width)
            rows = jnp.dot(pick, self.block_ref[:, here], preferred_element_type=jnp.float32)
            store(here, rows.astype(jnp.bfloat16))


def used_places(totals, first, sizes):
    choices = []
    for member in range(len(totals) - 1):
        used = totals[member + 1] - aligned(totals[member])
        choice = jnp.int32(0)
        for size in sizes[:-1]:
            choice = choice + jnp.where(used > first + size, 1, 0)
        choices.append(choice)
    return choices


def choice_bits(sizes):
    return (len(sizes) - 1).bit_length()


def sent_kernel(members, offsets, sizes, lengths_ref, features_ref, *refs):
    count = len(offsets)
    outs, choice_ref = refs[: 2 * count], refs[2 * count]
    block_ref, first_ref, more_ref, sems, out_sems, more_sems = refs[2 * count + 1 :]
    index = lax.axis_index("fsdp")
    blocks = [
        Block(features_ref, lax.rem(index + i, members), block_ref.at[n], sems.at[n])
        for n, i in enumerate(offsets)
    ]
    totals = live_before(lengths_ref, members)
    before, end = chosen(totals[:-1], index), chosen(totals[1:], index)
    places = token_places(lengths_ref, index, before, block_ref.shape[1])
    first, more = first_ref.shape[1], more_ref.shape[1]
    pick = picking(places, 0, first)
    copies = []
    for n, block in enumerate(blocks):

        def store(here, rows, n=n):
            first_ref[n, :, here] = rows
            copy = pltpu.make_async_copy(
                first_ref.at[n, :, here],
                outs[n].at[:, here],
                out_sems.at[n, here.start // (here.stop - here.start)],
            )
            copy.start()
            copies.append(copy)

        block.picked(pick, store, True)

    @pl.when(end - aligned(before) > first)
    def _():
        further = picking(places, first, more)
        for n, block in enumerate(blocks):

            def store(here, rows, n=n):
                more_ref[n, :, here] = rows

            block.picked(further, store, False)
            copy = pltpu.make_async_copy(more_ref.at[n], outs[count + n], more_sems.at[n])
            copy.start()
            copy.wait()

    packed = jnp.int32(0)
    for member, choice in enumerate(used_places(totals, first, sizes)):
        packed = packed | (choice << (member * choice_bits(sizes)))
    choice_ref[0] = packed
    for copy in copies:
        copy.wait()


def own_kernel(
    members,
    far,
    scale,
    lengths_ref,
    features_ref,
    targets_ref,
    master_ref,
    partner_ref,
    far_ref,
    *refs,
):
    held_more = refs[:members]
    rows_ref, keys_ref, low_ref, halves_ref = refs[members : members + 4]
    block_ref, first_ref, more_ref, sems, first_sem, more_sems = refs[members + 4 :]
    index = lax.axis_index("fsdp")
    block = Block(features_ref, index, block_ref, sems)
    far_copy = pltpu.make_async_copy(far_ref, first_ref, first_sem)
    far_copy.start()
    rows_ref[...] = jnp.zeros_like(rows_ref)
    low_ref[...] = master_ref[...].astype(jnp.bfloat16)
    halves_ref[...] = 0.5 * (master_ref[...] + partner_ref[...])
    totals = live_before(lengths_ref, members)
    before = chosen(totals[:-1], index)
    first, more = first_ref.shape[0], more_ref.shape[0]
    places = token_places(lengths_ref, index, before, block_ref.shape[0])
    pick = picking(places, 0, first + more)

    def store(here, rows):
        rows_ref[pl.ds(aligned(before), first + more), here] = rows

    block.picked(pick, store, True)
    far_start = aligned(chosen(totals[:-1], lax.rem(index + members - far, members)))
    far_copy.wait()
    rows_ref[pl.ds(far_start, first)] += first_ref[...]
    for member in range(members):
        start = aligned(totals[member])
        used = totals[member + 1] - start

        @pl.when((member != index) & (used > first))
        def _(member=member, start=start, used=used):
            copy = pltpu.make_async_copy(held_more[member], more_ref, more_sems.at[member])
            copy.start()
            copy.wait()
            for k in range(0, more, ALIGN):

                @pl.when(used > first + k)
                def _(k=k):
                    rows_ref[pl.ds(start + first + k, ALIGN)] += more_ref[k : k + ALIGN]

    height = (rows_ref.shape[0] - first - more) // members

    @pl.loop(0, members)
    def _(j):
        here = pl.ds(pl.multiple_of(j * height, ALIGN), height)
        keys_ref[here] = (
            jnp.dot(rows_ref[here], low_ref[...], preferred_element_type=jnp.float32) * scale
        )

    keys_ref[pl.ds(aligned(before), first + more)] -= jnp.dot(
        pick, targets_ref[...], preferred_element_type=jnp.float32
    )


def keys_kernel(members, near, scale, lengths_ref, low_ref, keys_ref, *refs):
    blocks, sums, total_ref = refs[: len(near)], refs[len(near) : -1], refs[-1]
    share, width = sums[0].shape

    @pl.loop(0, members)
    def _(j):
        rows = pl.ds(pl.multiple_of(j * share, ALIGN), share)
        total_ref[rows] = keys_ref[rows]

    index = lax.axis_index("fsdp")
    totals = live_before(lengths_ref, members)
    for i, block_ref in zip(near, blocks):
        start = aligned(chosen(totals[:-1], lax.rem(index + members - i, members)))
        total_ref[pl.ds(start, block_ref.shape[0])] += (
            jnp.dot(block_ref[...], low_ref[...], preferred_element_type=jnp.float32) * scale
        )
    for half in range(HALVES):
        for i in range(members):
            owner = lax.rem(index + i, members)
            rows = pl.ds(pl.multiple_of(owner * share, ALIGN), share)
            out_ref = sums[half * members + i]
            here = slice(half * width, (half + 1) * width)
            out_ref[...] = total_ref[rows, here].astype(out_ref.dtype)


def turn_kernel(members, near, lengths_ref, rows_ref, *refs):
    blocks, (turned_ref, all_ref) = refs[: len(near)], refs[len(near) :]
    index = lax.axis_index("fsdp")
    totals = live_before(lengths_ref, members)
    all_ref[...] = rows_ref[...]
    for i, block_ref in zip(near, blocks):
        start = aligned(chosen(totals[:-1], lax.rem(index + members - i, members)))
        all_ref[pl.ds(start, block_ref.shape[0])] += block_ref[...]
    for start in range(0, turned_ref.shape[1], 128):
        turned_ref[:, start : start + 128] = all_ref[start : start + 128, :].T


def gradient_kernel(members, turned_ref, *refs):
    residuals, (gradient_ref, low_ref, squares_ref, all_ref) = refs[:members], refs[members:]
    index = lax.axis_index("fsdp")
    share = residuals[0].shape[0]
    for i in range(members):
        owner = lax.rem(index + members - i, members)
        all_ref[pl.ds(pl.multiple_of(owner * share, ALIGN), share)] = residuals[i][...]
    squares_ref[...] = jnp.zeros_like(squares_ref)
    height = min(256, turned_ref.shape[0])

    @pl.loop(0, turned_ref.shape[0] // height)
    def _(j):
        rows = pl.ds(pl.multiple_of(j * height, height), height)
        gradient = jnp.dot(turned_ref[rows], all_ref[...], preferred_element_type=jnp.float32)
        gradient_ref[rows] = gradient
        low_ref[rows] = gradient.astype(low_ref.dtype)
        squares = jnp.sum((gradient * gradient).reshape(-1, 8, gradient.shape[1]), axis=0)
        lanes = squares.shape[1] // 128
        squares_ref[...] += sum(squares[:, 128 * k : 128 * (k + 1)] for k in range(lanes))


def average_kernel(entries, own_ref, other_ref, halves_ref, *refs):
    gradients, partners, (out_ref, done_ref, sems) = refs[:HALVES], refs[HALVES:-3], refs[-3:]
    rate = 0.5 * learning_rate
    own = rate * lax.rsqrt(jnp.sum(own_ref[...], keepdims=True) / entries + epsilon)
    other = rate * lax.rsqrt(jnp.sum(other_ref[...], keepdims=True) / entries + epsilon)
    pieces = sems.shape[0]
    height = done_ref.shape[0] // pieces
    width = done_ref.shape[1] // HALVES
    copies = []
    for j in range(pieces):
        rows = pl.ds(j * height, height)
        for half in range(HALVES):
            here = slice(half * width, (half + 1) * width)
            done_ref[rows, here] = (
                halves_ref[rows, here]
                - gradients[half][rows] * own
                - partners[half][rows].astype(jnp.float32) * other
            )
        copies.append(pltpu.make_async_copy(done_ref.at[rows], out_ref.at[rows], sems.at[j]))
        copies[-1].start()
    for copy in copies:
        copy.wait()


def more_rows(size, source, offsets, blocks):
    if size == 0:
        return blocks[0]
    members = lax.axis_size("fsdp")
    moved = [
        lax.ppermute(block[:size], "fsdp", [(source, (source + i) % members)])
        for i, block in zip(offsets, blocks)
    ]
    return jnp.pad(sum(moved[1:], moved[0]), ((0, blocks[0].shape[0] - size), (0, 0)))


def local(activations, targets, weights, lengths):
    features = activations[0]
    wanted = targets[0]
    master = weights[0]
    tokens_here = features.shape[0]
    local_rows, columns = master.shape
    members = lax.axis_size("fsdp")
    distance_bit = STEP % (lax.axis_size("replica").bit_length() - 1)
    share = tokens_here // 2
    first = -(-(share + 32) // ALIGN) * ALIGN
    more = -(-(tokens_here + ALIGN - first) // ALIGN) * ALIGN
    steps = (16, 32, 48, 64, 80, 96, 128) if members <= 4 else (96,)
    sizes = [0] + [size for size in steps if size < more] + [more]
    most = first + more
    scale = features.shape[1] ** (-0.5)
    places = members * share + most

    vmem = pl.BlockSpec(memory_space=pltpu.VMEM)
    anywhere = pl.BlockSpec(memory_space=pl.ANY)
    smem = pl.BlockSpec(memory_space=pltpu.SMEM)
    params = pltpu.CompilerParams(vmem_limit_bytes=16 * 2**20)
    middle = pltpu.CompilerParams(vmem_limit_bytes=40 * 2**20)
    large = pltpu.CompilerParams(vmem_limit_bytes=56 * 2**20)

    def array(rows, width, dtype):
        return jax.ShapeDtypeStruct((rows, width), dtype)

    def cost(flops, moved):
        return pl.CostEstimate(flops=flops, bytes_accessed=moved, transcendentals=0)

    def sent_to(offsets):
        count = len(offsets)
        pieces = max(1, local_rows // 256)
        *arrays, choice = pl.pallas_call(
            functools.partial(sent_kernel, members, offsets, sizes),
            in_specs=[smem, anywhere],
            out_specs=[anywhere] * (2 * count) + [smem],
            out_shape=[
                array(rows, local_rows, jnp.bfloat16) for rows in (first, more) for _ in offsets
            ]
            + [jax.ShapeDtypeStruct((1,), jnp.int32)],
            scratch_shapes=[
                pltpu.VMEM((count, tokens_here, local_rows), jnp.bfloat16),
                pltpu.VMEM((count, first, local_rows), jnp.bfloat16),
                pltpu.VMEM((count, more, local_rows), jnp.bfloat16),
                pltpu.SemaphoreType.DMA((count, pieces)),
                pltpu.SemaphoreType.DMA((count, pieces)),
                pltpu.SemaphoreType.DMA((count,)),
            ],
            compiler_params=large,
            cost_estimate=cost(
                2 * count * first * tokens_here * local_rows,
                2 * count * (tokens_here + first) * local_rows,
            ),
        )(lengths, features)
        return arrays[:count], arrays[count:], choice

    far = members // 2
    near = [i for i in range(1, members) if i != far]
    far_first, far_more, choice = sent_to([far])
    near_first, near_more, _ = sent_to(near)
    held_far = turned(far_first[0], far)
    offsets = [far] + near
    bits = choice_bits(sizes)
    held_more = [
        lax.switch(
            lax.shift_right_logical(choice[0], jnp.int32(source * bits)) & (2**bits - 1),
            [functools.partial(more_rows, size, source, offsets) for size in sizes],
            far_more + near_more,
        )
        for source in range(members)
    ]
    near_first, held_more, late_lengths = lax.optimization_barrier((near_first, held_more, lengths))
    held = [turned(block, i) for i, block in zip(near, near_first)]

    partner_master = swapped(master, "replica", distance_bit)
    rows, keys, low, halves = pl.pallas_call(
        functools.partial(own_kernel, members, far, scale),
        in_specs=[smem, anywhere, vmem, vmem, vmem, anywhere] + [anywhere] * members,
        out_specs=[vmem] * 4,
        out_shape=[
            array(places, local_rows, jnp.bfloat16),
            array(places, columns, jnp.float32),
            array(local_rows, columns, jnp.bfloat16),
            array(local_rows, columns, jnp.float32),
        ],
        scratch_shapes=[
            pltpu.VMEM((tokens_here, local_rows), jnp.bfloat16),
            pltpu.VMEM((first, local_rows), jnp.bfloat16),
            pltpu.VMEM((more, local_rows), jnp.bfloat16),
            pltpu.SemaphoreType.DMA((max(1, local_rows // 256),)),
            pltpu.SemaphoreType.DMA,
            pltpu.SemaphoreType.DMA((members,)),
        ],
        compiler_params=middle,
        cost_estimate=cost(
            2 * (most * tokens_here + members * share * columns) * (local_rows + columns),
            20 * local_rows * columns,
        ),
    )(late_lengths, features, wanted, master, partner_master, held_far, *held_more)

    width = columns // HALVES
    sum_shapes = [array(share, width, jnp.bfloat16 if i else jnp.float32) for i in range(members)]
    *sums, _ = pl.pallas_call(
        functools.partial(keys_kernel, members, near, scale),
        in_specs=[smem, vmem, vmem] + [vmem] * len(near),
        out_specs=[vmem] * (HALVES * members + 1),
        out_shape=sum_shapes * HALVES + [array(places, columns, jnp.float32)],
        input_output_aliases={2: HALVES * members},
        compiler_params=params,
        cost_estimate=cost(
            2 * len(near) * first * local_rows * columns, 8 * places * columns
        ),
    )(lengths, low, keys, *held)
    sums = [sums[half * members : (half + 1) * members] for half in range(HALVES)]

    turned_rows = pl.pallas_call(
        functools.partial(turn_kernel, members, near),
        in_specs=[smem, vmem] + [vmem] * len(near),
        out_specs=vmem,
        out_shape=array(local_rows, members * share, jnp.bfloat16),
        scratch_shapes=[pltpu.VMEM((places, local_rows), jnp.bfloat16)],
        compiler_params=params,
        cost_estimate=cost(0, 4 * members * share * local_rows),
    )(lengths, rows, *held)

    gradients, partners, squares = [], [], 0.0
    for half in range(HALVES):
        residual = sums[half][0]
        for i in range(1, members):
            residual = residual + turned(sums[half][i], i).astype(jnp.float32)
        residual = residual.astype(jnp.bfloat16)
        residuals = [residual] + [turned(residual, i) for i in range(1, members)]
        gradient, low_gradient, own_squares = pl.pallas_call(
            functools.partial(gradient_kernel, members),
            in_specs=[vmem] + [vmem] * members,
            out_specs=[vmem] * 3,
            out_shape=[
                array(local_rows, width, jnp.float32),
                array(local_rows, width, jnp.bfloat16),
                array(8, 128, jnp.float32),
            ],
            scratch_shapes=[pltpu.VMEM((members * share, width), jnp.bfloat16)],
            compiler_params=params,
            cost_estimate=cost(
                2 * members * share * local_rows * width, 8 * local_rows * width
            ),
        )(turned_rows, *residuals)
        gradients.append(gradient)
        partners.append(swapped(low_gradient, "replica", distance_bit))
        squares = squares + own_squares

    total = squares
    for i in range(1, members):
        total = total + turned(squares, i)
    partner_total = swapped(total, "replica", distance_bit)

    averaged = pl.pallas_call(
        functools.partial(average_kernel, members * local_rows * columns),
        in_specs=[vmem] * (3 + 2 * HALVES),
        out_specs=anywhere,
        out_shape=array(local_rows, columns, jnp.float32),
        scratch_shapes=[
            pltpu.VMEM((local_rows, columns), jnp.float32),
            pltpu.SemaphoreType.DMA((4,)),
        ],
        compiler_params=params,
    )(total, partner_total, halves, *gradients, *partners)
    return averaged[None]


def solution(mesh):
    return jax.shard_map(
        local,
        mesh=mesh,
        in_specs=(
            P("replica", "fsdp", None),
            P("replica", "fsdp", None),
            P("replica", "fsdp", None),
            P("replica", None),
        ),
        out_specs=P("replica", "fsdp", None),
        check_vma=False,
    )
```
